128 devices in a mesh: dp: 4 (over z), gx: 4 (over x_lo, core), gy: 8 (over y, x_hi).
Axes of the slice: x: 4 (x_hi: 2, x_lo: 2; x = x_hi * 2 + x_lo), y: 4, z: 4, core: 2. Of those that a mesh axis runs over, the one named last changes fastest.
Arguments:
- tokens_in: bfloat16 [16384, 1600], P(('dp', 'gy'), 'gx'), may hold values from -6 to 6
- segments: int32 [16, 1024], P(('dp', 'gx'), 'gy'), may hold values from 0 to 2, as said below
- norm1_gain: float32 [1600], P('gx'), may hold values from 0.25 to 1.75
- norm1_bias: float32 [1600], P('gx'), may hold values from -4 to 4
- qkv_weight: bfloat16 [1600, 4800], P('gx', 'gy'), may hold values from -0.15625 to 0.15625
- query_bias: float32 [1600], replicated, may hold values from -6 to 6
- value_bias: float32 [1600], replicated, may hold values from -0.75 to 0.75
- proj_weight: bfloat16 [1600, 1600], P('gx', 'gy'), may hold values from -1.25 to 1.25
- proj_bias: float32 [1600], P('gx'), may hold values from -4 to 4
- norm2_gain: float32 [1600], P('gx'), may hold values from 0.25 to 1.75
- norm2_bias: float32 [1600], P('gx'), may hold values from -4 to 4
- fc_weight: bfloat16 [1600, 6400], P('gx', 'gy'), may hold values from -0.15625 to 0.15625
- fc_bias: float32 [6400], P('gy'), may hold values from -6 to 6
- out_weight: bfloat16 [1600, 6400], P('gx', 'gy'), may hold values from -0.078125 to 0.078125
- out_bias: float32 [1600], P('gx'), may hold values from -4 to 4
- out_grad: bfloat16 [16384, 1600], P(('dp', 'gy'), 'gx'), may hold values from -6 to 6
Outputs:
- layer_out: bfloat16 [16384, 1600], P(('dp', 'gy'), 'gx')
- input_grad: float32 [16384, 1600], P(('dp', 'gy'), 'gx')
- norm1_gain_grad: float32 [1600], P('gx')
- norm1_bias_grad: float32 [1600], P('gx')
- qkv_weight_grad: float32 [1600, 4800], P('gx', 'gy')
- query_bias_grad: float32 [1600], replicated
- value_bias_grad: float32 [1600], replicated
- proj_weight_grad: float32 [1600, 1600], P('gx', 'gy')
- proj_bias_grad: float32 [1600], P('gx')
- norm2_gain_grad: float32 [1600], P('gx')
- norm2_bias_grad: float32 [1600], P('gx')
- fc_weight_grad: float32 [1600, 6400], P('gx', 'gy')
- fc_bias_grad: float32 [6400], P('gy')
- out_weight_grad: float32 [1600, 6400], P('gx', 'gy')
- out_bias_grad: float32 [1600], P('gx')
The draws below stay inside these ranges and needn't reach their ends.
Inputs may be any that keep to these rules, and one draw needn't show every extreme that they name: `segments`: each sequence of 1024 tokens holds three documents numbered 0, 1, 2 in order; document 1 has exactly 800 tokens and begins within the first eighth of the sequence.
All inputs are finite; a program needn't handle non-finite values.
Results may differ from the reference program's by a relative error of at most 0.014.
Values may be sent and summed in bfloat16 or wider, within the bound.
A program may use at most 192 MiB of HBM per device.

```python
import math
import jax
import jax.numpy as jnp
from jax import lax

HEADS = 25
HEAD_DIM = 64
D = 1600
FF = 6400
SEQ_LEN = 1024
DOC_MAX = 800
SEQ_COUNT = 16
TOKENS = 16384


def draw_segments(key, part):
    key = jax.random.fold_in(key, 7)
    shift = jax.random.randint(key, (SEQ_COUNT, 1), 0, SEQ_LEN // 32 - 1)
    begin = SEQ_LEN // 8 - 1 - shift
    place = jnp.arange(SEQ_LEN, dtype=jnp.int32)[None, :]
    ids = (place >= begin).astype(jnp.int32) + (place >= begin + DOC_MAX).astype(jnp.int32)
    return ids.astype(jnp.int32)


def level_of(own_key, dims, split, least, top_value):
    level = 1.0
    for dim, parts in split:
        draws = jax.random.uniform(jax.random.fold_in(jax.random.fold_in(own_key, 6), dim), (parts,), jnp.float32, least / len(split), top_value / len(split))
        level = level * jnp.repeat(jnp.exp(draws), dims[dim] // parts).reshape((-1,) + (1,) * (len(dims) - 1 - dim))
    return level


def gaussian(stream_key, dims, scale, bound, split=(), held_as=jnp.bfloat16):
    values = scale * jax.random.normal(stream_key, dims, jnp.float32)
    if split:
        values = values * level_of(stream_key, dims, split, -0.22, 0.18)
    return jnp.clip(values, -bound, bound).astype(held_as)


def setup_inputs(seed: int = 0) -> dict:
    key_list = jax.random.split(jax.random.key(seed), 17)
    tokens_in = gaussian(key_list[0], (TOKENS, D), 1.0, 6.0, ((0, 32), (1, 4)))
    segments = draw_segments(jax.random.fold_in(key_list[16], 71), 0)
    norm1_gain = jnp.clip(1.0 + 0.15 * jax.random.normal(key_list[2], (D,), jnp.float32), 0.25, 1.75)
    norm1_bias = gaussian(key_list[3], (D,), 0.3, 4.0, ((0, 4),), jnp.float32)
    qkv_weight = gaussian(key_list[4], (D, 3 * D), D ** -0.5, 0.15625, ((0, 4), (1, 8)))
    query_bias = gaussian(key_list[5], (D,), 0.5, 6.0, (), jnp.float32)
    value_bias = gaussian(key_list[6], (D,), 0.05, 0.75, (), jnp.float32)
    proj_weight = gaussian(key_list[7], (D, D), (max(D // 64, 1)) ** -0.5, 1.25, ((0, 4), (1, 8)))
    proj_bias = gaussian(key_list[8], (D,), 0.3, 4.0, ((0, 4),), jnp.float32)
    norm2_gain = jnp.clip(1.0 + 0.15 * jax.random.normal(key_list[9], (D,), jnp.float32), 0.25, 1.75)
    norm2_bias = gaussian(key_list[10], (D,), 0.3, 4.0, ((0, 4),), jnp.float32)
    fc_weight = gaussian(key_list[11], (D, FF), D ** -0.5, 0.15625, ((0, 4), (1, 8)))
    fc_bias = gaussian(key_list[12], (FF,), 0.5, 6.0, ((0, 8),), jnp.float32)
    out_weight = gaussian(key_list[13], (D, FF), FF ** -0.5, 0.078125, ((0, 4), (1, 8)))
    out_bias = gaussian(key_list[14], (D,), 0.3, 4.0, ((0, 4),), jnp.float32)
    out_grad = gaussian(key_list[15], (TOKENS, D), 1.0, 6.0, ((0, 32), (1, 4)))
    return {"tokens_in": tokens_in, "segments": segments, "norm1_gain": norm1_gain, "norm1_bias": norm1_bias, "qkv_weight": qkv_weight, "query_bias": query_bias, "value_bias": value_bias, "proj_weight": proj_weight, "proj_bias": proj_bias, "norm2_gain": norm2_gain, "norm2_bias": norm2_bias, "fc_weight": fc_weight, "fc_bias": fc_bias, "out_weight": out_weight, "out_bias": out_bias, "out_grad": out_grad}


NEG_FILL = -1e+30
HIGH = lax.Precision.HIGHEST

@jax.custom_vjp
def low(v):
    return lax.optimization_barrier(v.astype(jnp.bfloat16)).astype(jnp.float32)

@jax.custom_vjp
def low_back(v):
    return v

def low_keep(v):
    return (low(v), None)

def low_pass(kept, grad):
    return (grad,)

def back_keep(v):
    return (v, None)

def back_low(kept, grad):
    return (low(grad),)
low.defvjp(low_keep, low_pass)
low_back.defvjp(back_keep, back_low)

def layer_norm(values, gain, shift):
    mean = lax.optimization_barrier(jnp.mean(values, axis=-1, keepdims=True))
    spread = lax.optimization_barrier(jnp.mean(values * values, axis=-1, keepdims=True)) - mean * mean
    return (values - mean) * lax.rsqrt(spread + 1e-05) * gain + shift

def gelu(value):
    return 0.5 * value * (1.0 + jnp.tanh(0.7978845608028654 * (value + 0.044715 * value * value * value)))

def attend(queries, keys, values, seg_ids):
    size = math.gcd(SEQ_LEN, 512)
    count = SEQ_LEN // size
    scale = 1.0 / math.sqrt(HEAD_DIM)
    place = jnp.arange(SEQ_LEN, dtype=jnp.int32)

    @jax.checkpoint
    def block(item):
        query_block, query_pos, query_seg = item
        raw = low_back(jnp.einsum('ahe,bhe->hab', query_block, keys, precision=HIGH) * scale)
        allowed = (place[None, :] <= query_pos[:, None]) & (seg_ids[None, :] == query_seg[:, None])
        masked = jnp.where(allowed[None], raw, NEG_FILL)
        top = lax.optimization_barrier(jnp.max(masked, axis=-1, keepdims=True))
        expo = jnp.exp(masked - top)
        weights = low(expo / lax.optimization_barrier(jnp.sum(expo, axis=-1, keepdims=True)))
        return jnp.einsum('hab,bhe->ahe', weights, values, precision=HIGH)
    result = lax.map(block, (queries.reshape(count, size, HEADS, HEAD_DIM), place.reshape(count, size), seg_ids.reshape(count, size)))
    return result.reshape(SEQ_LEN, HEADS, HEAD_DIM)

def reference(tokens_in, segments, norm1_gain, norm1_bias, qkv_weight, query_bias, value_bias, proj_weight, proj_bias, norm2_gain, norm2_bias, fc_weight, fc_bias, out_weight, out_bias, out_grad):
    width = HEADS * HEAD_DIM
    seq_count = TOKENS // SEQ_LEN

    def forward(inputs, gain_one, shift_one, w_qkv, q_bias, v_bias, w_proj, b_proj, gain_two, shift_two, w_fc, b_fc, w_out, b_out):
        first = low(layer_norm(inputs, gain_one, shift_one))
        linear = jnp.dot(first, w_qkv, precision=HIGH) + jnp.concatenate([q_bias, jnp.zeros_like(q_bias), v_bias])
        qkv = low_back(low(linear))
        shaped = qkv.reshape(seq_count, SEQ_LEN, 3, HEADS, HEAD_DIM)
        attended = lax.map(lambda item: attend(item[0], item[1], item[2], item[3]), (shaped[:, :, 0], shaped[:, :, 1], shaped[:, :, 2], segments.reshape(seq_count, SEQ_LEN)))
        att = low_back(low(attended.reshape(TOKENS, width)))
        branch_one = low_back(jnp.dot(att, w_proj.T, precision=HIGH) + b_proj)
        resid = inputs + branch_one
        second = low(layer_norm(resid, gain_two, shift_two))
        pre = low_back(jnp.dot(second, w_fc, precision=HIGH) + b_fc)
        hidden = low(gelu(pre))
        branch_two = low_back(jnp.dot(hidden, w_out.T, precision=HIGH) + b_out)
        return resid + branch_two
    primal, pull = jax.vjp(forward, tokens_in.astype(jnp.float32), norm1_gain, norm1_bias, qkv_weight.astype(jnp.float32), query_bias, value_bias, proj_weight.astype(jnp.float32), proj_bias, norm2_gain, norm2_bias, fc_weight.astype(jnp.float32), fc_bias, out_weight.astype(jnp.float32), out_bias)
    grads = pull(out_grad.astype(jnp.float32))
    return (primal.astype(jnp.bfloat16), grads[0], grads[1], grads[2], grads[3], grads[4], grads[5], grads[6], grads[7], grads[8], grads[9], grads[10], grads[11], grads[12], grads[13])
```

```python
import math

import jax
import jax.numpy as jnp
from jax import lax
from jax.experimental import pallas as pl
from jax.experimental.pallas import tpu as pltpu
from jax.sharding import PartitionSpec as P

BF = jnp.bfloat16
F32 = jnp.float32
HEADS = 25
HEAD_DIM = 64
D = HEADS * HEAD_DIM
FF = 6400
SEQ = 1024
DOC = 800
ROWS = 128
QUARTER = 400
SUB = 200
FPAD = 208
FRAME = 256
TAIL = 64
NEG = -1e30
MESH = pl.DeviceIdType.MESH
VMEM = pl.BlockSpec(memory_space=pltpu.VMEM)
SMEM = pl.BlockSpec(memory_space=pltpu.SMEM)


def nt(a, b):
    return lax.dot_general(a, b, (((1,), (1,)), ((), ())), preferred_element_type=F32)


def nn(a, b):
    return lax.dot_general(a, b, (((1,), (0,)), ((), ())), preferred_element_type=F32)


def tn(a, b):
    return lax.dot_general(a, b, (((0,), (0,)), ((), ())), preferred_element_type=F32)


class Here:
    def __init__(self):
        self.z, self.gx, self.gy = (lax.axis_index(a) for a in ("dp", "gx", "gy"))
        self.y, self.xh = self.gy // 2, lax.rem(self.gy, 2)
        self.x = self.xh * 2 + self.gx // 2
        self.c = lax.rem(self.gx, 2)
        self.p = self.x * 2 + self.c

    def at(self, x, c, y, z):
        return (z, lax.rem(x, 2) * 2 + c, y * 2 + x // 2)

    def rel(self, dx=0, flip=0, dy=0, dz=0):
        c = 1 - self.c if flip else self.c
        return self.at(
            lax.rem(self.x + 4 + dx, 4), c, lax.rem(self.y + 4 + dy, 4), lax.rem(self.z + 4 + dz, 4)
        )

    def ring(self):
        return [self.rel(dx, f) for dx in range(4) for f in (0, 1) if dx or f]

    def gxd(self, d):
        return (self.z, self.gx ^ d, self.gy)

    def unit(self, i):
        if i == 3:
            return self.gy, 3
        t = 3 * self.gy + i
        return lax.rem(t, 8), t // 8

    def block(self, kind, p):
        if kind == 3:
            return p, 3
        t = kind * 8 + p
        return t // 3, lax.rem(t, 3)

    def holds(self, kind):
        return self.block(kind, self.p)[0] // 2 == self.y


def meet(peers):
    sem = pltpu.get_barrier_semaphore()
    for d in peers:
        pl.semaphore_signal(sem, inc=1, device_id=d, device_id_type=MESH)
    pl.semaphore_wait(sem, len(peers))


def push(src, dst, ss, rs, d):
    return pltpu.make_async_remote_copy(
        src_ref=src, dst_ref=dst, send_sem=ss, recv_sem=rs, device_id=d, device_id_type=MESH
    )


def stats(v):
    mean = jnp.sum(v, axis=1, keepdims=True) / D
    spread = jnp.sum(v * v, axis=1, keepdims=True) / D - mean * mean
    inv = lax.rsqrt(spread + 1e-5)
    return (v - mean) * inv, inv


def norm_back(u, gain, normed, inv):
    w = u * gain
    a = jnp.sum(w, axis=1, keepdims=True) / D
    b = jnp.sum(w * normed, axis=1, keepdims=True) / D
    return inv * (w - a - normed * b)


def rows_of(v):
    return jnp.sum(v, axis=0, keepdims=True)


class Gather:
    SEMS = 9

    def __init__(self, here, buf, ss, rs, base):
        self.h, self.buf, self.ss, self.rs, self.base = here, buf, ss, rs, base

    def slot(self, dx):
        return lax.rem(self.h.x + 4 + dx, 4) * 2 + self.h.c

    def go(self, k, slot, d, half=None):
        ref = self.buf.at[slot] if half is None else self.buf.at[slot, pl.ds(half * 64, 64)]
        i = self.base + k
        copy = push(ref, ref, self.ss.at[i], self.rs.at[i], d)
        copy.start()
        return copy

    def start(self):
        h = self.h
        self.right, self.left, self.sib = h.rel(1), h.rel(-1), h.rel(0, 1)
        self.a0 = self.go(0, self.slot(0), self.right)
        self.a1 = self.go(1, self.slot(0), self.left)
        self.f0 = self.go(2, self.slot(0), self.sib)

    def ready(self, s):
        h = self.h
        if s == 0:
            self.f0.wait_recv()
            return h.x
        if s == 1:
            self.a0.wait_recv()
            self.r0 = self.go(3, self.slot(-1), self.right, 0)
            self.f1 = self.go(5, self.slot(-1), self.sib)
            self.a1.wait_recv()
            self.r1 = self.go(4, self.slot(1), self.left, 1)
            self.f2 = self.go(6, self.slot(1), self.sib)
            self.f1.wait_recv()
            return lax.rem(h.x + 3, 4)
        if s == 2:
            self.f2.wait_recv()
            return lax.rem(h.x + 1, 4)
        self.r0.wait_recv()
        self.f3 = self.go(7, self.slot(2), self.sib, 0)
        self.r1.wait_recv()
        self.f4 = self.go(8, self.slot(2), self.sib, 1)
        self.f3.wait_recv()
        self.f4.wait_recv()
        return lax.rem(h.x + 2, 4)

    def finish(self):
        for c in (self.a0, self.a1, self.r0, self.r1, self.f0, self.f1, self.f2, self.f3, self.f4):
            c.wait_send()


class Scatter:
    SEMS = 7

    @staticmethod
    def scratch():
        return [
            pltpu.VMEM((2, ROWS, D), F32),
            pltpu.VMEM((4, ROWS, D), F32),
            pltpu.VMEM((4, ROWS, D), BF),
            pltpu.VMEM((4, ROWS, D), BF),
            pltpu.VMEM((3, ROWS, D), BF),
            pltpu.VMEM((3, ROWS, D), BF),
        ]

    def __init__(self, here, refs, ss, rs, base):
        self.h, self.ss, self.rs, self.base = here, ss, rs, base
        self.both, self.own, self.give, self.got, self.sums, self.far = refs
        self.steps = (2, 1, -1, 0)
        self.copies = {}

    def part(self, j, term):
        h = self.h
        chip = lax.rem(h.x + 4 + self.steps[j], 4)
        self.both[...] = term(chip).reshape(2, ROWS, D)
        self.own[j] = self.both[h.c]
        self.give[j] = self.both[1 - h.c].astype(BF)
        i = self.base + j
        c = push(self.give.at[j], self.got.at[j], self.ss.at[i], self.rs.at[i], h.rel(0, 1))
        c.start()
        self.copies[j] = c

    def combine(self, j):
        self.copies[j].wait_recv()
        if j == 3:
            return
        self.sums[j] = (self.own[j] + self.got[j].astype(F32)).astype(BF)
        i = self.base + 4 + j
        c = push(
            self.sums.at[j], self.far.at[j], self.ss.at[i], self.rs.at[i], self.h.rel(self.steps[j])
        )
        c.start()
        self.copies[4 + j] = c

    def run(self, term):
        self.part(0, term)
        self.part(1, term)
        self.combine(0)
        self.part(2, term)
        self.combine(1)
        self.part(3, term)
        self.combine(2)
        self.combine(3)

    def result(self):
        total = self.own[3] + self.got[3].astype(F32)
        for j in range(3):
            self.copies[4 + j].wait_recv()
            total = total + self.far[j].astype(F32)
        for c in self.copies.values():
            c.wait_send()
        return total


def join(blocks):
    return jnp.concatenate(blocks, axis=1)


def entry_kernel(
    tok, grd, wa, ff, vec, rows, grads, units, hidden, vecs,
    rt, rg, rwa, rff, rv, tsend, trecv, scr, frames, ss, rs, rsw,
):
    h = Here()
    nxt = lax.rem(h.gy + 1, 8)
    prv = lax.rem(h.gy + 7, 8)
    meet(h.ring() + [(h.z, h.gx, nxt), (h.z, h.gx, prv)])
    for k, i in enumerate((2, 3)):
        tsend[k] = wa[i].astype(F32)[SUB - TAIL :].astype(BF)
    tail = push(tsend, trecv, ss.at[0], rs.at[0], (h.z, h.gx, nxt))
    tail.start()
    copies = []
    for d in (1, 2, 3):
        for k, (src, dst) in enumerate(((tok, rt), (ff, rff), (grd, rg))):
            i = 3 * d + k
            copies.append(push(src.at[h.gx ^ d], dst.at[h.gx], ss.at[i], rs.at[i], h.gxd(d)))
        copies.append(push(vec, rv.at[h.gx], ss.at[12 + d], rs.at[12 + d], h.gxd(d)))
    for c in copies:
        c.start()
    rt[h.gx] = tok[h.gx]
    rg[h.gx] = grd[h.gx]
    rff[h.gx] = ff[h.gx]
    rv[h.gx] = vec[...]

    sends = []
    row = lax.broadcasted_iota(jnp.int32, (FRAME, QUARTER), 0)
    for i in (1, 2, 0, 3):
        p, kind = h.unit(i)
        if i == 0:
            tail.wait_recv()
        before = wa[i - 1].astype(F32)[SUB - TAIL :] if i in (1, 2) else trecv[i // 3].astype(F32)
        scr[pl.ds(pl.multiple_of(8 * p, 8), TAIL)] = before
        scr[pl.ds(pl.multiple_of(8 * p + TAIL, 8), SUB)] = wa[i].astype(F32)
        frame = jnp.where((row < 192) | (p == 7), scr[TAIL : TAIL + FRAME], 0.0)
        frames[i] = frame.astype(BF)
        c = push(
            frames.at[i], rwa.at[kind, h.gx], ss.at[16 + i], rsw.at[kind, h.gx],
            h.at(p // 2, lax.rem(p, 2), h.y, h.z),
        )
        mine = p == h.p

        @pl.when(mine)
        def _(i=i, kind=kind):
            rwa[kind, h.gx] = frames[i]

        @pl.when(jnp.logical_not(mine))
        def _(c=c):
            c.start()

        sends.append((c, mine))
    for c in copies:
        c.wait_recv()
    rows[...] = join([rt[g] for g in range(4)])
    grads[...] = join([rg[g] for g in range(4)])
    vecs[...] = join([rv[g] for g in range(4)])
    for k in range(2):
        hidden[k] = join([rff[g, k] for g in range(4)])
    for kind in range(4):
        gy, _ = h.block(kind, h.p)
        xh = lax.rem(gy, 2)
        for g in range(4):
            other = jnp.logical_not((g == h.gx) & (xh == h.xh))

            @pl.when(h.holds(kind) & other)
            def _(kind=kind, g=g):
                push(
                    frames.at[0], rwa.at[kind, g], ss.at[16], rsw.at[kind, g], h.rel(0, 1)
                ).wait_recv()

        @pl.when(h.holds(kind))
        def _(kind=kind):
            units[kind] = join([rwa[kind, g] for g in range(4)])

    tail.wait_send()
    for c in copies:
        c.wait_send()
    for c, mine in sends:

        @pl.when(jnp.logical_not(mine))
        def _(c=c):
            c.wait_send()


def entry(tok, grd, wa, ff, vec):
    return pl.pallas_call(
        entry_kernel,
        out_shape=[
            jax.ShapeDtypeStruct((ROWS, D), BF),
            jax.ShapeDtypeStruct((ROWS, D), BF),
            jax.ShapeDtypeStruct((4, FRAME, D), BF),
            jax.ShapeDtypeStruct((2, FPAD, D), BF),
            jax.ShapeDtypeStruct((8, D), F32),
        ],
        in_specs=[VMEM] * 5,
        out_specs=[VMEM] * 5,
        scratch_shapes=[
            pltpu.VMEM((4, ROWS, QUARTER), BF),
            pltpu.VMEM((4, ROWS, QUARTER), BF),
            pltpu.VMEM((4, 4, FRAME, QUARTER), BF),
            pltpu.VMEM((4, 2, FPAD, QUARTER), BF),
            pltpu.VMEM((4, 8, QUARTER), F32),
            pltpu.VMEM((2, TAIL, QUARTER), BF),
            pltpu.VMEM((2, TAIL, QUARTER), BF),
            pltpu.VMEM((336, QUARTER), F32),
            pltpu.VMEM((4, FRAME, QUARTER), BF),
            pltpu.SemaphoreType.DMA((20,)),
            pltpu.SemaphoreType.DMA((16,)),
            pltpu.SemaphoreType.DMA((4, 4)),
        ],
        compiler_params=pltpu.CompilerParams(
            collective_id=0, has_side_effects=True, vmem_limit_bytes=60 * 2**20
        ),
        name="entry",
    )(tok, grd, wa, ff, vec)


def set_masks(masks, begin):
    for i in range(4):
        n = 256 * (i + 1)
        b = lax.broadcasted_iota(jnp.int32, (n, 256), 0)
        a = lax.broadcasted_iota(jnp.int32, (n, 256), 1) + 256 * i

        def doc(t):
            return (t >= begin).astype(jnp.int32) + (t >= begin + DOC).astype(jnp.int32)

        masks[i, :n] = jnp.where((b <= a) & (doc(a) == doc(b)), 0.0, NEG)


def probs_t(key, query, mask):
    s = nt(key, query) + mask
    e = jnp.exp(s - jnp.max(s, axis=0, keepdims=True))
    return e * (1.0 / jnp.sum(e, axis=0, keepdims=True))


def halves(v):
    return v[:, :HEAD_DIM], v[:, HEAD_DIM:]


def attend_kernel(
    begin, rows, units, hidden, vecs, qkvb, fcb,
    firsts, weights, ffw, fcbs, qkv, att, resid, second,
    masks, *rest,
):
    scat_refs, (ss, rs, rsw) = rest[:6], rest[6:]
    h = Here()
    ys = [h.rel(dy=d) for d in (1, 2, 3)]
    meet(h.ring() + ys)
    x = rows[...].astype(F32)
    normed, _ = stats(x)
    firsts[h.p] = (normed * vecs[0:1] + vecs[1:2]).astype(BF)
    gather = Gather(h, firsts, ss, rs, 0)
    gather.start()
    wsend = []
    for kind in range(4):
        held = h.holds(kind)
        for d in (1, 2, 3):
            c = push(
                units.at[kind], weights.at[kind], ss.at[16 + 3 * kind + d - 1], rsw.at[kind], ys[d - 1]
            )
            wsend.append((c, held))

            @pl.when(held)
            def _(c=c):
                c.start()

        @pl.when(held)
        def _(kind=kind):
            weights[kind] = units[kind]

    fsend = []
    for d in (1, 2, 3):
        i = 28 + 2 * (d - 1)
        fsend.append(push(hidden, ffw.at[h.y], ss.at[i], rs.at[i], ys[d - 1]))
        fsend.append(push(fcb, fcbs.at[h.y], ss.at[i + 1], rs.at[i + 1], ys[d - 1]))
    for c in fsend:
        c.start()
    ffw[h.y] = hidden[...]
    fcbs[h.y] = fcb[...]
    set_masks(masks, begin[0])

    def wait_unit(kind):
        @pl.when(jnp.logical_not(h.holds(kind)))
        def _():
            push(units.at[0], weights.at[kind], ss.at[16], rsw.at[kind], ys[0]).wait_recv()

    for kind in range(3):
        wait_unit(kind)
    for s in range(4):
        chip = gather.ready(s)
        block = firsts[pl.ds(2 * chip, 2)].reshape(256, D)
        for kind in range(3):
            term = nt(block, weights[kind]) + qkvb[kind : kind + 1]
            qkv[kind, pl.ds(pl.multiple_of(256 * chip, 256), 256)] = term.astype(BF)
    gather.finish()

    @pl.loop(0, 2)
    def _(pair):
        lanes = pl.ds(pl.multiple_of(128 * pair, 128), 128)
        for i in range(4):
            n = 256 * (i + 1)
            queries = halves(qkv[0, 256 * i : n, lanes])
            keys = halves(qkv[1, 0:n, lanes])
            values = halves(qkv[2, 0:n, lanes])
            outs = []
            for q, k, v in zip(queries, keys, values):
                probs = probs_t(k, q * 0.125, masks[i, :n])
                outs.append(tn(probs.astype(BF), v))
            att[256 * i : n, lanes] = join(outs).astype(BF)

    wait_unit(3)
    scatter = Scatter(h, scat_refs, ss, rs, 9)

    def term(chip):
        return nn(att[pl.ds(pl.multiple_of(256 * chip, 256), 256)], weights[3])

    scatter.run(term)
    res = rows[...].astype(F32) + scatter.result() + vecs[2:3]
    resid[...] = res
    normed, _ = stats(res)
    second[...] = (normed * vecs[3:4] + vecs[4:5]).astype(BF)
    for c, held in wsend:

        @pl.when(held)
        def _(c=c):
            c.wait_send()

    for c in fsend:
        c.wait()


def attend(begin, rows, units, hidden, vecs, qkvb, fcb):
    return pl.pallas_call(
        attend_kernel,
        out_shape=[
            jax.ShapeDtypeStruct((8, ROWS, D), BF),
            jax.ShapeDtypeStruct((4, FRAME, D), BF),
            jax.ShapeDtypeStruct((4, 2, FPAD, D), BF),
            jax.ShapeDtypeStruct((4, 8, FPAD), F32),
            jax.ShapeDtypeStruct((3, SEQ, FRAME), BF),
            jax.ShapeDtypeStruct((SEQ, FRAME), BF),
            jax.ShapeDtypeStruct((ROWS, D), F32),
            jax.ShapeDtypeStruct((ROWS, D), BF),
        ],
        in_specs=[SMEM] + [VMEM] * 6,
        out_specs=[VMEM] * 8,
        scratch_shapes=[
            pltpu.VMEM((4, SEQ, 256), F32),
            *Scatter.scratch(),
            pltpu.SemaphoreType.DMA((34,)),
            pltpu.SemaphoreType.DMA((34,)),
            pltpu.SemaphoreType.DMA((4,)),
        ],
        compiler_params=pltpu.CompilerParams(
            collective_id=1, has_side_effects=True, vmem_limit_bytes=62 * 2**20
        ),
        name="attend",
    )(begin, rows, units, hidden, vecs, qkvb, fcb)


def feed_kernel(
    second, resid, grad, ffw, fcbs, vecs,
    layer_out, grad_resid, branch, dff, gvec, fcg,
    seconds, grads, hid, gpre, outs, *rest,
):
    s1, s2, (ss, rs) = rest[:6], rest[6:12], rest[12:]
    h = Here()
    meet(h.ring())
    seconds[h.p] = second[...]
    grads[h.p] = grad[...]
    g1 = Gather(h, seconds, ss, rs, 0)
    g2 = Gather(h, grads, ss, rs, 9)
    g1.start()
    g2.start()
    fcg[...] = jnp.zeros_like(fcg)
    for s in range(4):
        chip = g1.ready(s)
        g2.ready(s)
        span = pl.ds(pl.multiple_of(256 * chip, 256), 256)

        @pl.loop(0, 4)
        def _(y, chip=chip, span=span):
            a = seconds[pl.ds(2 * chip, 2)].reshape(256, D)
            b = grads[pl.ds(2 * chip, 2)].reshape(256, D)
            v = nt(a, ffw[y, 0]) + fcbs[y, 0:1]
            up = nt(b, ffw[y, 1])
            t = jnp.tanh(0.7978845608028654 * (v + 0.044715 * v * v * v))
            hid[y, span] = (0.5 * v * (1.0 + t)).astype(BF)
            slope = 0.5 * (1.0 + t) + 0.5 * v * (1.0 - t * t) * (
                0.7978845608028654 * (1.0 + 3 * 0.044715 * v * v)
            )
            low = (up * slope).astype(BF)
            gpre[y, span] = low
            fcg[y, 0:1] += rows_of(low.astype(F32))

    g1.finish()
    g2.finish()

    def total(src, k):
        def term(chip):
            span = pl.ds(pl.multiple_of(256 * chip, 256), 256)
            return sum(nn(src[y, span], ffw[y, k]) for y in range(4))

        return term

    back = Scatter(h, s2, ss, rs, 18)
    back.run(total(gpre, 0))
    forth = Scatter(h, s1, ss, rs, 25)
    forth.run(total(hid, 1))

    gs = back.result()
    normed, inv = stats(resid[...])
    up = grad[...].astype(F32)
    gres = up + norm_back(gs, vecs[3:4], normed, inv)
    grad_resid[...] = gres
    low = gres.astype(BF)
    branch[...] = low
    gvec[...] = jnp.zeros_like(gvec)
    gvec[0:1] = rows_of(gs * normed)
    gvec[1:2] = rows_of(gs)
    gvec[2:3] = rows_of(low.astype(F32))
    gvec[3:4] = rows_of(up)

    @pl.loop(0, 4)
    def _(y):
        dff[y, 0] = tn(gpre[y], seconds[...].reshape(SEQ, D)).astype(BF)
        dff[y, 1] = tn(hid[y], grads[...].reshape(SEQ, D)).astype(BF)

    out = (resid[...] + forth.result() + vecs[5:6]).astype(BF)
    for g in range(4):
        outs[g] = out[:, QUARTER * g : QUARTER * (g + 1)]
    spread(h, outs, layer_out, ss, rs, 32)


def spread(h, src, dst, ss, rs, base):
    copies = [
        push(src.at[h.gx ^ d], dst.at[h.gx], ss.at[base + d - 1], rs.at[base + d - 1], h.gxd(d))
        for d in (1, 2, 3)
    ]
    for c in copies:
        c.start()
    dst[h.gx] = src[h.gx]
    for c in copies:
        c.wait()


def feed(second, resid, grad, ffw, fcbs, vecs):
    return pl.pallas_call(
        feed_kernel,
        out_shape=[
            jax.ShapeDtypeStruct((4, ROWS, QUARTER), BF),
            jax.ShapeDtypeStruct((ROWS, D), F32),
            jax.ShapeDtypeStruct((ROWS, D), BF),
            jax.ShapeDtypeStruct((4, 2, FPAD, D), BF),
            jax.ShapeDtypeStruct((8, D), F32),
            jax.ShapeDtypeStruct((4, 8, FPAD), F32),
        ],
        in_specs=[VMEM] * 6,
        out_specs=[VMEM] * 6,
        scratch_shapes=[
            pltpu.VMEM((8, ROWS, D), BF),
            pltpu.VMEM((8, ROWS, D), BF),
            pltpu.VMEM((4, SEQ, FPAD), BF),
            pltpu.VMEM((4, SEQ, FPAD), BF),
            pltpu.VMEM((4, ROWS, QUARTER), BF),
            *Scatter.scratch(),
            *Scatter.scratch(),
            pltpu.SemaphoreType.DMA((35,)),
            pltpu.SemaphoreType.DMA((35,)),
        ],
        compiler_params=pltpu.CompilerParams(
            collective_id=2, has_side_effects=True, vmem_limit_bytes=62 * 2**20
        ),
        name="feed",
    )(second, resid, grad, ffw, fcbs, vecs)


def back_kernel(
    begin, branch, grad_resid, rows, firsts, weights, qkv, att, vecs,
    input_grad, dwa, gvec, qvg,
    masks, branches, gatt, dqkv, dk, dv, outs, got, *rest,
):
    scat_refs, (ss, rs) = rest[:6], rest[6:]
    h = Here()
    meet(h.ring())
    branches[h.p] = branch[...]
    gather = Gather(h, branches, ss, rs, 0)
    gather.start()
    set_masks(masks, begin[0])
    for s in range(4):
        chip = gather.ready(s)
        block = branches[pl.ds(2 * chip, 2)].reshape(256, D)
        gatt[pl.ds(pl.multiple_of(256 * chip, 256), 256)] = nt(block, weights[3]).astype(BF)
    gather.finish()

    @pl.loop(0, 2)
    def _(pair):
        lanes = pl.ds(pl.multiple_of(128 * pair, 128), 128)
        dk[...] = jnp.zeros_like(dk)
        dv[...] = jnp.zeros_like(dv)
        for i in range(4):
            n = 256 * (i + 1)
            queries = halves(qkv[0, 256 * i : n, lanes])
            keys = halves(qkv[1, 0:n, lanes])
            values = halves(qkv[2, 0:n, lanes])
            ups = halves(gatt[256 * i : n, lanes])
            dqs = []
            for s, (q, k, v, g) in enumerate(zip(queries, keys, values, ups)):
                q = q * 0.125
                probs = probs_t(k, q, masks[i, :n])
                dv[s, :n] += nn(probs.astype(BF), g)
                prod = probs * nt(v, g)
                ds = (prod - probs * jnp.sum(prod, axis=0, keepdims=True)).astype(BF)
                dk[s, :n] += nn(ds, q)
                dqs.append(tn(ds, k) * 0.125)
            dqkv[0, 256 * i : n, lanes] = join(dqs).astype(BF)
        dqkv[1, :, lanes] = join([dk[0], dk[1]]).astype(BF)
        dqkv[2, :, lanes] = join([dv[0], dv[1]]).astype(BF)

    scatter = Scatter(h, scat_refs, ss, rs, 9)

    def term(chip):
        span = pl.ds(pl.multiple_of(256 * chip, 256), 256)
        return sum(nn(dqkv[k, span], weights[k]) for k in range(3))

    scatter.run(term)
    qvg[...] = jnp.zeros_like(qvg)
    qvg[0:1] = rows_of(dqkv[0].astype(F32))
    qvg[1:2] = rows_of(dqkv[2].astype(F32))

    @pl.loop(0, 3)
    def _(kind):
        dwa[kind] = tn(dqkv[kind], firsts[...].reshape(SEQ, D)).astype(BF)

    dwa[3] = tn(att[...], branches[...].reshape(SEQ, D)).astype(BF)

    gf = scatter.result()
    normed, inv = stats(rows[...].astype(F32))
    out = grad_resid[...] + norm_back(gf, vecs[0:1], normed, inv)
    gvec[...] = jnp.zeros_like(gvec)
    gvec[0:1] = rows_of(gf * normed)
    gvec[1:2] = rows_of(gf)
    low = out.astype(BF)
    for g in range(4):
        outs[g] = low[:, QUARTER * g : QUARTER * (g + 1)]
    spread(h, outs, got, ss, rs, 16)
    input_grad[...] = got[...].astype(F32)


def back(begin, branch, grad_resid, rows, firsts, weights, qkv, att, vecs):
    return pl.pallas_call(
        back_kernel,
        out_shape=[
            jax.ShapeDtypeStruct((4, ROWS, QUARTER), F32),
            jax.ShapeDtypeStruct((4, FRAME, D), BF),
            jax.ShapeDtypeStruct((8, D), F32),
            jax.ShapeDtypeStruct((8, FRAME), F32),
        ],
        in_specs=[SMEM] + [VMEM] * 8,
        out_specs=[VMEM] * 4,
        scratch_shapes=[
            pltpu.VMEM((4, SEQ, 256), F32),
            pltpu.VMEM((8, ROWS, D), BF),
            pltpu.VMEM((SEQ, FRAME), BF),
            pltpu.VMEM((3, SEQ, FRAME), BF),
            pltpu.VMEM((2, SEQ, HEAD_DIM), F32),
            pltpu.VMEM((2, SEQ, HEAD_DIM), F32),
            pltpu.VMEM((4, ROWS, QUARTER), BF),
            pltpu.VMEM((4, ROWS, QUARTER), BF),
            *Scatter.scratch(),
            pltpu.SemaphoreType.DMA((19,)),
            pltpu.SemaphoreType.DMA((19,)),
        ],
        compiler_params=pltpu.CompilerParams(
            collective_id=3, has_side_effects=True, vmem_limit_bytes=62 * 2**20
        ),
        name="back",
    )(begin, branch, grad_resid, rows, firsts, weights, qkv, att, vecs)


ZF = 112
ZW = 64


def sums_kernel(
    dff, dwa, ffo, wao,
    ry, ryw, sf, sw, rz, rzw, zf, zw, ffs, was, main, tails, scr,
    ss, rs, ssw, rsw, rsm, rst,
):
    h = Here()
    ys = [h.rel(dy=d) for d in (1, 2, 3)]
    zs = [h.rel(dz=d) for d in (1, 2, 3)]
    plane = [h.rel(dx, f, dy) for dy in range(4) for dx in range(4) for f in (0, 1) if dx or f or dy]
    meet(plane + zs)
    n_ff = []
    for d in (1, 2, 3):
        to = lax.rem(h.y + d, 4)
        c = push(dff.at[to], ry.at[d - 1], ss.at[d - 1], rs.at[d - 1], ys[d - 1])
        c.start()
        n_ff.append(c)
    out_w = []
    for kind in range(4):
        home = h.block(kind, h.p)[0] // 2
        for d in (1, 2, 3):
            c = push(dwa.at[kind], ryw.at[d - 1, kind], ssw.at[kind], rsw.at[d - 1, kind], ys[d - 1])
            cond = lax.rem(h.y + d, 4) == home

            @pl.when(cond)
            def _(c=c):
                c.start()

            out_w.append((c, cond))
    for c in n_ff:
        c.wait_recv()
    for k in range(2):
        s = dff[h.y, k].astype(F32)
        for d in range(3):
            s = s + ry[d, k].astype(F32)
        sf[k] = s.astype(BF)
    zsend = []
    for d in (1, 2, 3):
        q = lax.rem(h.z + d, 4)
        src = sf.at[q // 2, pl.ds(pl.multiple_of(96 * lax.rem(q, 2), 16), ZF)]
        c = push(src, rz.at[d - 1], ss.at[2 + d], rs.at[2 + d], zs[d - 1])
        c.start()
        zsend.append(c)
    for kind in range(4):
        for d in (1, 2, 3):

            @pl.when(h.holds(kind))
            def _(kind=kind, d=d):
                push(
                    dwa.at[0], ryw.at[d - 1, kind], ssw.at[0], rsw.at[d - 1, kind], ys[0]
                ).wait_recv()

        @pl.when(h.holds(kind))
        def _(kind=kind):
            s = dwa[kind].astype(F32)
            for d in range(3):
                s = s + ryw[d, kind].astype(F32)
            sw[kind] = s.astype(BF)
            for d in (1, 2, 3):
                q = lax.rem(h.z + d, 4)
                src = sw.at[kind, pl.ds(pl.multiple_of(ZW * q, ZW), ZW)]
                push(
                    src, rzw.at[d - 1, kind], ssw.at[4 + 3 * kind + d - 1],
                    rsw.at[2 + d, kind], zs[d - 1],
                ).start()

    for c in zsend:
        c.wait_recv()
    s = sf[h.z // 2, pl.ds(pl.multiple_of(96 * lax.rem(h.z, 2), 16), ZF)].astype(F32)
    for d in range(3):
        s = s + rz[d].astype(F32)
    zf[h.z] = s.astype(BF)
    zback = []
    for d in (1, 2, 3):
        c = push(zf.at[h.z], zf.at[h.z], ss.at[5 + d], rs.at[5 + d], zs[d - 1])
        c.start()
        zback.append(c)
    for kind in range(4):

        @pl.when(h.holds(kind))
        def _(kind=kind):
            s = sw[kind, pl.ds(pl.multiple_of(ZW * h.z, ZW), ZW)].astype(F32)
            for d in (1, 2, 3):
                push(
                    dwa.at[0, pl.ds(0, ZW)], rzw.at[d - 1, kind], ssw.at[4],
                    rsw.at[2 + d, kind], zs[0],
                ).wait_recv()
                s = s + rzw[d - 1, kind].astype(F32)
            zw[kind, h.z] = s.astype(BF)
            for d in (1, 2, 3):
                push(
                    zw.at[kind, h.z], zw.at[kind, h.z], ssw.at[16 + 3 * kind + d - 1],
                    rsw.at[5 + d, kind], zs[d - 1],
                ).start()

    for c in zback:
        c.wait_recv()
    for k in range(2):
        full = jnp.concatenate([zf[2 * k], zf[2 * k + 1][16:]], axis=0)
        for g in range(4):
            ffs[g, k] = full[:, QUARTER * g : QUARTER * (g + 1)]
    spread_start = [
        push(ffs.at[h.gx ^ d], ffo.at[h.gx], ss.at[8 + d], rs.at[8 + d], h.gxd(d)) for d in (1, 2, 3)
    ]
    for c in spread_start:
        c.start()
    ffo[h.gx] = ffs[h.gx]

    for kind in range(4):
        gy, place = h.block(kind, h.p)
        gyt, placet = h.block(kind, h.p - 1)
        xh, xht, yt = lax.rem(gy, 2), lax.rem(gyt, 2), gyt // 2

        @pl.when(h.holds(kind))
        def _(kind=kind, gy=gy, place=place, gyt=gyt, placet=placet, xh=xh, xht=xht, yt=yt):
            for d in (1, 2, 3):
                push(
                    zw.at[0, 0], zw.at[kind, 0], ssw.at[4], rsw.at[5 + d, kind], zs[0]
                ).wait_recv()
            full = zw[kind].reshape(FRAME, D)
            for g in range(4):
                was[kind, g] = full[:, QUARTER * g : QUARTER * (g + 1)]
            for g in range(4):
                same = (g == h.gx) & (xh == h.xh)
                c = push(
                    was.at[kind, g], main.at[place], ssw.at[28 + 4 * kind + g], rsm.at[place],
                    (h.z, g, gy),
                )

                @pl.when(same)
                def _():
                    main[place] = was[kind, g]

                @pl.when(jnp.logical_not(same))
                def _():
                    c.start()

                @pl.when(h.p > 0)
                def _():
                    samet = (g == h.gx) & (xht == h.xh) & (yt == h.y)
                    t = push(
                        was.at[kind, g, pl.ds(0, TAIL)], tails.at[placet],
                        ssw.at[44 + 4 * kind + g], rst.at[placet], (h.z, g, gyt),
                    )

                    @pl.when(samet)
                    def _():
                        tails[placet] = was[kind, g, 0:TAIL]

                    @pl.when(jnp.logical_not(samet))
                    def _():
                        t.start()

    row = lax.broadcasted_iota(jnp.int32, (SUB, QUARTER), 0)
    for i in range(4):
        p, _ = h.unit(i)

        @pl.when(p != h.p)
        def _(i=i):
            push(main.at[0], main.at[i], ssw.at[28], rsm.at[i], ys[0]).wait_recv()

        nxt = p + 1
        kindv = h.unit(i)[1]
        if i == 3:
            ynext = nxt // 2
        else:
            ynext = (kindv * 8 + nxt) // 6

        @pl.when((p < 7) & jnp.logical_not((nxt == h.p) & (ynext == h.y)))
        def _(i=i):
            push(tails.at[0], tails.at[i], ssw.at[44], rst.at[i], ys[0]).wait_recv()

        scr[0:FRAME] = main[i].astype(F32)

        @pl.when(p < 7)
        def _(i=i):
            scr[192 : 192 + TAIL] = tails[i].astype(F32)

        wao[i] = scr[pl.ds(pl.multiple_of(8 * p, 8), SUB)]

    for c in n_ff + zsend + zback:
        c.wait_send()
    for c in spread_start:
        c.wait()
    for c, cond in out_w:

        @pl.when(cond)
        def _(c=c):
            c.wait_send()

    for kind in range(4):
        gy, place = h.block(kind, h.p)
        gyt, placet = h.block(kind, h.p - 1)
        xh, xht, yt = lax.rem(gy, 2), lax.rem(gyt, 2), gyt // 2

        @pl.when(h.holds(kind))
        def _(kind=kind, xh=xh, xht=xht, yt=yt):
            for d in (1, 2, 3):
                push(
                    sw.at[kind, pl.ds(0, ZW)], rzw.at[0, kind], ssw.at[4 + 3 * kind + d - 1],
                    rsw.at[3, kind], zs[0],
                ).wait_send()
                push(
                    zw.at[kind, 0], zw.at[kind, 0], ssw.at[16 + 3 * kind + d - 1], rsw.at[6, kind], zs[0]
                ).wait_send()
            for g in range(4):

                @pl.when(jnp.logical_not((g == h.gx) & (xh == h.xh)))
                def _():
                    push(
                        was.at[kind, g], main.at[0], ssw.at[28 + 4 * kind + g], rsm.at[0], ys[0]
                    ).wait_send()

                @pl.when((h.p > 0) & jnp.logical_not((g == h.gx) & (xht == h.xh) & (yt == h.y)))
                def _():
                    push(
                        was.at[kind, g, pl.ds(0, TAIL)], tails.at[0], ssw.at[44 + 4 * kind + g],
                        rst.at[0], ys[0],
                    ).wait_send()


def sums(dff, dwa):
    return pl.pallas_call(
        sums_kernel,
        out_shape=[
            jax.ShapeDtypeStruct((4, 2, FPAD, QUARTER), BF),
            jax.ShapeDtypeStruct((4, SUB, QUARTER), F32),
        ],
        in_specs=[VMEM] * 2,
        out_specs=[VMEM] * 2,
        scratch_shapes=[
            pltpu.VMEM((3, 2, FPAD, D), BF),
            pltpu.VMEM((3, 4, FRAME, D), BF),
            pltpu.VMEM((2, FPAD, D), BF),
            pltpu.VMEM((4, FRAME, D), BF),
            pltpu.VMEM((3, ZF, D), BF),
            pltpu.VMEM((3, 4, ZW, D), BF),
            pltpu.VMEM((4, ZF, D), BF),
            pltpu.VMEM((4, 4, ZW, D), BF),
            pltpu.VMEM((4, 2, FPAD, QUARTER), BF),
            pltpu.VMEM((4, 4, FRAME, QUARTER), BF),
            pltpu.VMEM((4, FRAME, QUARTER), BF),
            pltpu.VMEM((4, TAIL, QUARTER), BF),
            pltpu.VMEM((FRAME, QUARTER), F32),
            pltpu.SemaphoreType.DMA((12,)),
            pltpu.SemaphoreType.DMA((12,)),
            pltpu.SemaphoreType.DMA((60,)),
            pltpu.SemaphoreType.DMA((9, 4)),
            pltpu.SemaphoreType.DMA((4,)),
            pltpu.SemaphoreType.DMA((4,)),
        ],
        compiler_params=pltpu.CompilerParams(
            collective_id=4, has_side_effects=True, vmem_limit_bytes=62 * 2**20
        ),
        name="sums",
    )(dff, dwa)


def per_device(
    tokens_in, segments, norm1_gain, norm1_bias, qkv_weight, query_bias, value_bias, proj_weight,
    proj_bias, norm2_gain, norm2_bias, fc_weight, fc_bias, out_weight, out_bias, out_grad,
):
    gx, gy = lax.axis_index("gx"), lax.axis_index("gy")
    y, xh = gy // 2, lax.rem(gy, 2)
    p = xh * 4 + gx
    zeros = jnp.sum((segments == 0).astype(jnp.int32))
    begins = lax.psum(
        jnp.where((jnp.arange(4) == gx) & (gy == 0), zeros, 0).astype(jnp.int32), ("gx", "gy")
    )
    begin = lax.dynamic_slice_in_dim(begins, y, 1)

    wa = jnp.concatenate([qkv_weight.T.reshape(3, SUB, QUARTER), proj_weight.T[None]])
    ff = jnp.stack(
        [fc_weight.T.reshape(4, SUB, QUARTER), out_weight.T.reshape(4, SUB, QUARTER)], axis=1
    )
    ff = jnp.pad(ff, ((0, 0), (0, 0), (0, FPAD - SUB), (0, 0)))
    zero = jnp.zeros_like(norm1_gain)
    vec = jnp.stack(
        [norm1_gain, norm1_bias, proj_bias, norm2_gain, norm2_bias, out_bias, zero, zero]
    )
    rows, grads, units, hidden, vecs = entry(
        tokens_in.reshape(4, ROWS, QUARTER), out_grad.reshape(4, ROWS, QUARTER), wa, ff, vec
    )

    valid = (jnp.arange(FRAME) < 192) | (p == 7)
    qb = jnp.where(valid, lax.dynamic_slice_in_dim(query_bias, 192 * p, FRAME), 0.0)
    vb = jnp.where(valid, lax.dynamic_slice_in_dim(value_bias, 192 * p, FRAME), 0.0)
    nil = jnp.zeros_like(qb)
    qkvb = jnp.stack([qb, nil, vb, nil, nil, nil, nil, nil])
    fcb = jnp.pad(lax.dynamic_slice_in_dim(fc_bias, SUB * gx, SUB), (0, FPAD - SUB))
    fcb = jnp.broadcast_to(fcb, (8, FPAD))

    firsts, weights, ffw, fcbs, qkv, att, resid, second = attend(
        begin, rows, units, hidden, vecs, qkvb, fcb
    )
    layer_out, grad_resid, branch, dff, gvec2, fcg = feed(second, resid, grads, ffw, fcbs, vecs)
    input_grad, dwa, gvec1, qvg = back(
        begin, branch, grad_resid, rows, firsts, weights, qkv, att, vecs
    )
    ffo, wao = sums(dff, dwa)

    qv = jnp.zeros((2, D), F32)
    qv = lax.dynamic_update_slice(qv, qvg[0:2], (0, 192 * p))
    fcp = jnp.zeros((4, 2, 4, SUB), F32)
    fcp = lax.dynamic_update_slice(fcp, fcg[:, 0, :SUB][:, None, None], (0, xh, gx, 0))
    both = jnp.concatenate([gvec1[0:2], gvec2[0:4]])
    both, qv, fcp = lax.psum((both, qv, fcp), ("dp", "gx", "gy"))
    mine = lax.dynamic_slice_in_dim(both, QUARTER * gx, QUARTER, 1)
    fcp = lax.dynamic_slice(fcp, (y, xh, 0, 0), (1, 1, 4, SUB)).reshape(4 * SUB)

    def whole(v):
        return v[:, :SUB].reshape(4 * SUB, QUARTER).T.astype(F32)

    return (
        layer_out.reshape(4 * ROWS, QUARTER),
        input_grad.reshape(4 * ROWS, QUARTER),
        mine[0],
        mine[1],
        wao[0:3].reshape(3 * SUB, QUARTER).T,
        qv[0],
        qv[1],
        wao[3].T,
        mine[4],
        mine[2],
        mine[3],
        whole(ffo[:, 0]),
        fcp,
        whole(ffo[:, 1]),
        mine[5],
    )


def solution(mesh):
    return jax.shard_map(
        per_device,
        mesh=mesh,
        in_specs=(
            P(("dp", "gy"), "gx"), P(("dp", "gx"), "gy"), P("gx"), P("gx"), P("gx", "gy"), P(), P(),
            P("gx", "gy"), P("gx"), P("gx"), P("gx"), P("gx", "gy"), P("gy"), P("gx", "gy"), P("gx"),
            P(("dp", "gy"), "gx"),
        ),
        out_specs=(
            P(("dp", "gy"), "gx"), P(("dp", "gy"), "gx"), P("gx"), P("gx"), P("gx", "gy"), P(), P(),
            P("gx", "gy"), P("gx"), P("gx"), P("gx"), P("gx", "gy"), P("gy"), P("gx", "gy"), P("gx"),
        ),
        check_vma=False,
    )
```

```python
import math

import jax
import jax.numpy as jnp
from jax import lax
from jax.experimental import pallas as pl
from jax.experimental.pallas import tpu as pltpu
from jax.sharding import PartitionSpec as P

BF = jnp.bfloat16
F32 = jnp.float32
HEADS = 25
HEAD_DIM = 64
D = HEADS * HEAD_DIM
FF = 6400
SEQ = 1024
DOC = 800
ROWS = 128
QUARTER = 400
SUB = 200
FPAD = 208
FRAME = 256
TAIL = 64
NEG = -1e30
MESH = pl.DeviceIdType.MESH
VMEM = pl.BlockSpec(memory_space=pltpu.VMEM)
SMEM = pl.BlockSpec(memory_space=pltpu.SMEM)


def nt(a, b):
    return lax.dot_general(a, b, (((1,), (1,)), ((), ())), preferred_element_type=F32)


def nn(a, b):
    return lax.dot_general(a, b, (((1,), (0,)), ((), ())), preferred_element_type=F32)


def tn(a, b):
    return lax.dot_general(a, b, (((0,), (0,)), ((), ())), preferred_element_type=F32)


class Here:
    def __init__(self):
        self.z, self.gx, self.gy = (lax.axis_index(a) for a in ("dp", "gx", "gy"))
        self.y, self.xh = self.gy // 2, lax.rem(self.gy, 2)
        self.x = self.xh * 2 + self.gx // 2
        self.c = lax.rem(self.gx, 2)
        self.p = self.x * 2 + self.c

    def at(self, x, c, y, z):
        return (z, lax.rem(x, 2) * 2 + c, y * 2 + x // 2)

    def rel(self, dx=0, flip=0, dy=0, dz=0):
        c = 1 - self.c if flip else self.c
        return self.at(
            lax.rem(self.x + 4 + dx, 4), c, lax.rem(self.y + 4 + dy, 4), lax.rem(self.z + 4 + dz, 4)
        )

    def ring(self):
        return [self.rel(dx, f) for dx in range(4) for f in (0, 1) if dx or f]

    def gxd(self, d):
        return (self.z, self.gx ^ d, self.gy)

    def unit(self, i):
        if i == 3:
            return self.gy, 3
        t = 3 * self.gy + i
        return lax.rem(t, 8), t // 8

    def block(self, kind, p):
        if kind == 3:
            return p, 3
        t = kind * 8 + p
        return t // 3, lax.rem(t, 3)

    def holds(self, kind):
        return self.block(kind, self.p)[0] // 2 == self.y


def meet(peers):
    sem = pltpu.get_barrier_semaphore()
    for d in peers:
        pl.semaphore_signal(sem, inc=1, device_id=d, device_id_type=MESH)
    pl.semaphore_wait(sem, len(peers))


def push(src, dst, ss, rs, d):
    return pltpu.make_async_remote_copy(
        src_ref=src, dst_ref=dst, send_sem=ss, recv_sem=rs, device_id=d, device_id_type=MESH
    )


def stats(v):
    mean = jnp.sum(v, axis=1, keepdims=True) / D
    spread = jnp.sum(v * v, axis=1, keepdims=True) / D - mean * mean
    inv = lax.rsqrt(spread + 1e-5)
    return (v - mean) * inv, inv


def norm_back(u, gain, normed, inv):
    w = u * gain
    a = jnp.sum(w, axis=1, keepdims=True) / D
    b = jnp.sum(w * normed, axis=1, keepdims=True) / D
    return inv * (w - a - normed * b)


def cut(start, size):
    return pl.ds(start if isinstance(start, int) else pl.multiple_of(start, 16), size)


def rows_of(v):
    return jnp.sum(v, axis=0, keepdims=True)


class Copy:
    def __init__(self, desc, send_if=None, recv_if=None):
        self.desc, self.send_if, self.recv_if = desc, send_if, recv_if
        self.is_got = self.is_gone = False

    def on(self, cond, do):
        if cond is None:
            do()
        else:
            pl.when(cond)(do)

    def start(self):
        self.on(self.send_if, self.desc.start)

    def got(self):
        if not self.is_got:
            self.is_got = True
            self.on(self.recv_if, self.desc.wait_recv)

    def gone(self):
        if not self.is_gone:
            self.is_gone = True
            self.on(self.send_if, self.desc.wait_send)


class Net:
    SIZE = 360

    def __init__(self, ss, rs):
        self.ss, self.rs, self.n, self.copies = ss, rs, 0, []

    def make(self, src, dst, d, send_if=None, recv_if=None, rs=None):
        i = self.n
        self.n += 1
        assert i < self.SIZE
        c = Copy(push(src, dst, self.ss.at[i], self.rs.at[i] if rs is None else rs, d), send_if, recv_if)
        if rs is not None:
            c.is_got = True
        self.copies.append(c)
        return c

    def send(self, *args, **kw):
        c = self.make(*args, **kw)
        c.start()
        return c

    def finish(self):
        for c in self.copies:
            c.got()
            c.gone()


class Gather:
    def __init__(self, here, net, buf):
        self.h, self.net, self.buf = here, net, buf

    def row(self, dx):
        return (lax.rem(self.h.x + 4 + dx, 4) * 2 + self.h.c) * ROWS

    def go(self, dx, d, half=None):
        ref = self.buf.at[cut(self.row(dx), ROWS) if half is None else cut(self.row(dx) + 64 * half, 64)]
        return self.net.send(ref, ref, d)

    def start(self):
        h = self.h
        self.right, self.left, self.sib = h.rel(1), h.rel(-1), h.rel(0, 1)
        self.r = [self.go(0, self.right, 0), None]
        self.l = [None, self.go(0, self.left, 1)]
        self.r[1] = self.go(0, self.right, 1)
        self.l[0] = self.go(0, self.left, 0)
        self.own = self.go(0, self.sib)

    def ready(self, s):
        h = self.h
        if s == 0:
            self.own.got()
            return h.x
        if s == 1:
            self.r[0].got()
            self.rr = self.go(-1, self.right, 0)
            self.l[1].got()
            self.ll = self.go(1, self.left, 1)
            self.r[1].got()
            self.f1 = self.go(-1, self.sib)
            self.l[0].got()
            self.f2 = self.go(1, self.sib)
            self.f1.got()
            return lax.rem(h.x + 3, 4)
        if s == 2:
            self.f2.got()
            return lax.rem(h.x + 1, 4)
        self.rr.got()
        f3 = self.go(2, self.sib, 0)
        self.ll.got()
        f4 = self.go(2, self.sib, 1)
        f3.got()
        f4.got()
        for c in (*self.r, *self.l, self.own, self.rr, self.ll, self.f1, self.f2, f3, f4):
            c.gone()
        return lax.rem(h.x + 2, 4)


class Scatter:
    @staticmethod
    def scratch():
        return [
            pltpu.VMEM((4, 2, ROWS, D), BF),
            pltpu.VMEM((4, ROWS, D), BF),
            pltpu.VMEM((2, ROWS, D), BF),
            pltpu.VMEM((ROWS, D), BF),
        ]

    STEPS = (2, 1, -1, 0)

    def __init__(self, here, net, refs):
        self.h, self.net = here, net
        self.part, self.mate, self.far, self.relay = refs
        self.pair, self.out = {}, []

    def term(self, j, f):
        h = self.h
        chip = lax.rem(h.x + 4 + self.STEPS[j], 4)
        self.part[j] = f(chip).astype(BF).reshape(2, ROWS, D)
        self.pair[j] = self.net.send(self.part.at[j, 1 - h.c], self.mate.at[j], h.rel(0, 1))

    def total(self, j):
        self.pair[j].got()
        return self.part[j, self.h.c].astype(F32) + self.mate[j].astype(F32)

    def link(self, j, half, dst, dx):
        src = self.part.at[j, self.h.c, pl.ds(64 * half, 64)]
        c = self.net.send(src, dst, self.h.rel(dx))
        self.out.append(c)
        return c

    def first(self):
        self.part[0, self.h.c] = self.total(0).astype(BF)
        self.in_r = self.link(0, 0, self.relay.at[pl.ds(0, 64)], 1)
        self.in_l = self.link(0, 1, self.relay.at[pl.ds(64, 64)], -1)

    def side(self, j):
        half = 1 if j == 1 else 0
        self.part[j, self.h.c] = self.total(j).astype(BF)
        c = self.link(j, half, self.far.at[j - 1, pl.ds(64 * half, 64)], self.STEPS[j])
        self.ends = getattr(self, "ends", []) + [c]

    def relayed(self):
        for j, half, c in ((1, 0, self.in_r), (2, 1, self.in_l)):
            c.got()
            span = pl.ds(64 * half, 64)
            s = self.part[j, self.h.c, span].astype(F32) + self.relay[span].astype(F32)
            self.part[j, self.h.c, span] = s.astype(BF)
            self.ends.append(self.link(j, half, self.far.at[j - 1, span], self.STEPS[j]))

    def run(self, f):
        self.term(0, f)
        self.term(1, f)
        self.first()
        self.term(2, f)
        self.side(1)
        self.term(3, f)
        self.side(2)
        self.relayed()

    def result(self):
        t = self.total(3)
        for c in self.ends:
            c.got()
        t = t + self.far[0].astype(F32) + self.far[1].astype(F32)
        for c in list(self.pair.values()) + self.out:
            c.gone()
        return t


def join(blocks):
    return jnp.concatenate(blocks, axis=1)


def set_masks(masks, begin):
    for i in range(4):
        n = 256 * (i + 1)
        b = lax.broadcasted_iota(jnp.int32, (n, 256), 0)
        a = lax.broadcasted_iota(jnp.int32, (n, 256), 1) + 256 * i

        def doc(t):
            return (t >= begin).astype(jnp.int32) + (t >= begin + DOC).astype(jnp.int32)

        masks[MASK_AT[i] : MASK_AT[i] + n] = jnp.where((b <= a) & (doc(a) == doc(b)), 0.0, NEG)


def probs_t(key, query, mask):
    s = nt(key, query) + mask
    e = jnp.exp(s - jnp.max(s, axis=0, keepdims=True))
    return e * (1.0 / jnp.sum(e, axis=0, keepdims=True))


def halves(v):
    return v[:, :HEAD_DIM], v[:, HEAD_DIM:]


MASK_AT = (0, 256, 768, 1536)
A_ROWS, B_ROWS = 112, 96
HALF = 96
EXTRA = 32
VW = 1664 + 256


def layer_kernel(
    segs, tok, grd, wa, ff, vec, qkvb, fcb,
    layer_out, input_grad, ffo, wao, vsum, qf, saved,
    *refs,
):
    (
        fs, ga, ba, wt, fw, qkv, att, gat, masks, hid, gpre, dk, dv,
        a0, a1, a2, a3, b0, b1, b2, b3,
        rt, rg, rwa, rff, frames, tsend, trecv, scr, rv, vecs, seg, fcbs,
        res, gsave, rows, gown, yr, x2, s2, wx, tl, igot, v0, vy, vz, vx,
        ss, rs, rsw, rsx, rseg, rsm, rsn, rst, loc, hz, hb, hy,
    ) = refs
    h = Here()
    net = Net(ss, rs)
    par = lax.rem(h.z, 2)
    last = h.p == 7
    ys = [h.rel(dy=d) for d in (1, 2, 3)]
    zp, zm, zo = h.rel(dz=1), h.rel(dz=-1), h.rel(dz=2)
    plane = [h.rel(dx, f, dy) for dy in range(4) for dx in range(4) for f in (0, 1) if dx or f or dy]
    meet(plane + [zp, zm, zo])

    for k, i in enumerate((2, 3)):
        tsend[k] = wa[i].astype(F32)[SUB - TAIL :].astype(BF)
    tail = net.send(tsend, trecv, (h.z, h.gx, lax.rem(h.gy + 1, 8)))

    def by_gx(src, dst):
        out = [net.send(src.at[h.gx ^ d], dst.at[h.gx], h.gxd(d)) for d in (1, 2, 3)]
        return out

    toks = by_gx(tok, rt)
    vgot = [net.send(vec, rv.at[h.gx], h.gxd(d)) for d in (1, 2, 3)]
    rt[h.gx] = tok[h.gx]
    rv[h.gx] = vec[...]
    at_zero = h.gy == 0
    alone = at_zero & (h.gx == 0)
    for j in range(8):
        me = (h.gx == 0) if j == 0 else False
        cond = at_zero & jnp.logical_not(me)
        net.send(segs, seg, h.at(j // 2, j % 2, h.gx, h.z), send_if=cond, rs=rseg.at[0])

    @pl.when(alone)
    def _():
        seg[...] = segs[...]

    fgot = [net.send(fcb, fcbs.at[h.y], d) for d in ys]
    fcbs[h.y] = fcb[...]

    row = lax.broadcasted_iota(jnp.int32, (FRAME, QUARTER), 0)
    half_own = cut(HALF * par, HALF)
    extra_own = cut(192 + EXTRA * par, EXTRA)
    fsends = []
    for i in (1, 2, 0, 3):
        p, kind = h.unit(i)
        slot = i // 3
        if i == 0:
            tail.got()
        before = wa[i - 1].astype(F32)[SUB - TAIL :] if i in (1, 2) else trecv[i // 3].astype(F32)
        scr[pl.ds(pl.multiple_of(8 * p, 8), TAIL)] = before
        scr[pl.ds(pl.multiple_of(8 * p + TAIL, 8), SUB)] = wa[i].astype(F32)
        frames[i] = jnp.where((row < 192) | (p == 7), scr[TAIL : TAIL + FRAME], 0.0).astype(BF)
        dest = h.at(p // 2, lax.rem(p, 2), h.y, h.z)
        mine = p == h.p
        far = jnp.logical_not(mine)
        fsends.append(net.send(
            frames.at[i, half_own], rwa.at[slot, h.gx, pl.ds(0, HALF)], dest,
            send_if=far, rs=rsw.at[slot, h.gx],
        ))
        fsends.append(net.send(
            frames.at[i, extra_own], rwa.at[slot, h.gx, pl.ds(HALF, EXTRA)], dest,
            send_if=far & (p == 7), rs=rsx.at[slot, h.gx],
        ))

        @pl.when(mine)
        def _(i=i, slot=slot):
            rwa[slot, h.gx, 0:HALF] = frames[i, half_own]
            rwa[slot, h.gx, HALF : HALF + EXTRA] = frames[i, extra_own]

    for c in vgot:
        c.got()
    vecs[...] = join([rv[g] for g in range(4)])
    for c in toks:
        c.got()
    x = join([rt[g] for g in range(4)])
    rows[...] = x
    normed, _ = stats(x.astype(F32))
    my_rows = cut(ROWS * h.p, ROWS)
    fs[my_rows] = (normed * vecs[0:1] + vecs[1:2]).astype(BF)
    gather = Gather(h, net, fs)
    gather.start()
    ffs = [
        net.send(ff.at[h.gx ^ d, par], rff.at[h.gx], h.gxd(d)) for d in (1, 2, 3)
    ]
    ff_own = pltpu.make_async_copy(ff.at[h.gx, par], rff.at[h.gx], loc.at[0])
    ff_own.start()
    grds = by_gx(grd, rg)
    rg[h.gx] = grd[h.gx]

    by_y = {}
    for kind in range(4):
        slot = kind // 3
        held = h.holds(kind)
        gy, _ = h.block(kind, h.p)
        xh = lax.rem(gy, 2)
        for g in range(4):
            other = held & jnp.logical_not((g == h.gx) & (xh == h.xh))

            @pl.when(other)
            def _(slot=slot, g=g):
                push(
                    frames.at[0, pl.ds(0, HALF)], rwa.at[slot, g, pl.ds(0, HALF)], ss.at[0],
                    rsw.at[slot, g], ys[0],
                ).wait_recv()

            @pl.when(other & last)
            def _(slot=slot, g=g):
                push(
                    frames.at[0, pl.ds(0, EXTRA)], rwa.at[slot, g, pl.ds(HALF, EXTRA)], ss.at[0],
                    rsx.at[slot, g], ys[0],
                ).wait_recv()

        @pl.when(held)
        def _(kind=kind, slot=slot):
            wt[kind, half_own] = join([rwa[slot, g, 0:HALF] for g in range(4)])

        @pl.when(held & last)
        def _(kind=kind, slot=slot):
            wt[kind, extra_own] = join([rwa[slot, g, HALF : HALF + EXTRA] for g in range(4)])

        @pl.when(jnp.logical_not(last))
        def _(kind=kind):
            wt[kind, 192:FRAME] = jnp.zeros((64, D), BF)

        free = jnp.logical_not(held)
        for d in (1, 2, 3):
            comes = h.block(kind, h.p)[0] // 2 == lax.rem(h.y + 4 - d, 4)
            for what, cond in ((half_own, None), (extra_own, last)):
                s_if = held if cond is None else held & cond
                r_if = comes if cond is None else comes & cond
                ref = wt.at[kind, what]
                by_y.setdefault(kind, []).append(
                    net.send(ref, ref, ys[d - 1], send_if=s_if, recv_if=r_if)
                )

    by_z = {}

    def pass_z(kind):
        for c in by_y[kind]:
            c.got()
        for base, size, cond in ((HALF * par, 48, None), (192 + EXTRA * par, 16, last)):
            for off, d in ((0, zm), (size, zp)):
                ref = wt.at[kind, cut(base + off, size)]
                by_z.setdefault(kind, []).append(net.send(ref, ref, d, send_if=cond, recv_if=cond))

    gather.ready(0)
    gather.ready(1)
    for kind in range(3):
        pass_z(kind)
    gather.ready(2)
    gather.ready(3)

    ff_own.wait()
    for c in ffs:
        c.got()
    fslab = lambda y, k: cut((2 * y + k) * FPAD, FPAD)
    mine_ff = fslab(h.y, par)
    fw[mine_ff] = join([rff[g] for g in range(4)])
    ff_y = [net.send(fw.at[mine_ff], fw.at[mine_ff], d) for d in ys]
    ff_z = []

    def ff_pass(d):
        if d:
            ff_y[d - 1].got()
        base = (2 * lax.rem(h.y + 4 - d, 4) + par) * FPAD
        for off, size, to in ((0, A_ROWS, zm), (A_ROWS, B_ROWS, zp)):
            ref = fw.at[cut(base + off, size)]
            ff_z.append(net.send(ref, ref, to))

    ff_pass(0)
    for c in grds:
        c.got()
    gown[...] = join([rg[g] for g in range(4)])
    ga[my_rows] = gown[...]
    ggather = Gather(h, net, ga)
    ggather.start()

    @pl.when(jnp.logical_not(alone))
    def _():
        push(segs, seg, ss.at[0], rseg.at[0], ys[0]).wait_recv()

    begin = jnp.sum((seg[0:1] == 0).astype(F32), axis=1, keepdims=True).astype(jnp.int32)
    set_masks(masks, begin)
    for kind in range(3):
        for c in by_z[kind]:
            c.got()

    @pl.loop(0, 4)
    def _(chip):
        span = cut(256 * chip, 256)
        for kind in range(3):
            qkv[kind, span] = (nt(fs[span], wt[kind]) + qkvb[kind : kind + 1]).astype(BF)

    save = pltpu.make_async_copy(fs, saved, loc.at[1])
    save.start()
    for c in fsends:
        c.gone()
    pass_z(3)
    ggather.ready(0)
    ggather.ready(1)

    def attend(pair):
        lanes = pl.ds(128 * pair, 128)
        for i in range(4):
            n = 256 * (i + 1)
            mask = masks[MASK_AT[i] : MASK_AT[i] + n]
            outs = []
            for q, k, v in zip(
                halves(qkv[0, 256 * i : n, lanes]), halves(qkv[1, 0:n, lanes]), halves(qkv[2, 0:n, lanes])
            ):
                outs.append(tn(probs_t(k, q * 0.125, mask).astype(BF), v))
            att[256 * i : n, lanes] = join(outs).astype(BF)

    attend(0)
    ff_pass(1)
    ff_pass(3)
    ggather.ready(2)
    ggather.ready(3)
    attend(1)
    ff_pass(2)
    save.wait()
    for c in by_z[3]:
        c.got()

    sa = Scatter(h, net, (a0, a1, a2, a3))
    sa.run(lambda chip: nn(att[cut(256 * chip, 256)], wt[3]))
    r = rows[...].astype(F32) + sa.result() + vecs[2:3]
    res[...] = r
    normed, _ = stats(r)

    fs[my_rows] = (normed * vecs[3:4] + vecs[4:5]).astype(BF)
    gather = Gather(h, net, fs)
    gather.start()
    for c in ff_z + fgot:
        c.got()
    v0[...] = jnp.zeros_like(v0)
    for s in range(4):
        chip = gather.ready(s)

        @pl.loop(0, 4)
        def _(y, chip=chip):
            span = cut(256 * chip, 256)
            v = nt(fs[span], fw[fslab(y, 0)]) + fcbs[y, 0:1]
            up = nt(ga[span], fw[fslab(y, 1)])
            t = jnp.tanh(0.7978845608028654 * (v + 0.044715 * v * v * v))
            hid[y, span] = (0.5 * v * (1.0 + t)).astype(BF)
            slope = 0.5 * (1.0 + t) + 0.5 * v * (1.0 - t * t) * (
                0.7978845608028654 * (1.0 + 3 * 0.044715 * v * v)
            )
            gpre[y, span] = (up * slope).astype(BF)

    def total(src, k):
        def f(chip):
            return sum(nn(src[y, cut(256 * chip, 256)], fw[fslab(y, k)]) for y in range(4))

        return f

    sb = Scatter(h, net, (b0, b1, b2, b3))
    sb.run(total(gpre, 0))
    for c in ff_y + ff_z:
        c.gone()
    sa = Scatter(h, net, (a0, a1, a2, a3))
    for j in range(4):
        sa.term(j, total(hid, 1))

    @pl.loop(0, 4)
    def _(y):
        fw[fslab(y, 0)] = tn(gpre[y], fs[...]).astype(BF)
        fw[fslab(y, 1)] = tn(hid[y], ga[...]).astype(BF)

    for y in range(4):
        v0[2 + y : 3 + y, 1664 : 1664 + FPAD] = rows_of(gpre[y].astype(F32))
    for d in (zm, zp):
        pl.semaphore_signal(hz, inc=1, device_id=d, device_id_type=MESH)
    load = pltpu.make_async_copy(saved, fs, loc.at[1])
    load.start()

    gs = sb.result()
    normed, inv = stats(res[...])
    up = gown[...].astype(F32)
    gres = up + norm_back(gs, vecs[3:4], normed, inv)
    gsave[...] = gres
    low = gres.astype(BF)
    ba[my_rows] = low
    gather = Gather(h, net, ba)
    gather.start()
    v0[2:3, 0:D] = rows_of(gs * normed)
    v0[3:4, 0:D] = rows_of(gs)
    v0[4:5, 0:D] = rows_of(low.astype(F32))
    v0[5:6, 0:D] = rows_of(up)

    pl.semaphore_wait(hz, 2)
    one = {}
    for d in (2, 1, 3, 0):
        y = lax.rem(h.y + d, 4)
        base = (2 * y + 1 - par) * FPAD
        one[d] = [
            net.send(fw.at[cut(base + off, size)], ga.at[cut(FPAD * y + off, size)], to)
            for off, size, to in ((0, A_ROWS, zm), (A_ROWS, B_ROWS, zp))
        ]

    for s in range(4):
        chip = gather.ready(s)
        span = cut(256 * chip, 256)
        gat[span] = nt(ba[span], wt[3]).astype(BF)
    for j in (1, 2):
        if j == 1:
            sa.first()
        sa.side(j)
    for kind in range(4):
        for c in by_y[kind] + by_z[kind]:
            c.gone()
    wt[3] = tn(att[...], ba[...]).astype(BF)
    for d in (zm, zp):
        pl.semaphore_signal(hb, inc=1, device_id=d, device_id_type=MESH)

    two = {}

    def collect(d):
        for c in one[d]:
            c.got()
        y = lax.rem(h.y + d, 4)
        span = fslab(y, par)
        fw[span] = (fw[span].astype(F32) + ga[cut(FPAD * y, FPAD)].astype(F32)).astype(BF)
        if d:
            two[d] = net.send(fw.at[span], yr.at[d - 1, pl.ds(0, FPAD)], ys[d - 1])

    def attend_back(pair):
        lanes = pl.ds(128 * pair, 128)
        dk[...] = jnp.zeros_like(dk)
        dv[...] = jnp.zeros_like(dv)
        for i in range(4):
            n = 256 * (i + 1)
            mask = masks[MASK_AT[i] : MASK_AT[i] + n]
            dqs, dks, dvs = [], [], []
            for q, k, v, g in zip(
                halves(qkv[0, 256 * i : n, lanes]), halves(qkv[1, 0:n, lanes]),
                halves(qkv[2, 0:n, lanes]), halves(gat[256 * i : n, lanes]),
            ):
                q = q * 0.125
                probs = probs_t(k, q, mask)
                dvs.append(nn(probs.astype(BF), g))
                prod = probs * nt(v, g)
                ds = (prod - probs * jnp.sum(prod, axis=0, keepdims=True)).astype(BF)
                dks.append(nn(ds, q))
                dqs.append(tn(ds, k) * 0.125)
            dv[:n] += join(dvs)
            dk[:n] += join(dks)
            qkv[0, 256 * i : n, lanes] = join(dqs).astype(BF)
        qkv[1, :, lanes] = dk[...].astype(BF)
        qkv[2, :, lanes] = dv[...].astype(BF)

    attend_back(0)
    sa.relayed()
    collect(2)
    collect(1)
    attend_back(1)
    collect(3)
    collect(0)

    for c in toks:
        c.gone()
    out = (res[...] + sa.result() + vecs[5:6]).astype(BF)
    for g in range(4):
        rt[g] = out[:, QUARTER * g : QUARTER * (g + 1)]
    by_gx(rt, layer_out)
    lo_own = pltpu.make_async_copy(rt.at[h.gx], layer_out.at[h.gx], loc.at[2])
    lo_own.start()

    sb = Scatter(h, net, (b0, b1, b2, b3))
    sb.run(lambda chip: sum(nn(qkv[k, cut(256 * chip, 256)], wt[k]) for k in range(3)))
    load.wait()

    @pl.loop(0, 3)
    def _(kind):
        wt[kind] = tn(qkv[kind], fs[...]).astype(BF)

    pl.semaphore_wait(hb, 2)
    wone = {}
    for kind in (3, 0, 1, 2):
        for base, at, size, cond in (
            (HALF * (1 - par), 0, 48, None), (192 + EXTRA * (1 - par), HALF, 16, last),
        ):
            for k, to in ((0, zm), (1, zp)):
                wone.setdefault(kind, []).append(
                    net.send(
                        wt.at[kind, cut(base + size * k, size)],
                        ba.at[pl.ds(128 * kind + at + size * k, size)], to, send_if=cond, recv_if=cond,
                    )
                )
    v0[0:1, 1664:VW] = rows_of(qkv[0].astype(F32))
    v0[1:2, 1664:VW] = rows_of(qkv[2].astype(F32))

    s = fw[fslab(h.y, par)].astype(F32)
    for d in (1, 2, 3):
        two[d].got()
        s = s + yr[d - 1, 0:FPAD].astype(F32)
    s2[0:FPAD] = s.astype(BF)
    for d in ys:
        pl.semaphore_signal(hy, inc=1, device_id=d, device_id_type=MESH)
    three = net.send(s2.at[pl.ds(0, FPAD)], x2, zo)

    gf = sb.result()
    normed, inv = stats(rows[...].astype(F32))
    low = (gsave[...] + norm_back(gf, vecs[0:1], normed, inv)).astype(BF)
    v0[0:1, 0:D] = rows_of(gf * normed)
    v0[1:2, 0:D] = rows_of(gf)
    for c in grds:
        c.gone()
    for g in range(4):
        rg[g] = low[:, QUARTER * g : QUARTER * (g + 1)]
    igs = by_gx(rg, igot)
    igot[h.gx] = rg[h.gx]
    vys = [net.send(v0, vy.at[h.y], d) for d in ys]
    vy[h.y] = v0[...]

    three.got()
    full = (s2[0:FPAD].astype(F32) + x2[...].astype(F32)).astype(BF)
    for c in ffs:
        c.gone()
    for g in range(4):
        rff[g] = full[:, QUARTER * g : QUARTER * (g + 1)]
    four = [net.send(rff.at[h.gx ^ d], ffo.at[par, h.gx], h.gxd(d)) for d in (1, 2, 3)]
    ffo_own = pltpu.make_async_copy(rff.at[h.gx], ffo.at[par, h.gx], loc.at[3])
    ffo_own.start()
    three.gone()

    pl.semaphore_wait(hy, 3)
    wtwo = {}
    spans = ((half_own, 0, HALF, None), (extra_own, HALF, EXTRA, last))
    for kind in range(4):
        slot, held = kind // 3, h.holds(kind)
        home = h.block(kind, h.p)[0] // 2
        for c in wone[kind]:
            c.got()
        for mine, at, size, cond in spans:

            def add(mine=mine, at=at, size=size, kind=kind):
                s = wt[kind, mine].astype(F32) + ba[128 * kind + at : 128 * kind + at + size].astype(F32)
                wt[kind, mine] = s.astype(BF)

            if cond is None:
                add()
            else:
                pl.when(cond)(add)
            for d in (1, 2, 3):
                goes, comes = lax.rem(h.y + d, 4) == home, held
                if cond is not None:
                    goes, comes = goes & cond, comes & cond
                wtwo.setdefault(kind, []).append(
                    net.send(
                        wt.at[kind, mine], yr.at[d - 1, pl.ds(128 * slot + at, size)], ys[d - 1],
                        send_if=goes, recv_if=comes,
                    )
                )

    for c in igs:
        c.got()
    input_grad[...] = igot[...].astype(F32)
    for c in vys:
        c.got()
    vz[h.z] = (vy[0] + vy[1]) + (vy[2] + vy[3])
    vzs = [net.send(vz.at[h.z], vz.at[h.z], h.rel(dz=d)) for d in (1, 2, 3)]

    ffo_own.wait()
    for c in four:
        c.got()
    for at, size, to in ((0, A_ROWS, zm), (A_ROWS, B_ROWS, zp)):
        ref = ffo.at[par, :, pl.ds(at, size)]
        net.send(ref, ref, to)

    wthree = {}
    for kind in range(4):
        slot, held = kind // 3, h.holds(kind)
        for c in wtwo[kind]:
            c.got()
        for mine, at, size, cond in spans:
            ok = held if cond is None else held & cond
            low_at = 128 * slot + at

            @pl.when(ok)
            def _(kind=kind, mine=mine, size=size, low_at=low_at):
                s = wt[kind, mine].astype(F32)
                for d in range(3):
                    s = s + yr[d, low_at : low_at + size].astype(F32)
                s2[low_at : low_at + size] = s.astype(BF)

            wthree.setdefault(kind, []).append(
                net.send(
                    s2.at[pl.ds(low_at, size)], wx.at[pl.ds(low_at, size)], zo, send_if=ok, recv_if=ok
                )
            )

    for c in vzs:
        c.got()
    vx[h.p] = (vz[0] + vz[1]) + (vz[2] + vz[3])
    vxs = [net.send(vx.at[h.p], vx.at[h.p], d) for d in h.ring()]

    for kind in range(4):
        slot, held = kind // 3, h.holds(kind)
        gy, place = h.block(kind, h.p)
        gyt, placet = h.block(kind, h.p - 1)
        xh, xht, yt = lax.rem(gy, 2), lax.rem(gyt, 2), gyt // 2
        for c in wthree[kind]:
            c.got()
        for mine, at, size, cond in spans:
            ok = held if cond is None else held & cond
            low_at = 128 * slot + at

            @pl.when(ok)
            def _(slot=slot, at=at, size=size, low_at=low_at):
                span = slice(low_at, low_at + size)
                full = (s2[span].astype(F32) + wx[span].astype(F32)).astype(BF)
                for g in range(4):
                    rwa[slot, g, at : at + size] = full[:, QUARTER * g : QUARTER * (g + 1)]

            for g in range(4):
                same = (g == h.gx) & (xh == h.xh)
                net.send(
                    rwa.at[slot, g, pl.ds(at, size)], frames.at[place, mine], (h.z, g, gy),
                    send_if=ok & jnp.logical_not(same), rs=(rsm if cond is None else rsn).at[place],
                )

                @pl.when(ok & same)
                def _(slot=slot, g=g, place=place, mine=mine, at=at, size=size):
                    frames[place, mine] = rwa[slot, g, at : at + size]

        for g in range(4):
            same = (g == h.gx) & (xht == h.xh) & (yt == h.y)
            ok = held & (h.p > 0) & (par == 0)
            net.send(
                rwa.at[slot, g, pl.ds(0, TAIL)], tl.at[placet], (h.z, g, gyt),
                send_if=ok & jnp.logical_not(same), rs=rst.at[placet],
            )

            @pl.when(ok & same)
            def _(slot=slot, g=g, placet=placet):
                tl[placet] = rwa[slot, g, 0:TAIL]

    wfive = {}
    for i in range(4):
        p, kind = h.unit(i)
        four_heads = p == 7
        far = p != h.p

        @pl.when(far)
        def _(i=i):
            push(
                frames.at[0, pl.ds(0, HALF)], frames.at[i, pl.ds(0, HALF)], ss.at[0], rsm.at[i], ys[0]
            ).wait_recv()

        @pl.when(far & four_heads)
        def _(i=i):
            push(
                frames.at[0, pl.ds(0, EXTRA)], frames.at[i, pl.ds(0, EXTRA)], ss.at[0], rsn.at[i], ys[0]
            ).wait_recv()

        follow = (p + 1) // 2 if i == 3 else (kind * 8 + p + 1) // 6
        has_tail = jnp.logical_not(four_heads)

        @pl.when(has_tail & (par == 0) & jnp.logical_not((p + 1 == h.p) & (follow == h.y)))
        def _(i=i):
            push(tl.at[0], tl.at[i], ss.at[0], rst.at[i], ys[0]).wait_recv()

        for base, size, cond in (
            (HALF * par, 48, None), (192 + EXTRA * par, 16, four_heads),
        ):
            for k, to in ((0, zm), (1, zp)):
                ref = frames.at[i, cut(base + size * k, size)]
                wfive.setdefault(i, []).append(net.send(ref, ref, to, send_if=cond, recv_if=cond))
        for k, to in ((0, zm), (1, zp)):
            ref = tl.at[i, pl.ds(32 * k, 32)]
            wfive[i].append(
                net.send(
                    ref, ref, to, send_if=has_tail & (par == 0), recv_if=has_tail & (par == 1)
                )
            )

    for c in vxs:
        c.got()
    total_v = vx[0]
    for p in range(1, 8):
        total_v = total_v + vx[p]
    vsum[...] = total_v[:, 0:D]
    qf[...] = vx[:, :, 1664:VW]
    for i in range(4):
        p, _ = h.unit(i)
        for c in wfive[i]:
            c.got()
        scr[0:FRAME] = frames[i].astype(F32)

        @pl.when(p < 7)
        def _(i=i):
            scr[192 : 192 + TAIL] = tl[i].astype(F32)

        wao[i] = scr[pl.ds(pl.multiple_of(8 * p, 8), SUB)].astype(BF)

    lo_own.wait()
    net.finish()


def layer(segs, tok, grd, wa, ff, vec, qkvb, fcb):
    any_ = pl.BlockSpec(memory_space=pl.ANY)
    scratch = [
        pltpu.VMEM((SEQ, D), BF),
        pltpu.VMEM((SEQ, D), BF),
        pltpu.VMEM((SEQ, D), BF),
        pltpu.VMEM((4, FRAME, D), BF),
        pltpu.VMEM((8 * FPAD, D), BF),
        pltpu.VMEM((3, SEQ, FRAME), BF),
        pltpu.VMEM((SEQ, FRAME), BF),
        pltpu.VMEM((SEQ, FRAME), BF),
        pltpu.VMEM((2560, 256), F32),
        pltpu.VMEM((4, SEQ, FPAD), BF),
        pltpu.VMEM((4, SEQ, FPAD), BF),
        pltpu.VMEM((SEQ, 2 * HEAD_DIM), F32),
        pltpu.VMEM((SEQ, 2 * HEAD_DIM), F32),
        *Scatter.scratch(),
        *Scatter.scratch(),
        pltpu.VMEM((4, ROWS, QUARTER), BF),
        pltpu.VMEM((4, ROWS, QUARTER), BF),
        pltpu.VMEM((2, 4, HALF + EXTRA, QUARTER), BF),
        pltpu.VMEM((4, FPAD, QUARTER), BF),
        pltpu.VMEM((4, FRAME, QUARTER), BF),
        pltpu.VMEM((2, TAIL, QUARTER), BF),
        pltpu.VMEM((2, TAIL, QUARTER), BF),
        pltpu.VMEM((336, QUARTER), F32),
        pltpu.VMEM((4, 8, QUARTER), F32),
        pltpu.VMEM((8, D), F32),
        pltpu.VMEM((8, 128), jnp.int32),
        pltpu.VMEM((4, 8, FPAD), F32),
        pltpu.VMEM((ROWS, D), F32),
        pltpu.VMEM((ROWS, D), F32),
        pltpu.VMEM((ROWS, D), BF),
        pltpu.VMEM((ROWS, D), BF),
        pltpu.VMEM((3, FRAME, D), BF),
        pltpu.VMEM((FPAD, D), BF),
        pltpu.VMEM((FRAME, D), BF),
        pltpu.VMEM((FRAME, D), BF),
        pltpu.VMEM((4, TAIL, QUARTER), BF),
        pltpu.VMEM((4, ROWS, QUARTER), BF),
        pltpu.VMEM((8, VW), F32),
        pltpu.VMEM((4, 8, VW), F32),
        pltpu.VMEM((4, 8, VW), F32),
        pltpu.VMEM((8, 8, VW), F32),
        pltpu.SemaphoreType.DMA((Net.SIZE,)),
        pltpu.SemaphoreType.DMA((Net.SIZE,)),
        pltpu.SemaphoreType.DMA((2, 4)),
        pltpu.SemaphoreType.DMA((2, 4)),
        pltpu.SemaphoreType.DMA((1,)),
        pltpu.SemaphoreType.DMA((4,)),
        pltpu.SemaphoreType.DMA((4,)),
        pltpu.SemaphoreType.DMA((4,)),
        pltpu.SemaphoreType.DMA((4,)),
        pltpu.SemaphoreType.REGULAR,
        pltpu.SemaphoreType.REGULAR,
        pltpu.SemaphoreType.REGULAR,
    ]
    return pl.pallas_call(
        layer_kernel,
        out_shape=[
            jax.ShapeDtypeStruct((4, ROWS, QUARTER), BF),
            jax.ShapeDtypeStruct((4, ROWS, QUARTER), F32),
            jax.ShapeDtypeStruct((2, 4, FPAD, QUARTER), BF),
            jax.ShapeDtypeStruct((4, SUB, QUARTER), BF),
            jax.ShapeDtypeStruct((8, D), F32),
            jax.ShapeDtypeStruct((8, 8, 256), F32),
            jax.ShapeDtypeStruct((SEQ, D), BF),
        ],
        in_specs=[VMEM, VMEM, VMEM, VMEM, any_, VMEM, VMEM, VMEM],
        out_specs=[any_, VMEM, any_, VMEM, VMEM, VMEM, any_],
        scratch_shapes=scratch,
        compiler_params=pltpu.CompilerParams(
            collective_id=0, has_side_effects=True, vmem_limit_bytes=64 * 2**20 - 2**16
        ),
        name="layer",
    )(segs, tok, grd, wa, ff, vec, qkvb, fcb)


def per_device(
    tokens_in, segments, norm1_gain, norm1_bias, qkv_weight, query_bias, value_bias, proj_weight,
    proj_bias, norm2_gain, norm2_bias, fc_weight, fc_bias, out_weight, out_bias, out_grad,
):
    gx, gy = lax.axis_index("gx"), lax.axis_index("gy")
    y, xh = gy // 2, lax.rem(gy, 2)
    p = xh * 4 + gx
    wa = jnp.concatenate([qkv_weight.T.reshape(3, SUB, QUARTER), proj_weight.T[None]])
    ff = jnp.stack(
        [fc_weight.T.reshape(4, SUB, QUARTER), out_weight.T.reshape(4, SUB, QUARTER)], axis=1
    )
    ff = jnp.pad(ff, ((0, 0), (0, 0), (0, FPAD - SUB), (0, 0)))
    zero = jnp.zeros_like(norm1_gain)
    vec = jnp.stack(
        [norm1_gain, norm1_bias, proj_bias, norm2_gain, norm2_bias, out_bias, zero, zero]
    )
    valid = (jnp.arange(FRAME) < 192) | (p == 7)
    qb = jnp.where(valid, lax.dynamic_slice_in_dim(query_bias, 192 * p, FRAME), 0.0)
    vb = jnp.where(valid, lax.dynamic_slice_in_dim(value_bias, 192 * p, FRAME), 0.0)
    nil = jnp.zeros_like(qb)
    qkvb = jnp.stack([qb, nil, vb, nil, nil, nil, nil, nil])
    fcb = jnp.pad(lax.dynamic_slice_in_dim(fc_bias, SUB * gx, SUB), (0, FPAD - SUB))
    fcb = jnp.broadcast_to(fcb, (8, FPAD))
    layer_out, input_grad, ffo, wao, vsum, qf, _ = layer(
        jnp.broadcast_to(segments, (8, ROWS)),
        tokens_in.reshape(4, ROWS, QUARTER), out_grad.reshape(4, ROWS, QUARTER),
        wa, ff, vec, qkvb, fcb,
    )
    mine = lax.dynamic_slice_in_dim(vsum, QUARTER * gx, QUARTER, 1)

    def heads(v):
        return jnp.concatenate([v[:, :192].reshape(8 * 192), v[7, 192:]])

    fcp = lax.dynamic_slice(qf, (4 * xh, 2 + y, 0), (4, 1, SUB)).reshape(4 * SUB)

    def whole(v):
        return v[:, :SUB].reshape(4 * SUB, QUARTER).T.astype(F32)

    return (
        layer_out.reshape(4 * ROWS, QUARTER),
        input_grad.reshape(4 * ROWS, QUARTER),
        mine[0],
        mine[1],
        wao[0:3].reshape(3 * SUB, QUARTER).T.astype(F32),
        heads(qf[:, 0]),
        heads(qf[:, 1]),
        wao[3].T.astype(F32),
        mine[4],
        mine[2],
        mine[3],
        whole(ffo[0]),
        fcp,
        whole(ffo[1]),
        mine[5],
    )


def solution(mesh):
    return jax.shard_map(
        per_device,
        mesh=mesh,
        in_specs=(
            P(("dp", "gy"), "gx"), P(("dp", "gx"), "gy"), P("gx"), P("gx"), P("gx", "gy"), P(), P(),
            P("gx", "gy"), P("gx"), P("gx"), P("gx"), P("gx", "gy"), P("gy"), P("gx", "gy"), P("gx"),
            P(("dp", "gy"), "gx"),
        ),
        out_specs=(
            P(("dp", "gy"), "gx"), P(("dp", "gy"), "gx"), P("gx"), P("gx"), P("gx", "gy"), P(), P(),
            P("gx", "gy"), P("gx"), P("gx"), P("gx"), P("gx", "gy"), P("gy"), P("gx", "gy"), P("gx"),
        ),
        check_vma=False,
    )
```

```python
import math

import jax
import jax.numpy as jnp
from jax import lax
from jax.experimental import pallas as pl
from jax.experimental.pallas import tpu as pltpu
from jax.sharding import PartitionSpec as P

BF = jnp.bfloat16
F32 = jnp.float32
HEADS = 25
HEAD_DIM = 64
D = HEADS * HEAD_DIM
FF = 6400
SEQ = 1024
DOC = 800
ROWS = 128
QUARTER = 400
SUB = 200
FPAD = 208
FRAME = 256
TAIL = 64
NEG = -1e30
MESH = pl.DeviceIdType.MESH
VMEM = pl.BlockSpec(memory_space=pltpu.VMEM)
SMEM = pl.BlockSpec(memory_space=pltpu.SMEM)


def nt(a, b):
    return lax.dot_general(a, b, (((1,), (1,)), ((), ())), preferred_element_type=F32)


def nn(a, b):
    return lax.dot_general(a, b, (((1,), (0,)), ((), ())), preferred_element_type=F32)


def tn(a, b):
    return lax.dot_general(a, b, (((0,), (0,)), ((), ())), preferred_element_type=F32)


class Here:
    def __init__(self):
        self.z, self.gx, self.gy = (lax.axis_index(a) for a in ("dp", "gx", "gy"))
        self.y, self.xh = self.gy // 2, lax.rem(self.gy, 2)
        self.x = self.xh * 2 + self.gx // 2
        self.c = lax.rem(self.gx, 2)
        self.p = self.x * 2 + self.c

    def at(self, x, c, y, z):
        return (z, lax.rem(x, 2) * 2 + c, y * 2 + x // 2)

    def rel(self, dx=0, flip=0, dy=0, dz=0):
        c = 1 - self.c if flip else self.c
        return self.at(
            lax.rem(self.x + 4 + dx, 4), c, lax.rem(self.y + 4 + dy, 4), lax.rem(self.z + 4 + dz, 4)
        )

    def ring(self):
        return [self.rel(dx, f) for dx in range(4) for f in (0, 1) if dx or f]

    def gxd(self, d):
        return (self.z, self.gx ^ d, self.gy)

    def unit(self, i):
        if i == 3:
            return self.gy, 3
        t = 3 * self.gy + i
        return lax.rem(t, 8), t // 8

    def block(self, kind, p):
        if kind == 3:
            return p, 3
        t = kind * 8 + p
        return t // 3, lax.rem(t, 3)

    def holds(self, kind):
        return self.block(kind, self.p)[0] // 2 == self.y


def meet(peers):
    sem = pltpu.get_barrier_semaphore()
    for d in peers:
        pl.semaphore_signal(sem, inc=1, device_id=d, device_id_type=MESH)
    pl.semaphore_wait(sem, len(peers))


def push(src, dst, ss, rs, d):
    return pltpu.make_async_remote_copy(
        src_ref=src, dst_ref=dst, send_sem=ss, recv_sem=rs, device_id=d, device_id_type=MESH
    )


def stats(v):
    mean = jnp.sum(v, axis=1, keepdims=True) / D
    spread = jnp.sum(v * v, axis=1, keepdims=True) / D - mean * mean
    inv = lax.rsqrt(spread + 1e-5)
    return (v - mean) * inv, inv


def norm_back(u, gain, normed, inv):
    w = u * gain
    a = jnp.sum(w, axis=1, keepdims=True) / D
    b = jnp.sum(w * normed, axis=1, keepdims=True) / D
    return inv * (w - a - normed * b)


def cut(start, size):
    return pl.ds(start if isinstance(start, int) else pl.multiple_of(start, 16), size)


def rows_of(v):
    return jnp.sum(v, axis=0, keepdims=True)


class Copy:
    def __init__(self, desc, send_if=None, recv_if=None):
        self.desc, self.send_if, self.recv_if = desc, send_if, recv_if
        self.is_got = self.is_gone = False

    def on(self, cond, do):
        if cond is None:
            do()
        else:
            pl.when(cond)(do)

    def start(self):
        self.on(self.send_if, self.desc.start)

    def got(self):
        if not self.is_got:
            self.is_got = True
            self.on(self.recv_if, self.desc.wait_recv)

    def gone(self):
        if not self.is_gone:
            self.is_gone = True
            self.on(self.send_if, self.desc.wait_send)


class Net:
    SIZE = 424

    def __init__(self, ss, rs):
        self.ss, self.rs, self.n, self.copies = ss, rs, 0, []

    def make(self, src, dst, d, send_if=None, recv_if=None, rs=None):
        i = self.n
        self.n += 1
        assert i < self.SIZE
        c = Copy(push(src, dst, self.ss.at[i], self.rs.at[i] if rs is None else rs, d), send_if, recv_if)
        if rs is not None:
            c.is_got = True
        self.copies.append(c)
        return c

    def send(self, *args, **kw):
        c = self.make(*args, **kw)
        c.start()
        return c

    def finish(self):
        for c in self.copies:
            c.got()
            c.gone()


class Gather:
    def __init__(self, here, net, buf):
        self.h, self.net, self.buf = here, net, buf

    def row(self, dx):
        return (lax.rem(self.h.x + 4 + dx, 4) * 2 + self.h.c) * ROWS

    def go(self, dx, d, half=None):
        ref = self.buf.at[cut(self.row(dx), ROWS) if half is None else cut(self.row(dx) + 64 * half, 64)]
        return self.net.send(ref, ref, d)

    def start(self):
        h = self.h
        self.right, self.left, self.sib = h.rel(1), h.rel(-1), h.rel(0, 1)
        self.r = [self.go(0, self.right, 0), None]
        self.l = [None, self.go(0, self.left, 1)]
        self.r[1] = self.go(0, self.right, 1)
        self.l[0] = self.go(0, self.left, 0)
        self.own = self.go(0, self.sib)

    def chip(self, s):
        return lax.rem(self.h.x + (0, 3, 1, 2)[s], 4)

    def ready(self, s):
        h = self.h
        if s == 0:
            self.own.got()
            return h.x
        if s == 1:
            self.r[0].got()
            self.rr = self.go(-1, self.right, 0)
            self.l[1].got()
            self.ll = self.go(1, self.left, 1)
            self.r[1].got()
            self.f1 = self.go(-1, self.sib)
            self.l[0].got()
            self.f2 = self.go(1, self.sib)
            self.f1.got()
            return lax.rem(h.x + 3, 4)
        if s == 2:
            self.f2.got()
            return lax.rem(h.x + 1, 4)
        self.rr.got()
        f3 = self.go(2, self.sib, 0)
        self.ll.got()
        f4 = self.go(2, self.sib, 1)
        f3.got()
        f4.got()
        for c in (*self.r, *self.l, self.own, self.rr, self.ll, self.f1, self.f2, f3, f4):
            c.gone()
        return lax.rem(h.x + 2, 4)


class Scatter:
    @staticmethod
    def scratch():
        return [
            pltpu.VMEM((SEQ, D), BF),
            pltpu.VMEM((4, ROWS, D), BF),
            pltpu.VMEM((2, ROWS, D), BF),
            pltpu.VMEM((ROWS, D), BF),
        ]

    STEPS = (2, 1, -1, 0)

    def __init__(self, here, net, refs):
        self.h, self.net = here, net
        self.part, self.mate, self.far, self.relay = refs
        self.pair, self.out, self.ends = {}, [], []

    def at(self, j, c, half=None):
        base = 256 * j + ROWS * c
        return cut(base, ROWS) if half is None else cut(base + 64 * half, 64)

    def term(self, j, f):
        h = self.h
        chip = lax.rem(h.x + 4 + self.STEPS[j], 4)
        self.part[256 * j : 256 * (j + 1)] = f(chip).astype(BF)
        self.pair[j] = self.net.send(
            self.part.at[self.at(j, 1 - h.c)], self.mate.at[j], h.rel(0, 1)
        )

    def total(self, j):
        self.pair[j].got()
        return self.part[self.at(j, self.h.c)].astype(F32) + self.mate[j].astype(F32)

    def link(self, j, half, dst, dx):
        c = self.net.send(self.part.at[self.at(j, self.h.c, half)], dst, self.h.rel(dx))
        self.out.append(c)
        return c

    def first(self):
        self.part[self.at(0, self.h.c)] = self.total(0).astype(BF)
        self.in_r = self.link(0, 0, self.relay.at[pl.ds(0, 64)], 1)
        self.in_l = self.link(0, 1, self.relay.at[pl.ds(64, 64)], -1)

    def side(self, j):
        half = 1 if j == 1 else 0
        self.part[self.at(j, self.h.c)] = self.total(j).astype(BF)
        self.ends.append(self.link(j, half, self.far.at[j - 1, pl.ds(64 * half, 64)], self.STEPS[j]))

    def relayed(self):
        for j, half, c in ((1, 0, self.in_r), (2, 1, self.in_l)):
            c.got()
            span, mine = pl.ds(64 * half, 64), self.at(j, self.h.c, half)
            s = self.part[mine].astype(F32) + self.relay[span].astype(F32)
            self.part[mine] = s.astype(BF)
            self.ends.append(self.link(j, half, self.far.at[j - 1, span], self.STEPS[j]))

    def begin(self, f):
        self.term(0, f)
        self.term(1, f)
        self.first()
        self.term(2, f)
        self.side(1)
        self.term(3, f)
        self.side(2)

    def run(self, f):
        self.begin(f)
        self.relayed()

    def result(self):
        t = self.total(3)
        for c in self.ends:
            c.got()
        t = t + self.far[0].astype(F32) + self.far[1].astype(F32)
        for c in list(self.pair.values()) + self.out:
            c.gone()
        return t


def join(blocks):
    return jnp.concatenate(blocks, axis=1)


def set_masks(masks, begin):
    for i in range(4):
        n = 256 * (i + 1)
        b = lax.broadcasted_iota(jnp.int32, (n, 256), 0)
        a = lax.broadcasted_iota(jnp.int32, (n, 256), 1) + 256 * i

        def doc(t):
            return (t >= begin).astype(jnp.int32) + (t >= begin + DOC).astype(jnp.int32)

        masks[MASK_AT[i] : MASK_AT[i] + n] = jnp.where(
            (b <= a) & (doc(a) == doc(b)), 0.0, NEG
        ).astype(BF)


def probs_t(key, query, mask):
    s = nt(key, query) + mask.astype(F32)
    e = jnp.exp(s - jnp.max(s, axis=0, keepdims=True))
    return e * (1.0 / jnp.sum(e, axis=0, keepdims=True))


def halves(v):
    return v[:, :HEAD_DIM], v[:, HEAD_DIM:]


MASK_AT = (0, 256, 768, 1536)
A_ROWS, B_ROWS = 112, 96
HALF = 96
EXTRA = 32
VW = 1664 + 256


def layer_kernel(
    segs, tok, grd, wq, wp, fcw, otw, vec, bias,
    layer_out, input_grad, gwa, gfc, got_, vsum, qsum, fsum, ffo, saved,
    *refs,
):
    (
        fs, ga, ba, wt, fw, qkv, att, gat, masks, hid, gpre, dk, dv,
        a0, a1, a2, a3, b0, b1, b2, b3,
        rt, rg, rwa, rff, frames, tsend, trecv, scr, t32, stage, fbuf, rv, vecs, seg, fcb, fcbs,
        res, gsave, rows, yr, s2, wx, tl, v0, vy, vz, vx,
        ss, rs, rsw, rsx, rseg, rsm, rsn, rst, loc, hz, hb, hy, ho,
    ) = refs
    h = Here()
    net = Net(ss, rs)
    par = lax.rem(h.z, 2)
    last = h.p == 7
    ys = [h.rel(dy=d) for d in (1, 2, 3)]
    zp, zm, zo = h.rel(dz=1), h.rel(dz=-1), h.rel(dz=2)
    plane = [h.rel(dx, f, dy) for dy in range(4) for dx in range(4) for f in (0, 1) if dx or f or dy]
    everyone = plane + [zp, zm, zo]
    barrier = pltpu.get_barrier_semaphore()
    for d in everyone:
        pl.semaphore_signal(barrier, inc=1, device_id=d, device_id_type=MESH)

    @pl.when(par == 0)
    def _():
        pltpu.make_async_copy(fcw, stage, loc.at[0]).start()

    @pl.when(par == 1)
    def _():
        pltpu.make_async_copy(otw, stage, loc.at[0]).start()

    t32[0 : 3 * SUB] = jnp.transpose(wq[...]).astype(F32)
    t32[3 * SUB : 4 * SUB] = jnp.transpose(wp[...]).astype(F32)

    def sub_tail(i):
        return t32[SUB * (i + 1) - TAIL : SUB * (i + 1)]

    for k, i in enumerate((2, 3)):
        tsend[k] = sub_tail(i).astype(BF)
    row = lax.broadcasted_iota(jnp.int32, (FRAME, QUARTER), 0)
    half_own = cut(HALF * par, HALF)
    extra_own = cut(192 + EXTRA * par, EXTRA)

    def frame(i, before):
        p, _ = h.unit(i)
        scr[pl.ds(pl.multiple_of(8 * p, 8), TAIL), 0:QUARTER] = before
        scr[pl.ds(pl.multiple_of(8 * p + TAIL, 8), SUB), 0:QUARTER] = t32[SUB * i : SUB * (i + 1)]
        frames[i] = jnp.where((row < 192) | (p == 7), scr[TAIL : TAIL + FRAME, 0:QUARTER], 0.0).astype(BF)

    fsends = []

    def send_frame(i):
        p, _ = h.unit(i)
        slot = i // 3
        dest = h.at(p // 2, lax.rem(p, 2), h.y, h.z)
        mine = p == h.p
        far = jnp.logical_not(mine)
        for src, at, size, cond, sem in (
            (half_own, 0, HALF, far, rsw), (extra_own, HALF, EXTRA, far & (p == 7), rsx),
        ):
            fsends.append(
                net.send(
                    frames.at[i, src], rwa.at[slot, h.gx, pl.ds(at, size)], dest,
                    send_if=cond, rs=sem.at[slot, h.gx],
                )
            )

        @pl.when(mine)
        def _():
            rwa[slot, h.gx, 0:HALF] = frames[i, half_own]
            rwa[slot, h.gx, HALF : HALF + EXTRA] = frames[i, extra_own]

    for i in (1, 2):
        frame(i, sub_tail(i - 1))
    pl.semaphore_wait(barrier, len(everyone))

    tail = net.send(tsend, trecv, (h.z, h.gx, lax.rem(h.gy + 1, 8)))

    def lanes_of(g):
        return pl.ds(pl.multiple_of(ROWS * g, ROWS), ROWS)

    def by_gx(src, dst):
        return [net.send(src(h.gx ^ d), dst(h.gx), h.gxd(d)) for d in (1, 2, 3)]

    toks = by_gx(lambda g: tok.at[:, lanes_of(g)], lambda g: rt.at[g])
    for i in (1, 2):
        send_frame(i)
    vgot = [net.send(vec, rv.at[h.gx], h.gxd(d)) for d in (1, 2, 3)]
    tok_own = pltpu.make_async_copy(tok.at[:, lanes_of(h.gx)], rt.at[h.gx], loc.at[2])
    tok_own.start()
    rv[h.gx] = vec[...]
    at_zero = h.gy == 0
    alone = at_zero & (h.gx == 0)
    for j in range(8):
        me = (h.gx == 0) if j == 0 else False
        cond = at_zero & jnp.logical_not(me)
        net.send(segs, seg, h.at(j // 2, j % 2, h.gx, h.z), send_if=cond, rs=rseg.at[0])

    @pl.when(alone)
    def _():
        seg[...] = segs[...]

    def pick(values, index):
        out = values[0]
        for k, v in enumerate(values[1:]):
            out = jnp.where(index == k + 1, v, out)
        return out

    for c in vgot:
        c.got()
    vecs[...] = join([rv[g] for g in range(4)])
    for c in toks:
        c.got()
    tok_own.wait()

    def turn(ref):
        return jnp.transpose(jnp.concatenate([ref[g] for g in range(4)], axis=0))

    x = turn(rt)
    rows[...] = x
    normed, _ = stats(x.astype(F32))
    my_rows = cut(ROWS * h.p, ROWS)
    fs[my_rows] = (normed * vecs[0:1] + vecs[1:2]).astype(BF)
    tail.got()
    for i in (0, 3):
        frame(i, trecv[i // 3].astype(F32))
        send_frame(i)

    gather = Gather(h, net, fs)
    gather.start()

    @pl.when(par == 0)
    def _():
        pltpu.make_async_copy(fcw, stage, loc.at[0]).wait()

    @pl.when(par == 1)
    def _():
        pltpu.make_async_copy(otw, stage, loc.at[0]).wait()

    t32[...] = jnp.transpose(stage[...]).astype(F32)
    blank = jnp.zeros((FPAD - SUB, QUARTER), F32)
    for g in range(4):
        fbuf[g] = jnp.concatenate([t32[SUB * g : SUB * (g + 1)], blank], axis=0).astype(BF)
    ffs = by_gx(lambda g: fbuf.at[g], lambda g: rff.at[g])
    rff[h.gx] = fbuf[h.gx]

    low_bias = pick([bias[2:3, SUB * g : SUB * (g + 1)] for g in range(4)], h.gx)
    fcb[...] = jnp.broadcast_to(join([low_bias, jnp.zeros((1, FPAD - SUB), F32)]), (8, FPAD))
    fgot = [net.send(fcb, fcbs.at[h.y], d) for d in ys]
    fcbs[h.y] = fcb[...]
    lane = lax.broadcasted_iota(jnp.int32, (1, FRAME), 1)
    qb, vb = (
        jnp.where(
            (lane < 192) | last, pick([bias[k : k + 1, 192 * p : 192 * p + FRAME] for p in range(8)], h.p), 0.0
        )
        for k in (0, 1)
    )
    qkvb = (qb, jnp.zeros_like(qb), vb)

    def wrow(kind, start, size):
        return cut(FRAME * kind + start, size)

    w_half = lambda kind: wrow(kind, HALF * par, HALF)
    w_extra = lambda kind: wrow(kind, 192 + EXTRA * par, EXTRA)

    def wspan(kind):
        return slice(FRAME * kind, FRAME * (kind + 1))

    def take_frames(kind):
        slot = kind // 3
        held = h.holds(kind)
        gy, _ = h.block(kind, h.p)
        xh = lax.rem(gy, 2)
        for g in range(4):
            other = held & jnp.logical_not((g == h.gx) & (xh == h.xh))

            @pl.when(other)
            def _(slot=slot, g=g):
                push(
                    frames.at[0, pl.ds(0, HALF)], rwa.at[slot, g, pl.ds(0, HALF)], ss.at[0],
                    rsw.at[slot, g], ys[0],
                ).wait_recv()

            @pl.when(other & last)
            def _(slot=slot, g=g):
                push(
                    frames.at[0, pl.ds(0, EXTRA)], rwa.at[slot, g, pl.ds(HALF, EXTRA)], ss.at[0],
                    rsx.at[slot, g], ys[0],
                ).wait_recv()

        @pl.when(held)
        def _():
            wt[w_half(kind)] = join([rwa[slot, g, 0:HALF] for g in range(4)])

        @pl.when(held & last)
        def _():
            wt[w_extra(kind)] = join([rwa[slot, g, HALF : HALF + EXTRA] for g in range(4)])

        @pl.when(jnp.logical_not(last))
        def _():
            wt[wrow(kind, 192, 64)] = jnp.zeros((64, D), BF)

    by_y, by_z = {}, {}

    chunks = lambda q: (
        (HALF * q, 0, 64, None), (HALF * q + 64, 64, 32, None), (192 + EXTRA * q, HALF, EXTRA, last),
    )

    def pass_y(kind):
        held = h.holds(kind)
        for k, (start, _, size, cond) in enumerate(chunks(par)):
            by_y[kind, k] = []
            for d in (2, 1, 3):
                comes = h.block(kind, h.p)[0] // 2 == lax.rem(h.y + 4 - d, 4)
                s_if = held if cond is None else held & cond
                r_if = comes if cond is None else comes & cond
                ref = wt.at[wrow(kind, start, size)]
                by_y[kind, k].append(net.send(ref, ref, ys[d - 1], send_if=s_if, recv_if=r_if))

    def pass_z(kind, k):
        start, _, size, cond = chunks(par)[k]
        for c in by_y[kind, k]:
            c.got()
        for off, d in ((0, zm), (size // 2, zp)):
            ref = wt.at[wrow(kind, start + off, size // 2)]
            by_z.setdefault(kind, []).append(net.send(ref, ref, d, send_if=cond, recv_if=cond))

    for kind in range(3):
        take_frames(kind)
        pass_y(kind)
    gather.ready(0)
    gather.ready(1)
    for kind in range(3):
        pass_z(kind, 0)
    grds = by_gx(lambda g: grd.at[:, lanes_of(g)], lambda g: rg.at[g])
    grd_own = pltpu.make_async_copy(grd.at[:, lanes_of(h.gx)], rg.at[h.gx], loc.at[3])
    grd_own.start()
    for k in (1, 2):
        for kind in range(3):
            pass_z(kind, k)
    gather.ready(2)
    gather.ready(3)
    take_frames(3)
    pass_y(3)

    for c in ffs:
        c.got()
        c.gone()
    fslab = lambda y, k: cut((2 * y + k) * FPAD, FPAD)
    mine_ff = fslab(h.y, par)
    fw[mine_ff] = join([rff[g] for g in range(4)])
    ff_y = [net.send(fw.at[mine_ff], fw.at[mine_ff], d) for d in ys]
    ff_z = []

    def ff_pass(d):
        if d:
            ff_y[d - 1].got()
        base = (2 * lax.rem(h.y + 4 - d, 4) + par) * FPAD
        for off, size, to in ((0, A_ROWS, zm), (A_ROWS, B_ROWS, zp)):
            ref = fw.at[cut(base + off, size)]
            ff_z.append(net.send(ref, ref, to))

    @pl.when(jnp.logical_not(alone))
    def _():
        push(segs, seg, ss.at[0], rseg.at[0], ys[0]).wait_recv()

    begin = jnp.sum((seg[...] == 0).astype(F32), axis=1, keepdims=True).astype(jnp.int32)
    set_masks(masks, begin)
    for c in grds:
        c.got()
    grd_own.wait()
    ga[my_rows] = turn(rg)
    ggather = Gather(h, net, ga)
    ggather.start()
    for kind in range(3):
        for c in by_z[kind]:
            c.got()

    ff_pass(0)

    @pl.loop(0, 4)
    def _(chip):
        span = cut(256 * chip, 256)
        for kind in range(3):
            qkv[kind, span] = (nt(fs[span], wt[wspan(kind)]) + qkvb[kind]).astype(BF)

    save = pltpu.make_async_copy(fs, saved, loc.at[1])
    save.start()
    for c in fsends:
        c.gone()
    ggather.ready(0)
    ggather.ready(1)

    def attend(pair):
        lanes = pl.ds(128 * pair, 128)
        for i in range(4):
            n = 256 * (i + 1)
            mask = masks[MASK_AT[i] : MASK_AT[i] + n]
            outs = []
            for q, k, v in zip(
                halves(qkv[0, 256 * i : n, lanes]), halves(qkv[1, 0:n, lanes]), halves(qkv[2, 0:n, lanes])
            ):
                outs.append(tn(probs_t(k, q * 0.125, mask).astype(BF), v))
            att[256 * i : n, lanes] = join(outs).astype(BF)

    attend(0)
    ggather.ready(2)
    ggather.ready(3)
    for k in range(3):
        pass_z(3, k)
    attend(1)
    save.wait()
    for c in by_z[3]:
        c.got()

    sa = Scatter(h, net, (a0, a1, a2, a3))
    sa.run(lambda chip: nn(att[cut(256 * chip, 256)], wt[wspan(3)]))
    ff_pass(1)
    ff_pass(3)
    r = rows[...].astype(F32) + sa.result() + vecs[2:3]
    res[...] = r
    normed, _ = stats(r)

    fs[my_rows] = (normed * vecs[3:4] + vecs[4:5]).astype(BF)
    gather = Gather(h, net, fs)
    gather.start()
    ff_pass(2)
    for c in ff_z + fgot:
        c.got()
    v0[...] = jnp.zeros_like(v0)
    for s in range(4):
        chip = gather.ready(s)

        @pl.loop(0, 4)
        def _(y, chip=chip):
            span = cut(256 * chip, 256)
            v = nt(fs[span], fw[fslab(y, 0)]) + fcbs[y, 0:1]
            up = nt(ga[span], fw[fslab(y, 1)])
            t = jnp.tanh(0.7978845608028654 * (v + 0.044715 * v * v * v))
            hid[y, span] = (0.5 * v * (1.0 + t)).astype(BF)
            slope = 0.5 * (1.0 + t) + 0.5 * v * (1.0 - t * t) * (
                0.7978845608028654 * (1.0 + 3 * 0.044715 * v * v)
            )
            gpre[y, span] = (up * slope).astype(BF)

    def total(src, k):
        def f(chip):
            return sum(nn(src[y, cut(256 * chip, 256)], fw[fslab(y, k)]) for y in range(4))

        return f

    sb = Scatter(h, net, (b0, b1, b2, b3))
    sb.begin(total(gpre, 0))
    for c in ff_y + ff_z:
        c.gone()
    sa = Scatter(h, net, (a0, a1, a2, a3))
    for j in range(4):
        sa.term(j, total(hid, 1))
    sb.relayed()

    one = {}
    for d in (2, 1, 3, 0):
        y = lax.rem(h.y + d, 4)
        fw[fslab(y, 0)] = tn(gpre[y], fs[...]).astype(BF)
        fw[fslab(y, 1)] = tn(hid[y], ga[...]).astype(BF)
        base = (2 * y + 1 - par) * FPAD
        land = yr.at[d - 1] if d else wx
        one[d] = [
            net.send(fw.at[cut(base + off, size)], land.at[pl.ds(off, size)], to)
            for off, size, to in ((0, A_ROWS, zm), (A_ROWS, B_ROWS, zp))
        ]

    load = pltpu.make_async_copy(saved, fs, loc.at[1])
    load.start()
    gs = sb.result()
    normed, inv = stats(res[...])
    up = ga[my_rows].astype(F32)
    gres = up + norm_back(gs, vecs[3:4], normed, inv)
    gsave[...] = gres
    low = gres.astype(BF)
    ba[my_rows] = low
    gather = Gather(h, net, ba)
    gather.start()
    v0[2:3, 0:D] = rows_of(gs * normed)
    v0[3:4, 0:D] = rows_of(gs)
    v0[4:5, 0:D] = rows_of(low.astype(F32))
    v0[5:6, 0:D] = rows_of(up)
    for d in ys:
        pl.semaphore_signal(hz, inc=1, device_id=d, device_id_type=MESH)
    gather.ready(0)
    gather.ready(1)
    for y in range(4):
        v0[2 + y : 3 + y, 1664 : 1664 + FPAD] = rows_of(gpre[y].astype(F32))

    for s in range(4):
        if s > 1:
            gather.ready(s)
        span = cut(256 * gather.chip(s), 256)
        gat[span] = nt(ba[span], wt[wspan(3)]).astype(BF)
    sa.first()
    sa.side(1)
    sa.side(2)
    for kind in range(4):
        for c in by_y[kind, 0] + by_y[kind, 1] + by_y[kind, 2] + by_z[kind]:
            c.gone()
    wt[wspan(3)] = tn(att[...], ba[...]).astype(BF)
    for d in (zm, zp):
        pl.semaphore_signal(hb, inc=1, device_id=d, device_id_type=MESH)

    two = {}

    def collect(d):
        for c in one[d]:
            c.got()
        y = lax.rem(h.y + d, 4)
        span = fslab(y, par)
        other = yr[d - 1, 0:FPAD] if d else wx[0:FPAD]
        fw[span] = (fw[span].astype(F32) + other.astype(F32)).astype(BF)
        if d:
            two[d] = net.send(fw.at[span], ga.at[pl.ds(FPAD * (d - 1), FPAD)], ys[d - 1])

    def attend_back(pair):
        lanes = pl.ds(128 * pair, 128)
        dk[...] = jnp.zeros_like(dk)
        dv[...] = jnp.zeros_like(dv)
        for i in range(4):
            n = 256 * (i + 1)
            mask = masks[MASK_AT[i] : MASK_AT[i] + n]
            dqs, dks, dvs = [], [], []
            for q, k, v, g in zip(
                halves(qkv[0, 256 * i : n, lanes]), halves(qkv[1, 0:n, lanes]),
                halves(qkv[2, 0:n, lanes]), halves(gat[256 * i : n, lanes]),
            ):
                q = q * 0.125
                probs = probs_t(k, q, mask)
                dvs.append(nn(probs.astype(BF), g))
                prod = probs * nt(v, g)
                ds = (prod - probs * jnp.sum(prod, axis=0, keepdims=True)).astype(BF)
                dks.append(nn(ds, q))
                dqs.append(tn(ds, k) * 0.125)
            dv[:n] += join(dvs)
            dk[:n] += join(dks)
            qkv[0, 256 * i : n, lanes] = join(dqs).astype(BF)
        qkv[1, :, lanes] = dk[...].astype(BF)
        qkv[2, :, lanes] = dv[...].astype(BF)

    pl.semaphore_wait(hz, 3)
    collect(2)
    collect(1)
    sa.relayed()
    attend_back(0)
    collect(3)
    collect(0)
    pl.semaphore_signal(ho, inc=1, device_id=zo, device_id_type=MESH)
    for d in ys:
        pl.semaphore_signal(hy, inc=1, device_id=d, device_id_type=MESH)

    def turn_back(v, dst):
        t = jnp.transpose(v.astype(BF))
        for g in range(4):
            dst[g] = t[QUARTER * g : QUARTER * (g + 1)]

    turn_back(res[...] + sa.result() + vecs[5:6], rt)
    by_gx(lambda g: rt.at[g], lambda g: layer_out.at[:, lanes_of(g)])
    lo_own = pltpu.make_async_copy(rt.at[h.gx], layer_out.at[:, lanes_of(h.gx)], loc.at[2])
    lo_own.start()

    def dw(kind):
        return wt if kind == 3 else a0

    wone = {}

    def send_one(kind, k):
        start, at, size, cond = chunks(1 - par)[k]
        half = size // 2
        wone[kind, k] = [
            net.send(
                dw(kind).at[wrow(kind, start + half * i, half)],
                ba.at[pl.ds(128 * kind + at + half * i, half)], to, send_if=cond, recv_if=cond,
            )
            for i, to in ((0, zm), (1, zp))
        ]

    pl.semaphore_wait(hb, 2)
    for k in range(3):
        send_one(3, k)
    attend_back(1)
    load.wait()

    @pl.loop(0, 3)
    def _(kind):
        a0[cut(FRAME * kind, FRAME)] = tn(qkv[kind], fs[...]).astype(BF)

    for k in range(3):
        for kind in range(3):
            send_one(kind, k)
    sb = Scatter(h, net, (b0, b1, b2, b3))
    sb.begin(lambda chip: sum(nn(qkv[k, cut(256 * chip, 256)], wt[wspan(k)]) for k in range(3)))

    wtwo = {}

    def send_two(kind, k):
        slot, held = kind // 3, h.holds(kind)
        home = h.block(kind, h.p)[0] // 2
        start, at, size, cond = chunks(par)[k]
        mine = wrow(kind, start, size)
        for c in wone[kind, k]:
            c.got()

        def add():
            ref = dw(kind)
            s = ref[mine].astype(F32) + ba[128 * kind + at : 128 * kind + at + size].astype(F32)
            ref[mine] = s.astype(BF)

        if cond is None:
            add()
        else:
            pl.when(cond)(add)
        for d in (2, 1, 3):
            goes, comes = lax.rem(h.y + d, 4) == home, held
            if cond is not None:
                goes, comes = goes & cond, comes & cond
            wtwo.setdefault(kind, []).append(
                net.send(
                    dw(kind).at[mine], yr.at[d - 1, pl.ds(128 * slot + at, size)], ys[d - 1],
                    send_if=goes, recv_if=comes,
                )
            )

    pl.semaphore_wait(hy, 3)
    for k in range(3):
        send_two(3, k)
    for kind in range(3):
        send_two(kind, 0)
    sb.relayed()
    for k in (1, 2):
        for kind in range(3):
            send_two(kind, k)
    v0[0:1, 1664:VW] = rows_of(qkv[0].astype(F32))
    v0[1:2, 1664:VW] = rows_of(qkv[2].astype(F32))

    s = fw[fslab(h.y, par)].astype(F32)
    for d in (1, 2, 3):
        two[d].got()
        s = s + ga[FPAD * (d - 1) : FPAD * d].astype(F32)
    s2[0:FPAD] = s.astype(BF)
    pl.semaphore_wait(ho, 1)
    three = net.send(s2.at[pl.ds(0, FPAD)], wx.at[pl.ds(0, FPAD)], zo)

    gf = sb.result()
    normed, inv = stats(rows[...].astype(F32))
    low = gsave[...] + norm_back(gf, vecs[0:1], normed, inv)
    v0[0:1, 0:D] = rows_of(gf * normed)
    v0[1:2, 0:D] = rows_of(gf)
    for c in grds:
        c.gone()
    turn_back(low, rg)
    by_gx(lambda g: rg.at[g], lambda g: input_grad.at[:, lanes_of(g)])
    ig_own = pltpu.make_async_copy(rg.at[h.gx], input_grad.at[:, lanes_of(h.gx)], loc.at[0])
    ig_own.start()
    vys = [net.send(v0, vy.at[h.y], d) for d in ys]
    vy[h.y] = v0[...]

    three.got()
    full = (s2[0:FPAD].astype(F32) + wx[0:FPAD].astype(F32)).astype(BF)
    pl.semaphore_signal(ho, inc=1, device_id=zo, device_id_type=MESH)
    for g in range(4):
        rff[g] = full[:, QUARTER * g : QUARTER * (g + 1)]
    four = by_gx(lambda g: rff.at[g], lambda g: ffo.at[par, g])
    ffo_own = pltpu.make_async_copy(rff.at[h.gx], ffo.at[par, h.gx], loc.at[3])
    ffo_own.start()
    three.gone()

    spans = ((HALF * par, half_own, 0, HALF, None), (192 + EXTRA * par, extra_own, HALF, EXTRA, last))
    for c in vys:
        c.got()
    vz[h.z] = (vy[0] + vy[1]) + (vy[2] + vy[3])
    vzs = [net.send(vz.at[h.z], vz.at[h.z], h.rel(dz=d)) for d in (1, 2, 3)]

    ffo_own.wait()
    for c in four:
        c.got()
    five = []
    for at, size, to in ((0, A_ROWS, zm), (A_ROWS, B_ROWS, zp)):
        ref = ffo.at[par, :, pl.ds(at, size)]
        five.append(net.send(ref, ref, to))

    pl.semaphore_wait(ho, 1)
    wthree = {}
    for kind in range(4):
        slot, held = kind // 3, h.holds(kind)
        for c in wtwo[kind]:
            c.got()
        for start, _, at, size, cond in spans:
            ok = held if cond is None else held & cond
            low_at = 128 * slot + at

            @pl.when(ok)
            def _(kind=kind, start=start, size=size, low_at=low_at):
                s = dw(kind)[wrow(kind, start, size)].astype(F32)
                for d in range(3):
                    s = s + yr[d, low_at : low_at + size].astype(F32)
                s2[low_at : low_at + size] = s.astype(BF)

            wthree.setdefault(kind, []).append(
                net.send(
                    s2.at[pl.ds(low_at, size)], wx.at[pl.ds(low_at, size)], zo, send_if=ok, recv_if=ok
                )
            )

    for c in vzs:
        c.got()
    vx[h.p] = (vz[0] + vz[1]) + (vz[2] + vz[3])
    vxs = [net.send(vx.at[h.p], vx.at[h.p], d) for d in h.ring()]

    for kind in range(4):
        slot, held = kind // 3, h.holds(kind)
        gy, place = h.block(kind, h.p)
        gyt, placet = h.block(kind, h.p - 1)
        xh, xht, yt = lax.rem(gy, 2), lax.rem(gyt, 2), gyt // 2
        for c in wthree[kind]:
            c.got()
        for _, mine, at, size, cond in spans:
            ok = held if cond is None else held & cond
            low_at = 128 * slot + at

            @pl.when(ok)
            def _(slot=slot, at=at, size=size, low_at=low_at):
                span = slice(low_at, low_at + size)
                full = (s2[span].astype(F32) + wx[span].astype(F32)).astype(BF)
                for g in range(4):
                    rwa[slot, g, at : at + size] = full[:, QUARTER * g : QUARTER * (g + 1)]

            for g in range(4):
                same = (g == h.gx) & (xh == h.xh)
                net.send(
                    rwa.at[slot, g, pl.ds(at, size)], frames.at[place, mine], (h.z, g, gy),
                    send_if=ok & jnp.logical_not(same), rs=(rsm if cond is None else rsn).at[place],
                )

                @pl.when(ok & same)
                def _(slot=slot, g=g, place=place, mine=mine, at=at, size=size):
                    frames[place, mine] = rwa[slot, g, at : at + size]

        for g in range(4):
            same = (g == h.gx) & (xht == h.xh) & (yt == h.y)
            ok = held & (h.p > 0) & (par == 0)
            net.send(
                rwa.at[slot, g, pl.ds(0, TAIL)], tl.at[placet], (h.z, g, gyt),
                send_if=ok & jnp.logical_not(same), rs=rst.at[placet],
            )

            @pl.when(ok & same)
            def _(slot=slot, g=g, placet=placet):
                tl[placet] = rwa[slot, g, 0:TAIL]

    wfive = {}
    for i in range(4):
        p, kind = h.unit(i)
        four_heads = p == 7
        far = p != h.p

        @pl.when(far)
        def _(i=i):
            push(
                frames.at[0, pl.ds(0, HALF)], frames.at[i, pl.ds(0, HALF)], ss.at[0], rsm.at[i], ys[0]
            ).wait_recv()

        @pl.when(far & four_heads)
        def _(i=i):
            push(
                frames.at[0, pl.ds(0, EXTRA)], frames.at[i, pl.ds(0, EXTRA)], ss.at[0], rsn.at[i], ys[0]
            ).wait_recv()

        follow = (p + 1) // 2 if i == 3 else (kind * 8 + p + 1) // 6
        has_tail = jnp.logical_not(four_heads)

        @pl.when(has_tail & (par == 0) & jnp.logical_not((p + 1 == h.p) & (follow == h.y)))
        def _(i=i):
            push(tl.at[0], tl.at[i], ss.at[0], rst.at[i], ys[0]).wait_recv()

        for base, size, cond in (
            (HALF * par, 48, None), (192 + EXTRA * par, 16, four_heads),
        ):
            for k, to in ((0, zm), (1, zp)):
                ref = frames.at[i, cut(base + size * k, size)]
                wfive.setdefault(i, []).append(net.send(ref, ref, to, send_if=cond, recv_if=cond))
        for k, to in ((0, zm), (1, zp)):
            ref = tl.at[i, pl.ds(32 * k, 32)]
            wfive[i].append(
                net.send(
                    ref, ref, to, send_if=has_tail & (par == 0), recv_if=has_tail & (par == 1)
                )
            )

    for c in four + five:
        c.got()
        c.gone()
    for k, dst in ((0, gfc), (1, got_)):
        fetch = pltpu.make_async_copy(ffo.at[k], rff, loc.at[3])
        fetch.start()
        fetch.wait()
        for g in range(4):
            t32[SUB * g : SUB * (g + 1)] = rff[g].astype(F32)[0:SUB]
        if k:
            out_copy.wait()
        stage[...] = jnp.transpose(t32[...]).astype(BF)
        out_copy = pltpu.make_async_copy(stage, dst, loc.at[1])
        out_copy.start()

    out_copy.wait()
    for c in vxs:
        c.got()
    total_v = vx[0]
    for p in range(1, 8):
        total_v = total_v + vx[p]
    vsum[...] = pick([total_v[:, QUARTER * g : QUARTER * (g + 1)] for g in range(4)], h.gx)
    for k in (0, 1):
        parts = [vx[p, k : k + 1, 1664 : 1664 + (FRAME if p == 7 else 192)] for p in range(8)]
        qsum[k : k + 1] = join(parts)
    fsum[...] = join([vx[4 * h.xh + g, pl.ds(2 + h.y, 1), 1664 : 1664 + SUB] for g in range(4)])
    for i in range(4):
        p, _ = h.unit(i)
        for c in wfive[i]:
            c.got()
        scr[0:FRAME, 0:QUARTER] = frames[i].astype(F32)

        @pl.when(p < 7)
        def _(i=i):
            scr[192 : 192 + TAIL, 0:QUARTER] = tl[i].astype(F32)

        t32[SUB * i : SUB * (i + 1)] = scr[pl.ds(pl.multiple_of(8 * p, 8), SUB), 0:QUARTER]
    stage[...] = jnp.transpose(t32[...]).astype(BF)
    out_copy = pltpu.make_async_copy(stage, gwa, loc.at[1])
    out_copy.start()
    out_copy.wait()
    lo_own.wait()
    ig_own.wait()
    net.finish()


def layer(segs, tok, grd, wq, wp, fcw, otw, vec, bias):
    any_ = pl.BlockSpec(memory_space=pl.ANY)
    scratch = [
        pltpu.VMEM((SEQ, D), BF),
        pltpu.VMEM((SEQ, D), BF),
        pltpu.VMEM((SEQ, D), BF),
        pltpu.VMEM((SEQ, D), BF),
        pltpu.VMEM((8 * FPAD, D), BF),
        pltpu.VMEM((3, SEQ, FRAME), BF),
        pltpu.VMEM((SEQ, FRAME), BF),
        pltpu.VMEM((SEQ, FRAME), BF),
        pltpu.VMEM((2560, 256), BF),
        pltpu.VMEM((4, SEQ, FPAD), BF),
        pltpu.VMEM((4, SEQ, FPAD), BF),
        pltpu.VMEM((SEQ, 2 * HEAD_DIM), F32),
        pltpu.VMEM((SEQ, 2 * HEAD_DIM), F32),
        *Scatter.scratch(),
        *Scatter.scratch(),
        pltpu.VMEM((4, QUARTER, ROWS), BF),
        pltpu.VMEM((4, QUARTER, ROWS), BF),
        pltpu.VMEM((2, 4, HALF + EXTRA, QUARTER), BF),
        pltpu.VMEM((4, FPAD, QUARTER), BF),
        pltpu.VMEM((4, FRAME, QUARTER), BF),
        pltpu.VMEM((2, TAIL, QUARTER), BF),
        pltpu.VMEM((2, TAIL, QUARTER), BF),
        pltpu.VMEM((336, QUARTER), F32),
        pltpu.VMEM((4 * SUB, QUARTER), F32),
        pltpu.VMEM((QUARTER, 4 * SUB), BF),
        pltpu.VMEM((4, FPAD, QUARTER), BF),
        pltpu.VMEM((4, 8, QUARTER), F32),
        pltpu.VMEM((8, D), F32),
        pltpu.VMEM((1, 128), jnp.int32),
        pltpu.VMEM((8, FPAD), F32),
        pltpu.VMEM((4, 8, FPAD), F32),
        pltpu.VMEM((ROWS, D), F32),
        pltpu.VMEM((ROWS, D), F32),
        pltpu.VMEM((ROWS, D), BF),
        pltpu.VMEM((3, FRAME, D), BF),
        pltpu.VMEM((FRAME, D), BF),
        pltpu.VMEM((FRAME, D), BF),
        pltpu.VMEM((4, TAIL, QUARTER), BF),
        pltpu.VMEM((8, VW), F32),
        pltpu.VMEM((4, 8, VW), F32),
        pltpu.VMEM((4, 8, VW), F32),
        pltpu.VMEM((8, 8, VW), F32),
        pltpu.SemaphoreType.DMA((Net.SIZE,)),
        pltpu.SemaphoreType.DMA((Net.SIZE,)),
        pltpu.SemaphoreType.DMA((2, 4)),
        pltpu.SemaphoreType.DMA((2, 4)),
        pltpu.SemaphoreType.DMA((1,)),
        pltpu.SemaphoreType.DMA((4,)),
        pltpu.SemaphoreType.DMA((4,)),
        pltpu.SemaphoreType.DMA((4,)),
        pltpu.SemaphoreType.DMA((4,)),
        pltpu.SemaphoreType.REGULAR,
        pltpu.SemaphoreType.REGULAR,
        pltpu.SemaphoreType.REGULAR,
        pltpu.SemaphoreType.REGULAR,
    ]
    return pl.pallas_call(
        layer_kernel,
        out_shape=[
            jax.ShapeDtypeStruct((QUARTER, 4 * ROWS), BF),
            jax.ShapeDtypeStruct((QUARTER, 4 * ROWS), BF),
            jax.ShapeDtypeStruct((QUARTER, 4 * SUB), BF),
            jax.ShapeDtypeStruct((QUARTER, 4 * SUB), BF),
            jax.ShapeDtypeStruct((QUARTER, 4 * SUB), BF),
            jax.ShapeDtypeStruct((8, QUARTER), F32),
            jax.ShapeDtypeStruct((2, D), F32),
            jax.ShapeDtypeStruct((1, 4 * SUB), F32),
            jax.ShapeDtypeStruct((2, 4, FPAD, QUARTER), BF),
            jax.ShapeDtypeStruct((SEQ, D), BF),
        ],
        in_specs=[VMEM, any_, any_, VMEM, VMEM, any_, any_, VMEM, VMEM],
        out_specs=[any_, any_, any_, any_, any_, VMEM, VMEM, VMEM, any_, any_],
        scratch_shapes=scratch,
        compiler_params=pltpu.CompilerParams(
            collective_id=0, has_side_effects=True, vmem_limit_bytes=64 * 2**20 - 2**16
        ),
        name="layer",
    )(segs, tok, grd, wq, wp, fcw, otw, vec, bias)


def per_device(
    tokens_in, segments, norm1_gain, norm1_bias, qkv_weight, query_bias, value_bias, proj_weight,
    proj_bias, norm2_gain, norm2_bias, fc_weight, fc_bias, out_weight, out_bias, out_grad,
):
    zero = jnp.zeros_like(norm1_gain)
    vec = jnp.stack(
        [norm1_gain, norm1_bias, proj_bias, norm2_gain, norm2_bias, out_bias, zero, zero]
    )
    bias = jnp.stack([query_bias, value_bias, jnp.pad(fc_bias, (0, D - 4 * SUB))])
    layer_out, input_grad, gwa, gfc, got, vsum, qsum, fsum, _, _ = layer(
        segments, tokens_in.T, out_grad.T, qkv_weight, proj_weight, fc_weight, out_weight, vec, bias
    )
    return (
        layer_out.T,
        input_grad.T.astype(F32),
        vsum[0],
        vsum[1],
        gwa[:, : 3 * SUB].astype(F32),
        qsum[0],
        qsum[1],
        gwa[:, 3 * SUB :].astype(F32),
        vsum[4],
        vsum[2],
        vsum[3],
        gfc.astype(F32),
        fsum[0],
        got.astype(F32),
        vsum[5],
    )


def solution(mesh):
    return jax.shard_map(
        per_device,
        mesh=mesh,
        in_specs=(
            P(("dp", "gy"), "gx"), P(("dp", "gx"), "gy"), P("gx"), P("gx"), P("gx", "gy"), P(), P(),
            P("gx", "gy"), P("gx"), P("gx"), P("gx"), P("gx", "gy"), P("gy"), P("gx", "gy"), P("gx"),
            P(("dp", "gy"), "gx"),
        ),
        out_specs=(
            P(("dp", "gy"), "gx"), P(("dp", "gy"), "gx"), P("gx"), P("gx"), P("gx", "gy"), P(), P(),
            P("gx", "gy"), P("gx"), P("gx"), P("gx"), P("gx", "gy"), P("gy"), P("gx", "gy"), P("gx"),
        ),
        check_vma=False,
    )
```

```python
import math

import jax
import jax.numpy as jnp
from jax import lax
from jax.experimental import pallas as pl
from jax.experimental.pallas import tpu as pltpu
from jax.sharding import PartitionSpec as P

BF = jnp.bfloat16
F32 = jnp.float32
HEADS = 25
HEAD_DIM = 64
D = HEADS * HEAD_DIM
FF = 6400
SEQ = 1024
DOC = 800
ROWS = 128
QUARTER = 400
SUB = 200
FPAD = 208
FRAME = 256
TAIL = 64
NEG = -1e30
MESH = pl.DeviceIdType.MESH
VMEM = pl.BlockSpec(memory_space=pltpu.VMEM)
SMEM = pl.BlockSpec(memory_space=pltpu.SMEM)


def nt(a, b):
    return lax.dot_general(a, b, (((1,), (1,)), ((), ())), preferred_element_type=F32)


def nn(a, b):
    return lax.dot_general(a, b, (((1,), (0,)), ((), ())), preferred_element_type=F32)


def tn(a, b):
    return lax.dot_general(a, b, (((0,), (0,)), ((), ())), preferred_element_type=F32)


class Here:
    def __init__(self):
        self.z, self.gx, self.gy = (lax.axis_index(a) for a in ("dp", "gx", "gy"))
        self.y, self.xh = self.gy // 2, lax.rem(self.gy, 2)
        self.x = self.xh * 2 + self.gx // 2
        self.c = lax.rem(self.gx, 2)
        self.p = self.x * 2 + self.c

    def at(self, x, c, y, z):
        return (z, lax.rem(x, 2) * 2 + c, y * 2 + x // 2)

    def rel(self, dx=0, flip=0, dy=0, dz=0):
        c = 1 - self.c if flip else self.c
        return self.at(
            lax.rem(self.x + 4 + dx, 4), c, lax.rem(self.y + 4 + dy, 4), lax.rem(self.z + 4 + dz, 4)
        )

    def ring(self):
        return [self.rel(dx, f) for dx in range(4) for f in (0, 1) if dx or f]

    def gxd(self, d):
        return (self.z, self.gx ^ d, self.gy)

    def unit(self, i):
        if i == 3:
            return self.gy, 3
        t = 3 * self.gy + i
        return lax.rem(t, 8), t // 8

    def block(self, kind, p):
        if kind == 3:
            return p, 3
        t = kind * 8 + p
        return t // 3, lax.rem(t, 3)

    def holds(self, kind):
        return self.block(kind, self.p)[0] // 2 == self.y


def meet(peers):
    sem = pltpu.get_barrier_semaphore()
    for d in peers:
        pl.semaphore_signal(sem, inc=1, device_id=d, device_id_type=MESH)
    pl.semaphore_wait(sem, len(peers))


def push(src, dst, ss, rs, d):
    return pltpu.make_async_remote_copy(
        src_ref=src, dst_ref=dst, send_sem=ss, recv_sem=rs, device_id=d, device_id_type=MESH
    )


def stats(v):
    mean = jnp.sum(v, axis=1, keepdims=True) / D
    spread = jnp.sum(v * v, axis=1, keepdims=True) / D - mean * mean
    inv = lax.rsqrt(spread + 1e-5)
    return (v - mean) * inv, inv


def norm_back(u, gain, normed, inv):
    w = u * gain
    a = jnp.sum(w, axis=1, keepdims=True) / D
    b = jnp.sum(w * normed, axis=1, keepdims=True) / D
    return inv * (w - a - normed * b)


def cut(start, size):
    return pl.ds(start if isinstance(start, int) else pl.multiple_of(start, 16), size)


def rows_of(v):
    return jnp.sum(v, axis=0, keepdims=True)


class Copy:
    def __init__(self, desc, send_if=None, recv_if=None):
        self.desc, self.send_if, self.recv_if = desc, send_if, recv_if
        self.is_got = self.is_gone = False

    def on(self, cond, do):
        if cond is None:
            do()
        else:
            pl.when(cond)(do)

    def start(self):
        self.on(self.send_if, self.desc.start)

    def got(self):
        if not self.is_got:
            self.is_got = True
            self.on(self.recv_if, self.desc.wait_recv)

    def gone(self):
        if not self.is_gone:
            self.is_gone = True
            self.on(self.send_if, self.desc.wait_send)


class Net:
    SIZE = 424

    def __init__(self, ss, rs):
        self.ss, self.rs, self.n, self.copies = ss, rs, 0, []

    def make(self, src, dst, d, send_if=None, recv_if=None, rs=None):
        i = self.n
        self.n += 1
        assert i < self.SIZE
        c = Copy(push(src, dst, self.ss.at[i], self.rs.at[i] if rs is None else rs, d), send_if, recv_if)
        if rs is not None:
            c.is_got = True
        self.copies.append(c)
        return c

    def send(self, *args, **kw):
        c = self.make(*args, **kw)
        c.start()
        return c

    def finish(self):
        for c in self.copies:
            c.got()
            c.gone()


class Gather:
    def __init__(self, here, net, buf):
        self.h, self.net, self.buf = here, net, buf

    def row(self, dx):
        return (lax.rem(self.h.x + 4 + dx, 4) * 2 + self.h.c) * ROWS

    def ref(self, dx, half):
        return self.buf.at[cut(self.row(dx), ROWS) if half is None else cut(self.row(dx) + 64 * half, 64)]

    def go(self, dx, d, half=None):
        ref = self.ref(dx, half)
        return self.net.send(ref, ref, d)

    def start(self):
        h = self.h
        self.right, self.left, self.sib = h.rel(1), h.rel(-1), h.rel(0, 1)
        self.r = [self.go(0, self.right, 0), None]
        self.l = [None, self.go(0, self.left, 1)]
        self.r[1] = self.go(0, self.right, 1)
        self.l[0] = self.go(0, self.left, 0)
        self.own = self.go(0, self.sib)
        self.rr = None

    def relays(self):
        if self.rr is None:
            self.r[0].got()
            self.rr = self.go(-1, self.right, 0)
            self.l[1].got()
            self.ll = self.go(1, self.left, 1)

    def chip(self, s):
        return lax.rem(self.h.x + (0, 3, 1, 2)[s], 4)

    def ready(self, s):
        h = self.h
        if s == 0:
            self.own.got()
            return h.x
        if s == 1:
            self.relays()
            self.r[1].got()
            self.f1 = self.go(-1, self.sib)
            self.l[0].got()
            self.f2 = self.go(1, self.sib)
            self.f1.got()
            return lax.rem(h.x + 3, 4)
        if s == 2:
            self.f2.got()
            return lax.rem(h.x + 1, 4)
        self.rr.got()
        f3 = self.go(2, self.sib, 0)
        self.ll.got()
        f4 = self.go(2, self.sib, 1)
        f3.got()
        f4.got()
        for c in (*self.r, *self.l, self.own, self.rr, self.ll, self.f1, self.f2, f3, f4):
            c.gone()
        return lax.rem(h.x + 2, 4)


def raw_at(p, half=None):
    rows, lanes = QUARTER * (p // 3), 512 * (p % 3 if isinstance(p, int) else lax.rem(p, 3))
    if isinstance(p, int):
        return slice(rows, rows + QUARTER), slice(lanes, lanes + 512)
    if half is None:
        return cut(rows, QUARTER), pl.ds(pl.multiple_of(lanes, 256), 512)
    return cut(rows, QUARTER), pl.ds(pl.multiple_of(lanes + 256 * half, 256), 256)


class RawGather(Gather):
    def ref(self, dx, half):
        return self.buf.at[raw_at(lax.rem(self.h.x + 4 + dx, 4) * 2 + self.h.c, half)]


class Scatter:
    @staticmethod
    def scratch():
        return [
            pltpu.VMEM((SEQ, D), BF),
            pltpu.VMEM((4, ROWS, D), BF),
            pltpu.VMEM((2, ROWS, D), BF),
            pltpu.VMEM((ROWS, D), BF),
        ]

    STEPS = (2, 1, -1, 0)

    def __init__(self, here, net, refs):
        self.h, self.net = here, net
        self.part, self.mate, self.far, self.relay = refs
        self.pair, self.out, self.ends = {}, [], []

    def at(self, j, c, half=None):
        base = 256 * j + ROWS * c
        return cut(base, ROWS) if half is None else cut(base + 64 * half, 64)

    def term(self, j, f):
        h = self.h
        chip = lax.rem(h.x + 4 + self.STEPS[j], 4)
        self.part[256 * j : 256 * (j + 1)] = f(chip).astype(BF)
        self.pair[j] = self.net.send(
            self.part.at[self.at(j, 1 - h.c)], self.mate.at[j], h.rel(0, 1)
        )

    def total(self, j):
        self.pair[j].got()
        return self.part[self.at(j, self.h.c)].astype(F32) + self.mate[j].astype(F32)

    def link(self, j, half, dst, dx):
        c = self.net.send(self.part.at[self.at(j, self.h.c, half)], dst, self.h.rel(dx))
        self.out.append(c)
        return c

    def first(self):
        self.part[self.at(0, self.h.c)] = self.total(0).astype(BF)
        self.in_r = self.link(0, 0, self.relay.at[pl.ds(0, 64)], 1)
        self.in_l = self.link(0, 1, self.relay.at[pl.ds(64, 64)], -1)

    def side(self, j):
        half = 1 if j == 1 else 0
        self.part[self.at(j, self.h.c)] = self.total(j).astype(BF)
        self.ends.append(self.link(j, half, self.far.at[j - 1, pl.ds(64 * half, 64)], self.STEPS[j]))

    def relayed(self):
        for j, half, c in ((1, 0, self.in_r), (2, 1, self.in_l)):
            c.got()
            span, mine = pl.ds(64 * half, 64), self.at(j, self.h.c, half)
            s = self.part[mine].astype(F32) + self.relay[span].astype(F32)
            self.part[mine] = s.astype(BF)
            self.ends.append(self.link(j, half, self.far.at[j - 1, span], self.STEPS[j]))

    def begin(self, f):
        self.term(0, f)
        self.term(1, f)
        self.first()
        self.term(2, f)
        self.side(1)
        self.term(3, f)
        self.side(2)

    def run(self, f):
        self.begin(f)
        self.relayed()

    def result(self):
        t = self.total(3)
        for c in self.ends:
            c.got()
        t = t + self.far[0].astype(F32) + self.far[1].astype(F32)
        for c in list(self.pair.values()) + self.out:
            c.gone()
        return t


def join(blocks):
    return jnp.concatenate(blocks, axis=1)


def set_masks(masks, begin):
    for i in range(4):
        n = 256 * (i + 1)
        b = lax.broadcasted_iota(jnp.int32, (n, 256), 0)
        a = lax.broadcasted_iota(jnp.int32, (n, 256), 1) + 256 * i

        def doc(t):
            return (t >= begin).astype(jnp.int32) + (t >= begin + DOC).astype(jnp.int32)

        masks[MASK_AT[i] : MASK_AT[i] + n] = jnp.where(
            (b <= a) & (doc(a) == doc(b)), 0.0, NEG
        ).astype(BF)


def probs_t(key, query, mask):
    s = nt(key, query) + mask.astype(F32)
    e = jnp.exp(s - jnp.max(s, axis=0, keepdims=True))
    return e * (1.0 / jnp.sum(e, axis=0, keepdims=True))


def halves(v):
    return v[:, :HEAD_DIM], v[:, HEAD_DIM:]


MASK_AT = (0, 256, 768, 1536)
A_ROWS, B_ROWS = 112, 96
HALF = 96
EXTRA = 32
VW = 1664 + 256


def layer_kernel(
    segs, tok, grd, wq, wp, fcw, otw, g1, c1, pb, g2, c2, ob, qbias, vbias, fbias,
    layer_out, input_grad, gwa, gfc, got_, small, ffo, saved,
    *refs,
):
    (
        fs, ga, ba, wt, fw, qkv, att, gat, masks, hid, gpre, dk, dv,
        a0, a1, a2, a3, b0, b1, b2, b3,
        rt, rg, vec, rwa, rff, frames, tsend, trecv, scr, t32, stage, fbuf, rv, vecs, seg, fcb, fcbs,
        res, gsave, rows, yr, s2, wx, tl, v0, vy, vz, vx,
        ss, rs, rsw, rsx, rseg, rsm, rsn, rst, loc, hz, hb, hy, ho, hx,
    ) = refs
    h = Here()
    net = Net(ss, rs)
    par = lax.rem(h.z, 2)
    last = h.p == 7
    ys = [h.rel(dy=d) for d in (1, 2, 3)]
    zp, zm, zo = h.rel(dz=1), h.rel(dz=-1), h.rel(dz=2)
    plane = [h.rel(dx, f, dy) for dy in range(4) for dx in range(4) for f in (0, 1) if dx or f or dy]
    everyone = plane + [zp, zm, zo]
    barrier = pltpu.get_barrier_semaphore()
    for d in everyone:
        pl.semaphore_signal(barrier, inc=1, device_id=d, device_id_type=MESH)

    @pl.when(par == 0)
    def _():
        pltpu.make_async_copy(fcw, stage, loc.at[0]).start()

    @pl.when(par == 1)
    def _():
        pltpu.make_async_copy(otw, stage, loc.at[0]).start()

    mine_raw = fw.at[raw_at(h.p)]
    tok_own = pltpu.make_async_copy(tok, mine_raw, loc.at[2])
    tok_own.start()
    vec[...] = jnp.concatenate(
        [v[...].reshape(1, QUARTER) for v in (g1, c1, pb, g2, c2, ob)] + [jnp.zeros((2, QUARTER), F32)], axis=0
    )
    t32[0 : 3 * SUB] = jnp.transpose(wq[...]).astype(F32)
    t32[3 * SUB : 4 * SUB] = jnp.transpose(wp[...]).astype(F32)

    def sub_tail(i):
        return t32[SUB * (i + 1) - TAIL : SUB * (i + 1)]

    for k, i in enumerate((2, 3)):
        tsend[k] = sub_tail(i).astype(BF)
    row = lax.broadcasted_iota(jnp.int32, (FRAME, QUARTER), 0)
    half_own = cut(HALF * par, HALF)
    extra_own = cut(192 + EXTRA * par, EXTRA)

    def frame(i, before):
        p, _ = h.unit(i)
        scr[pl.ds(pl.multiple_of(8 * p, 8), TAIL), 0:QUARTER] = before
        scr[pl.ds(pl.multiple_of(8 * p + TAIL, 8), SUB), 0:QUARTER] = t32[SUB * i : SUB * (i + 1)]
        frames[i] = jnp.where((row < 192) | (p == 7), scr[TAIL : TAIL + FRAME, 0:QUARTER], 0.0).astype(BF)

    fsends = []

    def send_frame(i):
        p, _ = h.unit(i)
        slot = i // 3
        dest = h.at(p // 2, lax.rem(p, 2), h.y, h.z)
        mine = p == h.p
        far = jnp.logical_not(mine)
        for src, at, size, cond, sem in (
            (half_own, 0, HALF, far, rsw), (extra_own, HALF, EXTRA, far & (p == 7), rsx),
        ):
            fsends.append(
                net.send(
                    frames.at[i, src], rwa.at[slot, h.gx, pl.ds(at, size)], dest,
                    send_if=cond, rs=sem.at[slot, h.gx],
                )
            )

        @pl.when(mine)
        def _():
            rwa[slot, h.gx, 0:HALF] = frames[i, half_own]
            rwa[slot, h.gx, HALF : HALF + EXTRA] = frames[i, extra_own]

    for i in (1, 2):
        frame(i, sub_tail(i - 1))

    @pl.when(par == 0)
    def _():
        pltpu.make_async_copy(fcw, stage, loc.at[0]).wait()

    @pl.when(par == 1)
    def _():
        pltpu.make_async_copy(otw, stage, loc.at[0]).wait()

    turned = jnp.transpose(stage[...]).astype(F32)
    blank = jnp.zeros((FPAD - SUB, QUARTER), F32)
    for g in range(4):
        fbuf[g] = jnp.concatenate([turned[SUB * g : SUB * (g + 1)], blank], axis=0).astype(BF)
    tok_own.wait()
    pl.semaphore_wait(barrier, len(everyone))

    tail = net.send(tsend, trecv, (h.z, h.gx, lax.rem(h.gy + 1, 8)))

    def lanes_of(g):
        return pl.ds(pl.multiple_of(ROWS * g, ROWS), ROWS)

    def by_gx(src, dst):
        return [net.send(src(h.gx ^ d), dst(h.gx), h.gxd(d)) for d in (1, 2, 3)]

    for i in (1, 2):
        send_frame(i)
    gather = RawGather(h, net, fw)
    gather.start()
    vgot = [net.send(vec, rv.at[h.gx], h.gxd(d)) for d in (1, 2, 3)]
    rv[h.gx] = vec[...]
    at_zero = h.gy == 0
    alone = at_zero & (h.gx == 0)
    for j in range(8):
        me = (h.gx == 0) if j == 0 else False
        cond = at_zero & jnp.logical_not(me)
        net.send(segs, seg, h.at(j // 2, j % 2, h.gx, h.z), send_if=cond, rs=rseg.at[0])

    @pl.when(alone)
    def _():
        seg[...] = segs[...]

    def pick(values, index):
        out = values[0]
        for k, v in enumerate(values[1:]):
            out = jnp.where(index == k + 1, v, out)
        return out

    tail.got()
    for i in (0, 3):
        frame(i, trecv[i // 3].astype(F32))
        send_frame(i)

    my_rows = cut(ROWS * h.p, ROWS)

    def turn(ref):
        return jnp.transpose(jnp.concatenate([ref[g] for g in range(4)], axis=0))

    fbias1 = fbias[...].reshape(1, 4 * SUB)
    low_bias = pick([fbias1[:, SUB * g : SUB * (g + 1)] for g in range(4)], h.gx)
    fcb[...] = jnp.broadcast_to(join([low_bias, jnp.zeros((1, FPAD - SUB), F32)]), (8, FPAD))
    fgot = [net.send(fcb, fcbs.at[h.y], d) for d in ys]
    fcbs[h.y] = fcb[...]
    lane = lax.broadcasted_iota(jnp.int32, (1, FRAME), 1)
    qb, vb = (
        jnp.where(
            (lane < 192) | last, pick([v[:, 192 * p : 192 * p + FRAME] for p in range(8)], h.p), 0.0
        )
        for v in (qbias[...].reshape(1, D), vbias[...].reshape(1, D))
    )
    qkvb = (qb, jnp.zeros_like(qb), vb)

    def wrow(kind, start, size):
        return cut(FRAME * kind + start, size)

    w_half = lambda kind: wrow(kind, HALF * par, HALF)
    w_extra = lambda kind: wrow(kind, 192 + EXTRA * par, EXTRA)

    def wspan(kind):
        return slice(FRAME * kind, FRAME * (kind + 1))

    def take_frames(kind):
        slot = kind // 3
        held = h.holds(kind)
        gy, _ = h.block(kind, h.p)
        xh = lax.rem(gy, 2)
        for g in range(4):
            other = held & jnp.logical_not((g == h.gx) & (xh == h.xh))

            @pl.when(other)
            def _(slot=slot, g=g):
                push(
                    frames.at[0, pl.ds(0, HALF)], rwa.at[slot, g, pl.ds(0, HALF)], ss.at[0],
                    rsw.at[slot, g], ys[0],
                ).wait_recv()

            @pl.when(other & last)
            def _(slot=slot, g=g):
                push(
                    frames.at[0, pl.ds(0, EXTRA)], rwa.at[slot, g, pl.ds(HALF, EXTRA)], ss.at[0],
                    rsx.at[slot, g], ys[0],
                ).wait_recv()

        @pl.when(held)
        def _():
            wt[w_half(kind)] = join([rwa[slot, g, 0:HALF] for g in range(4)])

        @pl.when(held & last)
        def _():
            wt[w_extra(kind)] = join([rwa[slot, g, HALF : HALF + EXTRA] for g in range(4)])

        @pl.when(jnp.logical_not(last))
        def _():
            wt[wrow(kind, 192, 64)] = jnp.zeros((64, D), BF)

    by_y, by_z = {}, {}

    chunks = lambda q: (
        (HALF * q, 0, 64, None), (HALF * q + 64, 64, 32, None), (192 + EXTRA * q, HALF, EXTRA, last),
    )

    def pass_y(kind):
        held = h.holds(kind)
        for k, (start, _, size, cond) in enumerate(chunks(par)):
            by_y[kind, k] = []
            for d in (2, 1, 3):
                comes = h.block(kind, h.p)[0] // 2 == lax.rem(h.y + 4 - d, 4)
                s_if = held if cond is None else held & cond
                r_if = comes if cond is None else comes & cond
                ref = wt.at[wrow(kind, start, size)]
                by_y[kind, k].append(net.send(ref, ref, ys[d - 1], send_if=s_if, recv_if=r_if))

    def pass_z(kind, k):
        start, _, size, cond = chunks(par)[k]
        for c in by_y[kind, k]:
            c.got()
        for off, d in ((0, zm), (size // 2, zp)):
            ref = wt.at[wrow(kind, start + off, size // 2)]
            by_z.setdefault(kind, []).append(net.send(ref, ref, d, send_if=cond, recv_if=cond))

    gather.relays()
    for kind in range(3):
        take_frames(kind)
        pass_y(kind)
    gather.ready(0)
    gather.ready(1)
    ffs = by_gx(lambda g: fbuf.at[g], lambda g: rff.at[g])
    rff[h.gx] = fbuf[h.gx]
    for kind in range(3):
        pass_z(kind, 0)
    gather.ready(2)
    gather.ready(3)
    grds = by_gx(lambda g: grd.at[:, lanes_of(g)], lambda g: rg.at[g])
    grd_own = pltpu.make_async_copy(grd.at[:, lanes_of(h.gx)], rg.at[h.gx], loc.at[3])
    grd_own.start()
    for c in vgot:
        c.got()
    vecs[...] = join([rv[g] for g in range(4)])

    for xh in range(2):

        @pl.loop(0, 4)
        def _(j, xh=xh):
            blocks = []
            for g in range(4):
                r, l = raw_at(4 * xh + g)
                blocks.append(fw[r, pl.ds(pl.multiple_of(l.start + ROWS * j, ROWS), ROWS)])
            x = jnp.transpose(jnp.concatenate(blocks, axis=0))
            normed, _ = stats(x.astype(F32))
            fs[cut(512 * xh + ROWS * j, ROWS)] = (normed * vecs[0:1] + vecs[1:2]).astype(BF)

            @pl.when(h.p == 4 * xh + j)
            def _():
                rows[...] = x

    for d in ys + [zm, zp]:
        pl.semaphore_signal(hx, inc=1, device_id=d, device_id_type=MESH)
    for k in (1, 2):
        for kind in range(3):
            pass_z(kind, k)
    take_frames(3)
    pass_y(3)
    pl.semaphore_wait(hx, 5)

    for c in ffs:
        c.got()
        c.gone()
    fslab = lambda y, k: cut((2 * y + k) * FPAD, FPAD)
    mine_ff = fslab(h.y, par)
    fw[mine_ff] = join([rff[g] for g in range(4)])
    ff_y = [net.send(fw.at[mine_ff], fw.at[mine_ff], d) for d in ys]
    ff_z = []

    def ff_pass(d):
        if d:
            ff_y[d - 1].got()
        base = (2 * lax.rem(h.y + 4 - d, 4) + par) * FPAD
        for off, size, to in ((0, A_ROWS, zm), (A_ROWS, B_ROWS, zp)):
            ref = fw.at[cut(base + off, size)]
            ff_z.append(net.send(ref, ref, to))

    @pl.when(jnp.logical_not(alone))
    def _():
        push(segs, seg, ss.at[0], rseg.at[0], ys[0]).wait_recv()

    begin = jnp.sum((seg[...] == 0).astype(F32), axis=1, keepdims=True).astype(jnp.int32)
    set_masks(masks, begin)
    for c in grds:
        c.got()
    grd_own.wait()
    ga[my_rows] = turn(rg)
    ggather = Gather(h, net, ga)
    ggather.start()
    for kind in range(3):
        for c in by_z[kind]:
            c.got()

    ff_pass(0)

    @pl.loop(0, 4)
    def _(chip):
        span = cut(256 * chip, 256)
        for kind in range(3):
            qkv[kind, span] = (nt(fs[span], wt[wspan(kind)]) + qkvb[kind]).astype(BF)

    save = pltpu.make_async_copy(fs, saved, loc.at[1])
    save.start()
    for c in fsends:
        c.gone()
    ggather.ready(0)
    ggather.ready(1)

    def attend(pair):
        lanes = pl.ds(128 * pair, 128)
        for i in range(4):
            n = 256 * (i + 1)
            mask = masks[MASK_AT[i] : MASK_AT[i] + n]
            outs = []
            for q, k, v in zip(
                halves(qkv[0, 256 * i : n, lanes]), halves(qkv[1, 0:n, lanes]), halves(qkv[2, 0:n, lanes])
            ):
                outs.append(tn(probs_t(k, q * 0.125, mask).astype(BF), v))
            att[256 * i : n, lanes] = join(outs).astype(BF)

    attend(0)
    ggather.ready(2)
    ggather.ready(3)
    for k in range(3):
        pass_z(3, k)
    attend(1)
    save.wait()
    for c in by_z[3]:
        c.got()

    sa = Scatter(h, net, (a0, a1, a2, a3))
    sa.run(lambda chip: nn(att[cut(256 * chip, 256)], wt[wspan(3)]))
    ff_pass(1)
    ff_pass(3)
    r = rows[...].astype(F32) + sa.result() + vecs[2:3]
    res[...] = r
    normed, _ = stats(r)

    fs[my_rows] = (normed * vecs[3:4] + vecs[4:5]).astype(BF)
    gather = Gather(h, net, fs)
    gather.start()
    ff_pass(2)
    for c in ff_z + fgot:
        c.got()
    v0[...] = jnp.zeros_like(v0)
    for s in range(4):
        chip = gather.ready(s)

        @pl.loop(0, 4)
        def _(y, chip=chip):
            span = cut(256 * chip, 256)
            v = nt(fs[span], fw[fslab(y, 0)]) + fcbs[y, 0:1]
            up = nt(ga[span], fw[fslab(y, 1)])
            t = jnp.tanh(0.7978845608028654 * (v + 0.044715 * v * v * v))
            hid[y, span] = (0.5 * v * (1.0 + t)).astype(BF)
            slope = 0.5 * (1.0 + t) + 0.5 * v * (1.0 - t * t) * (
                0.7978845608028654 * (1.0 + 3 * 0.044715 * v * v)
            )
            gpre[y, span] = (up * slope).astype(BF)

    def total(src, k):
        def f(chip):
            return sum(nn(src[y, cut(256 * chip, 256)], fw[fslab(y, k)]) for y in range(4))

        return f

    sb = Scatter(h, net, (b0, b1, b2, b3))
    sb.begin(total(gpre, 0))
    for c in ff_y + ff_z:
        c.gone()
    sa = Scatter(h, net, (a0, a1, a2, a3))
    for j in range(4):
        sa.term(j, total(hid, 1))
    one = {}
    for d in (2, 1, 3, 0):
        y = lax.rem(h.y + d, 4)
        fw[fslab(y, 0)] = tn(gpre[y], fs[...]).astype(BF)
        fw[fslab(y, 1)] = tn(hid[y], ga[...]).astype(BF)
        base = (2 * y + 1 - par) * FPAD
        land = yr.at[d - 1] if d else wx
        one[d] = [
            net.send(fw.at[cut(base + off, size)], land.at[pl.ds(off, size)], to)
            for off, size, to in ((0, A_ROWS, zm), (A_ROWS, B_ROWS, zp))
        ]
        if d == 2:
            sb.relayed()

    load = pltpu.make_async_copy(saved, fs, loc.at[1])
    load.start()
    gs = sb.result()
    normed, inv = stats(res[...])
    up = ga[my_rows].astype(F32)
    gres = up + norm_back(gs, vecs[3:4], normed, inv)
    gsave[...] = gres
    low = gres.astype(BF)
    ba[my_rows] = low
    gather = Gather(h, net, ba)
    gather.start()
    v0[2:3, 0:D] = rows_of(gs * normed)
    v0[3:4, 0:D] = rows_of(gs)
    v0[4:5, 0:D] = rows_of(low.astype(F32))
    v0[5:6, 0:D] = rows_of(up)
    for d in ys:
        pl.semaphore_signal(hz, inc=1, device_id=d, device_id_type=MESH)
    gather.ready(0)
    gather.ready(1)
    for y in range(4):
        v0[2 + y : 3 + y, 1664 : 1664 + FPAD] = rows_of(gpre[y].astype(F32))

    for s in range(4):
        if s > 1:
            gather.ready(s)
        span = cut(256 * gather.chip(s), 256)
        gat[span] = nt(ba[span], wt[wspan(3)]).astype(BF)
    sa.first()
    sa.side(1)
    sa.side(2)
    for kind in range(4):
        for c in by_y[kind, 0] + by_y[kind, 1] + by_y[kind, 2] + by_z[kind]:
            c.gone()
    wt[wspan(3)] = tn(att[...], ba[...]).astype(BF)
    for d in (zm, zp):
        pl.semaphore_signal(hb, inc=1, device_id=d, device_id_type=MESH)

    two = {}

    def collect(d):
        for c in one[d]:
            c.got()
        y = lax.rem(h.y + d, 4)
        span = fslab(y, par)
        other = yr[d - 1, 0:FPAD] if d else wx[0:FPAD]
        fw[span] = (fw[span].astype(F32) + other.astype(F32)).astype(BF)
        if d:
            two[d] = net.send(fw.at[span], ga.at[pl.ds(FPAD * (d - 1), FPAD)], ys[d - 1])

    def attend_back(pair):
        lanes = pl.ds(128 * pair, 128)
        dk[...] = jnp.zeros_like(dk)
        dv[...] = jnp.zeros_like(dv)
        for i in range(4):
            n = 256 * (i + 1)
            mask = masks[MASK_AT[i] : MASK_AT[i] + n]
            dqs, dks, dvs = [], [], []
            for q, k, v, g in zip(
                halves(qkv[0, 256 * i : n, lanes]), halves(qkv[1, 0:n, lanes]),
                halves(qkv[2, 0:n, lanes]), halves(gat[256 * i : n, lanes]),
            ):
                q = q * 0.125
                probs = probs_t(k, q, mask)
                dvs.append(nn(probs.astype(BF), g))
                prod = probs * nt(v, g)
                ds = (prod - probs * jnp.sum(prod, axis=0, keepdims=True)).astype(BF)
                dks.append(nn(ds, q))
                dqs.append(tn(ds, k) * 0.125)
            dv[:n] += join(dvs)
            dk[:n] += join(dks)
            qkv[0, 256 * i : n, lanes] = join(dqs).astype(BF)
        qkv[1, :, lanes] = dk[...].astype(BF)
        qkv[2, :, lanes] = dv[...].astype(BF)

    pl.semaphore_wait(hz, 3)
    collect(2)
    collect(1)
    sa.relayed()
    attend_back(0)
    collect(3)
    collect(0)
    pl.semaphore_signal(ho, inc=1, device_id=zo, device_id_type=MESH)
    for d in ys:
        pl.semaphore_signal(hy, inc=1, device_id=d, device_id_type=MESH)

    def turn_back(v, dst):
        t = jnp.transpose(v.astype(BF))
        for g in range(4):
            dst[g] = t[QUARTER * g : QUARTER * (g + 1)]

    turn_back(res[...] + sa.result() + vecs[5:6], rt)
    by_gx(lambda g: rt.at[g], lambda g: layer_out.at[:, lanes_of(g)])
    lo_own = pltpu.make_async_copy(rt.at[h.gx], layer_out.at[:, lanes_of(h.gx)], loc.at[2])
    lo_own.start()

    def dw(kind):
        return wt if kind == 3 else a0

    wone = {}

    def send_one(kind, k):
        start, at, size, cond = chunks(1 - par)[k]
        half = size // 2
        wone[kind, k] = [
            net.send(
                dw(kind).at[wrow(kind, start + half * i, half)],
                ba.at[pl.ds(128 * kind + at + half * i, half)], to, send_if=cond, recv_if=cond,
            )
            for i, to in ((0, zm), (1, zp))
        ]

    pl.semaphore_wait(hb, 2)
    for k in range(3):
        send_one(3, k)
    attend_back(1)
    load.wait()

    @pl.loop(0, 3)
    def _(kind):
        a0[cut(FRAME * kind, FRAME)] = tn(qkv[kind], fs[...]).astype(BF)

    for k in range(3):
        for kind in range(3):
            send_one(kind, k)
    sb = Scatter(h, net, (b0, b1, b2, b3))
    sb.begin(lambda chip: sum(nn(qkv[k, cut(256 * chip, 256)], wt[wspan(k)]) for k in range(3)))

    wtwo = {}

    def send_two(kind, k):
        slot, held = kind // 3, h.holds(kind)
        home = h.block(kind, h.p)[0] // 2
        start, at, size, cond = chunks(par)[k]
        mine = wrow(kind, start, size)
        for c in wone[kind, k]:
            c.got()

        def add():
            ref = dw(kind)
            s = ref[mine].astype(F32) + ba[128 * kind + at : 128 * kind + at + size].astype(F32)
            ref[mine] = s.astype(BF)

        if cond is None:
            add()
        else:
            pl.when(cond)(add)
        for d in (2, 1, 3):
            goes, comes = lax.rem(h.y + d, 4) == home, held
            if cond is not None:
                goes, comes = goes & cond, comes & cond
            wtwo.setdefault(kind, []).append(
                net.send(
                    dw(kind).at[mine], yr.at[d - 1, pl.ds(128 * slot + at, size)], ys[d - 1],
                    send_if=goes, recv_if=comes,
                )
            )

    pl.semaphore_wait(hy, 3)
    for k in range(3):
        send_two(3, k)
    for kind in range(3):
        send_two(kind, 0)
    sb.relayed()
    for k in (1, 2):
        for kind in range(3):
            send_two(kind, k)
    v0[0:1, 1664:VW] = rows_of(qkv[0].astype(F32))
    v0[1:2, 1664:VW] = rows_of(qkv[2].astype(F32))

    s = fw[fslab(h.y, par)].astype(F32)
    for d in (1, 2, 3):
        two[d].got()
        s = s + ga[FPAD * (d - 1) : FPAD * d].astype(F32)
    s2[0:FPAD] = s.astype(BF)
    pl.semaphore_wait(ho, 1)
    three = net.send(s2.at[pl.ds(0, FPAD)], wx.at[pl.ds(0, FPAD)], zo)

    gf = sb.result()
    normed, inv = stats(rows[...].astype(F32))
    low = gsave[...] + norm_back(gf, vecs[0:1], normed, inv)
    v0[0:1, 0:D] = rows_of(gf * normed)
    v0[1:2, 0:D] = rows_of(gf)
    for c in grds:
        c.gone()
    turn_back(low, rg)
    by_gx(lambda g: rg.at[g], lambda g: input_grad.at[:, lanes_of(g)])
    ig_own = pltpu.make_async_copy(rg.at[h.gx], input_grad.at[:, lanes_of(h.gx)], loc.at[0])
    ig_own.start()
    vys = [net.send(v0, vy.at[h.y], d) for d in ys]
    vy[h.y] = v0[...]

    three.got()
    full = (s2[0:FPAD].astype(F32) + wx[0:FPAD].astype(F32)).astype(BF)
    pl.semaphore_signal(ho, inc=1, device_id=zo, device_id_type=MESH)
    for g in range(4):
        rff[g] = full[:, QUARTER * g : QUARTER * (g + 1)]
    four = by_gx(lambda g: rff.at[g], lambda g: ffo.at[par, g])
    ffo_own = pltpu.make_async_copy(rff.at[h.gx], ffo.at[par, h.gx], loc.at[3])
    ffo_own.start()
    three.gone()

    spans = ((HALF * par, half_own, 0, HALF, None), (192 + EXTRA * par, extra_own, HALF, EXTRA, last))
    for c in vys:
        c.got()
    vz[h.z] = (vy[0] + vy[1]) + (vy[2] + vy[3])
    vzs = [net.send(vz.at[h.z], vz.at[h.z], h.rel(dz=d)) for d in (1, 2, 3)]

    ffo_own.wait()
    for c in four:
        c.got()
    five = []
    for at, size, to in ((0, A_ROWS, zm), (A_ROWS, B_ROWS, zp)):
        ref = ffo.at[par, :, pl.ds(at, size)]
        five.append(net.send(ref, ref, to))

    pl.semaphore_wait(ho, 1)
    wthree = {}
    for kind in range(4):
        slot, held = kind // 3, h.holds(kind)
        for c in wtwo[kind]:
            c.got()
        for start, _, at, size, cond in spans:
            ok = held if cond is None else held & cond
            low_at = 128 * slot + at

            @pl.when(ok)
            def _(kind=kind, start=start, size=size, low_at=low_at):
                s = dw(kind)[wrow(kind, start, size)].astype(F32)
                for d in range(3):
                    s = s + yr[d, low_at : low_at + size].astype(F32)
                s2[low_at : low_at + size] = s.astype(BF)

            wthree.setdefault(kind, []).append(
                net.send(
                    s2.at[pl.ds(low_at, size)], wx.at[pl.ds(low_at, size)], zo, send_if=ok, recv_if=ok
                )
            )

    for c in vzs:
        c.got()
    vx[h.p] = (vz[0] + vz[1]) + (vz[2] + vz[3])
    vxs = [net.send(vx.at[h.p], vx.at[h.p], d) for d in h.ring()]

    for kind in range(4):
        slot, held = kind // 3, h.holds(kind)
        gy, place = h.block(kind, h.p)
        gyt, placet = h.block(kind, h.p - 1)
        xh, xht, yt = lax.rem(gy, 2), lax.rem(gyt, 2), gyt // 2
        for c in wthree[kind]:
            c.got()
        for _, mine, at, size, cond in spans:
            ok = held if cond is None else held & cond
            low_at = 128 * slot + at

            @pl.when(ok)
            def _(slot=slot, at=at, size=size, low_at=low_at):
                span = slice(low_at, low_at + size)
                full = (s2[span].astype(F32) + wx[span].astype(F32)).astype(BF)
                for g in range(4):
                    rwa[slot, g, at : at + size] = full[:, QUARTER * g : QUARTER * (g + 1)]

            for g in range(4):
                same = (g == h.gx) & (xh == h.xh)
                net.send(
                    rwa.at[slot, g, pl.ds(at, size)], frames.at[place, mine], (h.z, g, gy),
                    send_if=ok & jnp.logical_not(same), rs=(rsm if cond is None else rsn).at[place],
                )

                @pl.when(ok & same)
                def _(slot=slot, g=g, place=place, mine=mine, at=at, size=size):
                    frames[place, mine] = rwa[slot, g, at : at + size]

        for g in range(4):
            same = (g == h.gx) & (xht == h.xh) & (yt == h.y)
            ok = held & (h.p > 0) & (par == 0)
            net.send(
                rwa.at[slot, g, pl.ds(0, TAIL)], tl.at[placet], (h.z, g, gyt),
                send_if=ok & jnp.logical_not(same), rs=rst.at[placet],
            )

            @pl.when(ok & same)
            def _(slot=slot, g=g, placet=placet):
                tl[placet] = rwa[slot, g, 0:TAIL]

    wfive = {}
    for i in range(4):
        p, kind = h.unit(i)
        four_heads = p == 7
        far = p != h.p

        @pl.when(far)
        def _(i=i):
            push(
                frames.at[0, pl.ds(0, HALF)], frames.at[i, pl.ds(0, HALF)], ss.at[0], rsm.at[i], ys[0]
            ).wait_recv()

        @pl.when(far & four_heads)
        def _(i=i):
            push(
                frames.at[0, pl.ds(0, EXTRA)], frames.at[i, pl.ds(0, EXTRA)], ss.at[0], rsn.at[i], ys[0]
            ).wait_recv()

        follow = (p + 1) // 2 if i == 3 else (kind * 8 + p + 1) // 6
        has_tail = jnp.logical_not(four_heads)

        @pl.when(has_tail & (par == 0) & jnp.logical_not((p + 1 == h.p) & (follow == h.y)))
        def _(i=i):
            push(tl.at[0], tl.at[i], ss.at[0], rst.at[i], ys[0]).wait_recv()

        for base, size, cond in (
            (HALF * par, 48, None), (192 + EXTRA * par, 16, four_heads),
        ):
            for k, to in ((0, zm), (1, zp)):
                ref = frames.at[i, cut(base + size * k, size)]
                wfive.setdefault(i, []).append(net.send(ref, ref, to, send_if=cond, recv_if=cond))
        for k, to in ((0, zm), (1, zp)):
            ref = tl.at[i, pl.ds(32 * k, 32)]
            wfive[i].append(
                net.send(
                    ref, ref, to, send_if=has_tail & (par == 0), recv_if=has_tail & (par == 1)
                )
            )

    for c in four + five:
        c.got()
        c.gone()
    for k, dst in ((0, gfc), (1, got_)):
        fetch = pltpu.make_async_copy(ffo.at[k], rff, loc.at[3])
        fetch.start()
        fetch.wait()
        for g in range(4):
            t32[SUB * g : SUB * (g + 1)] = rff[g].astype(F32)[0:SUB]
        if k:
            out_copy.wait()
        stage[...] = jnp.transpose(t32[...]).astype(BF)
        out_copy = pltpu.make_async_copy(stage, dst, loc.at[1])
        out_copy.start()

    out_copy.wait()
    for c in vxs:
        c.got()
    total_v = vx[0]
    for p in range(1, 8):
        total_v = total_v + vx[p]
    small[0:8, 0:QUARTER] = pick([total_v[:, QUARTER * g : QUARTER * (g + 1)] for g in range(4)], h.gx)
    for k in (0, 1):
        parts = [vx[p, k : k + 1, 1664 : 1664 + (FRAME if p == 7 else 192)] for p in range(8)]
        small[8 + k : 9 + k] = join(parts)
    small[10:11, 0 : 4 * SUB] = join([vx[4 * h.xh + g, pl.ds(2 + h.y, 1), 1664 : 1664 + SUB] for g in range(4)])
    for i in range(4):
        p, _ = h.unit(i)
        for c in wfive[i]:
            c.got()
        scr[0:FRAME, 0:QUARTER] = frames[i].astype(F32)

        @pl.when(p < 7)
        def _(i=i):
            scr[192 : 192 + TAIL, 0:QUARTER] = tl[i].astype(F32)

        t32[SUB * i : SUB * (i + 1)] = scr[pl.ds(pl.multiple_of(8 * p, 8), SUB), 0:QUARTER]
    stage[...] = jnp.transpose(t32[...]).astype(BF)
    out_copy = pltpu.make_async_copy(stage, gwa, loc.at[1])
    out_copy.start()
    out_copy.wait()
    lo_own.wait()
    ig_own.wait()
    net.finish()


def layer(*args):
    any_ = pl.BlockSpec(memory_space=pl.ANY)
    scratch = [
        pltpu.VMEM((SEQ, D), BF),
        pltpu.VMEM((SEQ, D), BF),
        pltpu.VMEM((SEQ, D), BF),
        pltpu.VMEM((SEQ, D), BF),
        pltpu.VMEM((8 * FPAD, D), BF),
        pltpu.VMEM((3, SEQ, FRAME), BF),
        pltpu.VMEM((SEQ, FRAME), BF),
        pltpu.VMEM((SEQ, FRAME), BF),
        pltpu.VMEM((2560, 256), BF),
        pltpu.VMEM((4, SEQ, FPAD), BF),
        pltpu.VMEM((4, SEQ, FPAD), BF),
        pltpu.VMEM((SEQ, 2 * HEAD_DIM), F32),
        pltpu.VMEM((SEQ, 2 * HEAD_DIM), F32),
        *Scatter.scratch(),
        *Scatter.scratch(),
        pltpu.VMEM((4, QUARTER, ROWS), BF),
        pltpu.VMEM((4, QUARTER, ROWS), BF),
        pltpu.VMEM((8, QUARTER), F32),
        pltpu.VMEM((2, 4, HALF + EXTRA, QUARTER), BF),
        pltpu.VMEM((4, FPAD, QUARTER), BF),
        pltpu.VMEM((4, FRAME, QUARTER), BF),
        pltpu.VMEM((2, TAIL, QUARTER), BF),
        pltpu.VMEM((2, TAIL, QUARTER), BF),
        pltpu.VMEM((336, QUARTER), F32),
        pltpu.VMEM((4 * SUB, QUARTER), F32),
        pltpu.VMEM((QUARTER, 4 * SUB), BF),
        pltpu.VMEM((4, FPAD, QUARTER), BF),
        pltpu.VMEM((4, 8, QUARTER), F32),
        pltpu.VMEM((8, D), F32),
        pltpu.VMEM((1, 128), jnp.int32),
        pltpu.VMEM((8, FPAD), F32),
        pltpu.VMEM((4, 8, FPAD), F32),
        pltpu.VMEM((ROWS, D), F32),
        pltpu.VMEM((ROWS, D), F32),
        pltpu.VMEM((ROWS, D), BF),
        pltpu.VMEM((3, FRAME, D), BF),
        pltpu.VMEM((FRAME, D), BF),
        pltpu.VMEM((FRAME, D), BF),
        pltpu.VMEM((4, TAIL, QUARTER), BF),
        pltpu.VMEM((8, VW), F32),
        pltpu.VMEM((4, 8, VW), F32),
        pltpu.VMEM((4, 8, VW), F32),
        pltpu.VMEM((8, 8, VW), F32),
        pltpu.SemaphoreType.DMA((Net.SIZE,)),
        pltpu.SemaphoreType.DMA((Net.SIZE,)),
        pltpu.SemaphoreType.DMA((2, 4)),
        pltpu.SemaphoreType.DMA((2, 4)),
        pltpu.SemaphoreType.DMA((1,)),
        pltpu.SemaphoreType.DMA((4,)),
        pltpu.SemaphoreType.DMA((4,)),
        pltpu.SemaphoreType.DMA((4,)),
        pltpu.SemaphoreType.DMA((4,)),
        pltpu.SemaphoreType.REGULAR,
        pltpu.SemaphoreType.REGULAR,
        pltpu.SemaphoreType.REGULAR,
        pltpu.SemaphoreType.REGULAR,
        pltpu.SemaphoreType.REGULAR,
    ]
    return pl.pallas_call(
        layer_kernel,
        out_shape=[
            jax.ShapeDtypeStruct((QUARTER, 4 * ROWS), BF),
            jax.ShapeDtypeStruct((QUARTER, 4 * ROWS), BF),
            jax.ShapeDtypeStruct((QUARTER, 4 * SUB), BF),
            jax.ShapeDtypeStruct((QUARTER, 4 * SUB), BF),
            jax.ShapeDtypeStruct((QUARTER, 4 * SUB), BF),
            jax.ShapeDtypeStruct((16, D), F32),
            jax.ShapeDtypeStruct((2, 4, FPAD, QUARTER), BF),
            jax.ShapeDtypeStruct((SEQ, D), BF),
        ],
        in_specs=[VMEM, any_, any_, VMEM, VMEM, any_, any_] + [VMEM] * 9,
        out_specs=[any_, any_, any_, any_, any_, VMEM, any_, any_],
        scratch_shapes=scratch,
        compiler_params=pltpu.CompilerParams(
            collective_id=0, has_side_effects=True, vmem_limit_bytes=64 * 2**20 - 2**16
        ),
        name="layer",
    )(*args)


def per_device(
    tokens_in, segments, norm1_gain, norm1_bias, qkv_weight, query_bias, value_bias, proj_weight,
    proj_bias, norm2_gain, norm2_bias, fc_weight, fc_bias, out_weight, out_bias, out_grad,
):
    layer_out, input_grad, gwa, gfc, got, small, _, _ = layer(
        segments, tokens_in.T, out_grad.T, qkv_weight, proj_weight, fc_weight, out_weight,
        norm1_gain, norm1_bias, proj_bias, norm2_gain, norm2_bias, out_bias,
        query_bias, value_bias, fc_bias,
    )
    return (
        layer_out.T,
        input_grad.T.astype(F32),
        small[0, :QUARTER],
        small[1, :QUARTER],
        gwa[:, : 3 * SUB].astype(F32),
        small[8],
        small[9],
        gwa[:, 3 * SUB :].astype(F32),
        small[4, :QUARTER],
        small[2, :QUARTER],
        small[3, :QUARTER],
        gfc.astype(F32),
        small[10, : 4 * SUB],
        got.astype(F32),
        small[5, :QUARTER],
    )


def solution(mesh):
    return jax.shard_map(
        per_device,
        mesh=mesh,
        in_specs=(
            P(("dp", "gy"), "gx"), P(("dp", "gx"), "gy"), P("gx"), P("gx"), P("gx", "gy"), P(), P(),
            P("gx", "gy"), P("gx"), P("gx"), P("gx"), P("gx", "gy"), P("gy"), P("gx", "gy"), P("gx"),
            P(("dp", "gy"), "gx"),
        ),
        out_specs=(
            P(("dp", "gy"), "gx"), P(("dp", "gy"), "gx"), P("gx"), P("gx"), P("gx", "gy"), P(), P(),
            P("gx", "gy"), P("gx"), P("gx"), P("gx"), P("gx", "gy"), P("gy"), P("gx", "gy"), P("gx"),
        ),
        check_vma=False,
    )
```

```python
import math

import jax
import jax.numpy as jnp
from jax import lax
from jax.experimental import pallas as pl
from jax.experimental.pallas import tpu as pltpu
from jax.sharding import PartitionSpec as P

BF = jnp.bfloat16
F32 = jnp.float32
HEADS = 25
HEAD_DIM = 64
D = HEADS * HEAD_DIM
FF = 6400
SEQ = 1024
DOC = 800
ROWS = 128
QUARTER = 400
SUB = 200
FPAD = 208
FRAME = 256
TAIL = 64
NEG = -1e30
MESH = pl.DeviceIdType.MESH
VMEM = pl.BlockSpec(memory_space=pltpu.VMEM)
SMEM = pl.BlockSpec(memory_space=pltpu.SMEM)


def nt(a, b):
    return lax.dot_general(a, b, (((1,), (1,)), ((), ())), preferred_element_type=F32)


def nn(a, b):
    return lax.dot_general(a, b, (((1,), (0,)), ((), ())), preferred_element_type=F32)


def tn(a, b):
    return lax.dot_general(a, b, (((0,), (0,)), ((), ())), preferred_element_type=F32)


class Here:
    def __init__(self):
        self.z, self.gx, self.gy = (lax.axis_index(a) for a in ("dp", "gx", "gy"))
        self.y, self.xh = self.gy // 2, lax.rem(self.gy, 2)
        self.x = self.xh * 2 + self.gx // 2
        self.c = lax.rem(self.gx, 2)
        self.p = self.x * 2 + self.c

    def at(self, x, c, y, z):
        return (z, lax.rem(x, 2) * 2 + c, y * 2 + x // 2)

    def rel(self, dx=0, flip=0, dy=0, dz=0):
        c = 1 - self.c if flip else self.c
        return self.at(
            lax.rem(self.x + 4 + dx, 4), c, lax.rem(self.y + 4 + dy, 4), lax.rem(self.z + 4 + dz, 4)
        )

    def ring(self):
        return [self.rel(dx, f) for dx in range(4) for f in (0, 1) if dx or f]

    def gxd(self, d):
        return (self.z, self.gx ^ d, self.gy)

    def unit(self, i):
        if i == 3:
            return self.gy, 3
        t = 3 * self.gy + i
        return lax.rem(t, 8), t // 8

    def block(self, kind, p):
        if kind == 3:
            return p, 3
        t = kind * 8 + p
        return t // 3, lax.rem(t, 3)

    def holds(self, kind):
        return self.block(kind, self.p)[0] // 2 == self.y


def meet(peers):
    sem = pltpu.get_barrier_semaphore()
    for d in peers:
        pl.semaphore_signal(sem, inc=1, device_id=d, device_id_type=MESH)
    pl.semaphore_wait(sem, len(peers))


def push(src, dst, ss, rs, d):
    return pltpu.make_async_remote_copy(
        src_ref=src, dst_ref=dst, send_sem=ss, recv_sem=rs, device_id=d, device_id_type=MESH
    )


def stats(v):
    mean = jnp.sum(v, axis=1, keepdims=True) / D
    spread = jnp.sum(v * v, axis=1, keepdims=True) / D - mean * mean
    inv = lax.rsqrt(spread + 1e-5)
    return (v - mean) * inv, inv


def norm_back(u, gain, normed, inv):
    w = u * gain
    a = jnp.sum(w, axis=1, keepdims=True) / D
    b = jnp.sum(w * normed, axis=1, keepdims=True) / D
    return inv * (w - a - normed * b)


def cut(start, size):
    return pl.ds(start if isinstance(start, int) else pl.multiple_of(start, 16), size)


def rows_of(v):
    return jnp.sum(v, axis=0, keepdims=True)


class Copy:
    def __init__(self, desc, send_if=None, recv_if=None):
        self.desc, self.send_if, self.recv_if = desc, send_if, recv_if
        self.is_got = self.is_gone = False

    def on(self, cond, do):
        if cond is None:
            do()
        else:
            pl.when(cond)(do)

    def start(self):
        self.on(self.send_if, self.desc.start)

    def got(self):
        if not self.is_got:
            self.is_got = True
            self.on(self.recv_if, self.desc.wait_recv)

    def gone(self):
        if not self.is_gone:
            self.is_gone = True
            self.on(self.send_if, self.desc.wait_send)


class Net:
    SIZE = 424

    def __init__(self, ss, rs):
        self.ss, self.rs, self.n, self.copies = ss, rs, 0, []

    def make(self, src, dst, d, send_if=None, recv_if=None, rs=None):
        i = self.n
        self.n += 1
        assert i < self.SIZE
        c = Copy(push(src, dst, self.ss.at[i], self.rs.at[i] if rs is None else rs, d), send_if, recv_if)
        if rs is not None:
            c.is_got = True
        self.copies.append(c)
        return c

    def send(self, *args, **kw):
        c = self.make(*args, **kw)
        c.start()
        return c

    def finish(self):
        for c in self.copies:
            c.got()
            c.gone()


class Gather:
    def __init__(self, here, net, buf):
        self.h, self.net, self.buf = here, net, buf

    def row(self, dx):
        return (lax.rem(self.h.x + 4 + dx, 4) * 2 + self.h.c) * ROWS

    def ref(self, dx, half):
        return self.buf.at[cut(self.row(dx), ROWS) if half is None else cut(self.row(dx) + 64 * half, 64)]

    def go(self, dx, d, half=None):
        ref = self.ref(dx, half)
        return self.net.send(ref, ref, d)

    def start(self):
        h = self.h
        self.right, self.left, self.sib = h.rel(1), h.rel(-1), h.rel(0, 1)
        self.r = [self.go(0, self.right, 0), None]
        self.l = [None, self.go(0, self.left, 1)]
        self.r[1] = self.go(0, self.right, 1)
        self.l[0] = self.go(0, self.left, 0)
        self.own = self.go(0, self.sib)
        self.rr = None

    def relays(self):
        if self.rr is None:
            self.r[0].got()
            self.rr = self.go(-1, self.right, 0)
            self.l[1].got()
            self.ll = self.go(1, self.left, 1)

    def chip(self, s):
        return lax.rem(self.h.x + (0, 3, 1, 2)[s], 4)

    def ready(self, s):
        h = self.h
        if s == 0:
            self.own.got()
            return h.x
        if s == 1:
            self.relays()
            self.r[1].got()
            self.f1 = self.go(-1, self.sib)
            self.l[0].got()
            self.f2 = self.go(1, self.sib)
            self.f1.got()
            return lax.rem(h.x + 3, 4)
        if s == 2:
            self.f2.got()
            return lax.rem(h.x + 1, 4)
        self.rr.got()
        f3 = self.go(2, self.sib, 0)
        self.ll.got()
        f4 = self.go(2, self.sib, 1)
        f3.got()
        f4.got()
        for c in (*self.r, *self.l, self.own, self.rr, self.ll, self.f1, self.f2, f3, f4):
            c.gone()
        return lax.rem(h.x + 2, 4)


def raw_at(g, half=None):
    if isinstance(g, int):
        rows, lanes = QUARTER * (g // 3), 512 * (g % 3)
        return slice(rows, rows + QUARTER), slice(lanes, lanes + 512)
    rows, lanes = QUARTER * (g // 3), 512 * lax.rem(g, 3)
    if half is None:
        return cut(rows, QUARTER), pl.ds(pl.multiple_of(lanes, 256), 512)
    return cut(rows, QUARTER), pl.ds(pl.multiple_of(lanes + 256 * half, 256), 256)


class RawGather(Gather):
    def go(self, dx, d, half=None):
        x = lax.rem(self.h.x + 4 + dx, 4)
        where = raw_at(lax.rem(x, 2) * 2 + self.h.c, half)
        copies = []
        for xh in range(2):
            ref = self.buf[xh].at[where]
            i = self.net.n
            c = self.net.make(ref, ref, d)
            if xh:
                self.net.n -= 1
                self.net.copies.pop()
                c.desc = push(ref, ref, self.net.ss.at[i - 1], self.net.rs.at[i - 1], d)
            pl.when(x // 2 == xh)(c.desc.start)
            copies.append(c)
        return copies[0]


class Scatter:
    @staticmethod
    def scratch():
        return [
            pltpu.VMEM((SEQ, D), BF),
            pltpu.VMEM((4, ROWS, D), BF),
            pltpu.VMEM((2, ROWS, D), BF),
            pltpu.VMEM((ROWS, D), BF),
        ]

    STEPS = (2, 1, -1, 0)

    def __init__(self, here, net, refs):
        self.h, self.net = here, net
        self.part, self.mate, self.far, self.relay = refs
        self.pair, self.out, self.ends = {}, [], []

    def at(self, j, c, half=None):
        base = 256 * j + ROWS * c
        return cut(base, ROWS) if half is None else cut(base + 64 * half, 64)

    def term(self, j, f):
        h = self.h
        chip = lax.rem(h.x + 4 + self.STEPS[j], 4)
        self.part[256 * j : 256 * (j + 1)] = f(chip).astype(BF)
        self.pair[j] = self.net.send(
            self.part.at[self.at(j, 1 - h.c)], self.mate.at[j], h.rel(0, 1)
        )

    def total(self, j):
        self.pair[j].got()
        return self.part[self.at(j, self.h.c)].astype(F32) + self.mate[j].astype(F32)

    def link(self, j, half, dst, dx):
        c = self.net.send(self.part.at[self.at(j, self.h.c, half)], dst, self.h.rel(dx))
        self.out.append(c)
        return c

    def first(self):
        self.part[self.at(0, self.h.c)] = self.total(0).astype(BF)
        self.in_r = self.link(0, 0, self.relay.at[pl.ds(0, 64)], 1)
        self.in_l = self.link(0, 1, self.relay.at[pl.ds(64, 64)], -1)

    def side(self, j):
        half = 1 if j == 1 else 0
        self.part[self.at(j, self.h.c)] = self.total(j).astype(BF)
        self.ends.append(self.link(j, half, self.far.at[j - 1, pl.ds(64 * half, 64)], self.STEPS[j]))

    def relayed(self):
        for j, half, c in ((1, 0, self.in_r), (2, 1, self.in_l)):
            c.got()
            span, mine = pl.ds(64 * half, 64), self.at(j, self.h.c, half)
            s = self.part[mine].astype(F32) + self.relay[span].astype(F32)
            self.part[mine] = s.astype(BF)
            self.ends.append(self.link(j, half, self.far.at[j - 1, span], self.STEPS[j]))

    def begin(self, f):
        self.term(0, f)
        self.term(1, f)
        self.first()
        self.term(2, f)
        self.side(1)
        self.term(3, f)
        self.side(2)

    def run(self, f):
        self.begin(f)
        self.relayed()

    def result(self):
        t = self.total(3)
        for c in self.ends:
            c.got()
        t = t + self.far[0].astype(F32) + self.far[1].astype(F32)
        for c in list(self.pair.values()) + self.out:
            c.gone()
        return t


def join(blocks):
    return jnp.concatenate(blocks, axis=1)


def set_masks(masks, begin):
    for i in range(4):
        n = 256 * (i + 1)
        b = lax.broadcasted_iota(jnp.int32, (n, 256), 0)
        a = lax.broadcasted_iota(jnp.int32, (n, 256), 1) + 256 * i

        def doc(t):
            return (t >= begin).astype(jnp.int32) + (t >= begin + DOC).astype(jnp.int32)

        masks[MASK_AT[i] : MASK_AT[i] + n] = jnp.where(
            (b <= a) & (doc(a) == doc(b)), 0.0, NEG
        ).astype(BF)


def probs_t(key, query, mask):
    s = nt(key, query) + mask.astype(F32)
    e = jnp.exp(s - jnp.max(s, axis=0, keepdims=True))
    return e * (1.0 / jnp.sum(e, axis=0, keepdims=True))


def halves(v):
    return v[:, :HEAD_DIM], v[:, HEAD_DIM:]


MASK_AT = (0, 256, 768, 1536)
A_ROWS, B_ROWS = 112, 96
HALF = 96
EXTRA = 32
VW = 1664 + 256


def layer_kernel(
    segs, tok, grd, wq, wp, fcw, otw, g1, c1, pb, g2, c2, ob, qbias, vbias, fbias,
    layer_out, input_grad, gwa, gfc, got_, small, ffo, saved,
    *refs,
):
    (
        fs, ga, ba, wt, fw, qkv, att, gat, masks, hid, gpre, dk, dv,
        a0, a1, a2, a3, b0, b1, b2, b3,
        rt, rg, vec, rwa, rff, frames, tsend, trecv, scr, t32, stage, fbuf, rv, vecs, seg, fcb, fcbs,
        res, gsave, rows, yr, s2, wx, tl, v0, vy, vz, vx,
        ss, rs, rsw, rsx, rseg, rsm, rsn, rst, loc, hz, hb, hy, ho,
    ) = refs
    h = Here()
    net = Net(ss, rs)
    par = lax.rem(h.z, 2)
    last = h.p == 7
    ys = [h.rel(dy=d) for d in (1, 2, 3)]
    zp, zm, zo = h.rel(dz=1), h.rel(dz=-1), h.rel(dz=2)
    plane = [h.rel(dx, f, dy) for dy in range(4) for dx in range(4) for f in (0, 1) if dx or f or dy]
    everyone = plane + [zp, zm, zo]
    barrier = pltpu.get_barrier_semaphore()
    for d in everyone:
        pl.semaphore_signal(barrier, inc=1, device_id=d, device_id_type=MESH)

    @pl.when(par == 0)
    def _():
        pltpu.make_async_copy(fcw, stage, loc.at[0]).start()

    @pl.when(par == 1)
    def _():
        pltpu.make_async_copy(otw, stage, loc.at[0]).start()

    raws = (ba, b0)
    for k in range(2):

        @pl.when(h.xh == k)
        def _(k=k):
            pltpu.make_async_copy(tok, raws[k].at[raw_at(h.gx)], loc.at[2]).start()

    vec[...] = jnp.concatenate(
        [v[...].reshape(1, QUARTER) for v in (g1, c1, pb, g2, c2, ob)] + [jnp.zeros((2, QUARTER), F32)], axis=0
    )
    t32[0 : 3 * SUB] = jnp.transpose(wq[...]).astype(F32)
    t32[3 * SUB : 4 * SUB] = jnp.transpose(wp[...]).astype(F32)

    def sub_tail(i):
        return t32[SUB * (i + 1) - TAIL : SUB * (i + 1)]

    for k, i in enumerate((2, 3)):
        tsend[k] = sub_tail(i).astype(BF)
    row = lax.broadcasted_iota(jnp.int32, (FRAME, QUARTER), 0)
    half_own = cut(HALF * par, HALF)
    extra_own = cut(192 + EXTRA * par, EXTRA)

    def frame(i, before):
        p, _ = h.unit(i)
        scr[pl.ds(pl.multiple_of(8 * p, 8), TAIL), 0:QUARTER] = before
        scr[pl.ds(pl.multiple_of(8 * p + TAIL, 8), SUB), 0:QUARTER] = t32[SUB * i : SUB * (i + 1)]
        frames[i] = jnp.where((row < 192) | (p == 7), scr[TAIL : TAIL + FRAME, 0:QUARTER], 0.0).astype(BF)

    fsends = []

    def send_frame(i):
        p, _ = h.unit(i)
        slot = i // 3
        dest = h.at(p // 2, lax.rem(p, 2), h.y, h.z)
        mine = p == h.p
        far = jnp.logical_not(mine)
        for src, at, size, cond, sem in (
            (half_own, 0, HALF, far, rsw), (extra_own, HALF, EXTRA, far & (p == 7), rsx),
        ):
            fsends.append(
                net.send(
                    frames.at[i, src], rwa.at[slot, h.gx, pl.ds(at, size)], dest,
                    send_if=cond, rs=sem.at[slot, h.gx],
                )
            )

        @pl.when(mine)
        def _():
            rwa[slot, h.gx, 0:HALF] = frames[i, half_own]
            rwa[slot, h.gx, HALF : HALF + EXTRA] = frames[i, extra_own]

    for i in (1, 2):
        frame(i, sub_tail(i - 1))

    @pl.when(par == 0)
    def _():
        pltpu.make_async_copy(fcw, stage, loc.at[0]).wait()

    @pl.when(par == 1)
    def _():
        pltpu.make_async_copy(otw, stage, loc.at[0]).wait()

    turned = jnp.transpose(stage[...]).astype(F32)
    blank = jnp.zeros((FPAD - SUB, QUARTER), F32)
    for g in range(4):
        fbuf[g] = jnp.concatenate([turned[SUB * g : SUB * (g + 1)], blank], axis=0).astype(BF)
    for k in range(2):

        @pl.when(h.xh == k)
        def _(k=k):
            pltpu.make_async_copy(tok, raws[k].at[raw_at(h.gx)], loc.at[2]).wait()

    pl.semaphore_wait(barrier, len(everyone))

    tail = net.send(tsend, trecv, (h.z, h.gx, lax.rem(h.gy + 1, 8)))

    def lanes_of(g):
        return pl.ds(pl.multiple_of(ROWS * g, ROWS), ROWS)

    def by_gx(src, dst):
        return [net.send(src(h.gx ^ d), dst(h.gx), h.gxd(d)) for d in (1, 2, 3)]

    for i in (1, 2):
        send_frame(i)
    gather = RawGather(h, net, raws)
    gather.start()
    vgot = [net.send(vec, rv.at[h.gx], h.gxd(d)) for d in (1, 2, 3)]
    rv[h.gx] = vec[...]
    at_zero = h.gy == 0
    alone = at_zero & (h.gx == 0)
    for j in range(8):
        me = (h.gx == 0) if j == 0 else False
        cond = at_zero & jnp.logical_not(me)
        net.send(segs, seg, h.at(j // 2, j % 2, h.gx, h.z), send_if=cond, rs=rseg.at[0])

    @pl.when(alone)
    def _():
        seg[...] = segs[...]

    def pick(values, index):
        out = values[0]
        for k, v in enumerate(values[1:]):
            out = jnp.where(index == k + 1, v, out)
        return out

    tail.got()
    for i in (0, 3):
        frame(i, trecv[i // 3].astype(F32))
        send_frame(i)

    my_rows = cut(ROWS * h.p, ROWS)

    def turn(ref):
        return jnp.transpose(jnp.concatenate([ref[g] for g in range(4)], axis=0))

    fbias1 = fbias[...].reshape(1, 4 * SUB)
    low_bias = pick([fbias1[:, SUB * g : SUB * (g + 1)] for g in range(4)], h.gx)
    fcb[...] = jnp.broadcast_to(join([low_bias, jnp.zeros((1, FPAD - SUB), F32)]), (8, FPAD))
    fgot = [net.send(fcb, fcbs.at[h.y], d) for d in ys]
    fcbs[h.y] = fcb[...]
    lane = lax.broadcasted_iota(jnp.int32, (1, FRAME), 1)
    qb, vb = (
        jnp.where(
            (lane < 192) | last, pick([v[:, 192 * p : 192 * p + FRAME] for p in range(8)], h.p), 0.0
        )
        for v in (qbias[...].reshape(1, D), vbias[...].reshape(1, D))
    )
    qkvb = (qb, jnp.zeros_like(qb), vb)

    def wrow(kind, start, size):
        return cut(FRAME * kind + start, size)

    w_half = lambda kind: wrow(kind, HALF * par, HALF)
    w_extra = lambda kind: wrow(kind, 192 + EXTRA * par, EXTRA)

    def wspan(kind):
        return slice(FRAME * kind, FRAME * (kind + 1))

    def take_frames(kind):
        slot = kind // 3
        held = h.holds(kind)
        gy, _ = h.block(kind, h.p)
        xh = lax.rem(gy, 2)
        for g in range(4):
            other = held & jnp.logical_not((g == h.gx) & (xh == h.xh))

            @pl.when(other)
            def _(slot=slot, g=g):
                push(
                    frames.at[0, pl.ds(0, HALF)], rwa.at[slot, g, pl.ds(0, HALF)], ss.at[0],
                    rsw.at[slot, g], ys[0],
                ).wait_recv()

            @pl.when(other & last)
            def _(slot=slot, g=g):
                push(
                    frames.at[0, pl.ds(0, EXTRA)], rwa.at[slot, g, pl.ds(HALF, EXTRA)], ss.at[0],
                    rsx.at[slot, g], ys[0],
                ).wait_recv()

        @pl.when(held)
        def _():
            wt[w_half(kind)] = join([rwa[slot, g, 0:HALF] for g in range(4)])

        @pl.when(held & last)
        def _():
            wt[w_extra(kind)] = join([rwa[slot, g, HALF : HALF + EXTRA] for g in range(4)])

        @pl.when(jnp.logical_not(last))
        def _():
            wt[wrow(kind, 192, 64)] = jnp.zeros((64, D), BF)

    by_y, by_z = {}, {}

    chunks = lambda q: (
        (HALF * q, 0, 64, None), (HALF * q + 64, 64, 32, None), (192 + EXTRA * q, HALF, EXTRA, last),
    )

    def pass_y(kind):
        held = h.holds(kind)
        for k, (start, _, size, cond) in enumerate(chunks(par)):
            by_y[kind, k] = []
            for d in (2, 1, 3):
                comes = h.block(kind, h.p)[0] // 2 == lax.rem(h.y + 4 - d, 4)
                s_if = held if cond is None else held & cond
                r_if = comes if cond is None else comes & cond
                ref = wt.at[wrow(kind, start, size)]
                by_y[kind, k].append(net.send(ref, ref, ys[d - 1], send_if=s_if, recv_if=r_if))

    def pass_z(kind, k):
        start, _, size, cond = chunks(par)[k]
        for c in by_y[kind, k]:
            c.got()
        for off, d in ((0, zm), (size // 2, zp)):
            ref = wt.at[wrow(kind, start + off, size // 2)]
            by_z.setdefault(kind, []).append(net.send(ref, ref, d, send_if=cond, recv_if=cond))

    gather.relays()
    for kind in range(3):
        take_frames(kind)
        pass_y(kind)
    gather.ready(0)
    gather.ready(1)
    ffs = by_gx(lambda g: fbuf.at[g], lambda g: rff.at[g])
    rff[h.gx] = fbuf[h.gx]
    for kind in range(3):
        pass_z(kind, 0)

    gather.ready(2)
    gather.ready(3)
    grds = by_gx(lambda g: grd.at[:, lanes_of(g)], lambda g: rg.at[g])
    grd_own = pltpu.make_async_copy(grd.at[:, lanes_of(h.gx)], rg.at[h.gx], loc.at[3])
    grd_own.start()
    for k in (1, 2):
        for kind in range(3):
            pass_z(kind, k)
    take_frames(3)
    pass_y(3)

    for c in ffs:
        c.got()
        c.gone()
    fslab = lambda y, k: cut((2 * y + k) * FPAD, FPAD)
    mine_ff = fslab(h.y, par)
    fw[mine_ff] = join([rff[g] for g in range(4)])
    ff_y = [net.send(fw.at[mine_ff], fw.at[mine_ff], d) for d in ys]
    ff_z = []

    def ff_pass(d):
        if d:
            ff_y[d - 1].got()
        base = (2 * lax.rem(h.y + 4 - d, 4) + par) * FPAD
        for off, size, to in ((0, A_ROWS, zm), (A_ROWS, B_ROWS, zp)):
            ref = fw.at[cut(base + off, size)]
            ff_z.append(net.send(ref, ref, to))
    for c in vgot:
        c.got()
    vecs[...] = join([rv[g] for g in range(4)])

    for xh in range(2):

        @pl.loop(0, 4)
        def _(j, xh=xh):
            blocks = []
            for g in range(4):
                r, l = raw_at(g)
                blocks.append(raws[xh][r, pl.ds(pl.multiple_of(l.start + ROWS * j, ROWS), ROWS)])
            x = jnp.transpose(jnp.concatenate(blocks, axis=0))
            normed, _ = stats(x.astype(F32))
            fs[cut(512 * xh + ROWS * j, ROWS)] = (normed * vecs[0:1] + vecs[1:2]).astype(BF)

            @pl.when(h.p == 4 * xh + j)
            def _():
                rows[...] = x

    @pl.when(jnp.logical_not(alone))
    def _():
        push(segs, seg, ss.at[0], rseg.at[0], ys[0]).wait_recv()

    begin = jnp.sum((seg[...] == 0).astype(F32), axis=1, keepdims=True).astype(jnp.int32)
    set_masks(masks, begin)
    for c in grds:
        c.got()
    grd_own.wait()
    ga[my_rows] = turn(rg)
    ggather = Gather(h, net, ga)
    ggather.start()
    for kind in range(3):
        for c in by_z[kind]:
            c.got()

    ff_pass(0)

    @pl.loop(0, 4)
    def _(chip):
        span = cut(256 * chip, 256)
        for kind in range(3):
            qkv[kind, span] = (nt(fs[span], wt[wspan(kind)]) + qkvb[kind]).astype(BF)

    save = pltpu.make_async_copy(fs, saved, loc.at[1])
    save.start()
    for c in fsends:
        c.gone()
    ggather.ready(0)
    ggather.ready(1)

    def attend(pair):
        lanes = pl.ds(128 * pair, 128)
        for i in range(4):
            n = 256 * (i + 1)
            mask = masks[MASK_AT[i] : MASK_AT[i] + n]
            outs = []
            for q, k, v in zip(
                halves(qkv[0, 256 * i : n, lanes]), halves(qkv[1, 0:n, lanes]), halves(qkv[2, 0:n, lanes])
            ):
                outs.append(tn(probs_t(k, q * 0.125, mask).astype(BF), v))
            att[256 * i : n, lanes] = join(outs).astype(BF)

    attend(0)
    ggather.ready(2)
    ggather.ready(3)
    for k in range(3):
        pass_z(3, k)
    attend(1)
    save.wait()
    for c in by_z[3]:
        c.got()

    sa = Scatter(h, net, (a0, a1, a2, a3))
    sa.run(lambda chip: nn(att[cut(256 * chip, 256)], wt[wspan(3)]))
    ff_pass(1)
    ff_pass(3)
    r = rows[...].astype(F32) + sa.result() + vecs[2:3]
    res[...] = r
    normed, _ = stats(r)

    fs[my_rows] = (normed * vecs[3:4] + vecs[4:5]).astype(BF)
    gather = Gather(h, net, fs)
    gather.start()
    ff_pass(2)
    for c in ff_z + fgot:
        c.got()
    v0[...] = jnp.zeros_like(v0)
    for s in range(4):
        chip = gather.ready(s)

        @pl.loop(0, 4)
        def _(y, chip=chip):
            span = cut(256 * chip, 256)
            v = nt(fs[span], fw[fslab(y, 0)]) + fcbs[y, 0:1]
            up = nt(ga[span], fw[fslab(y, 1)])
            t = jnp.tanh(0.7978845608028654 * (v + 0.044715 * v * v * v))
            hid[y, span] = (0.5 * v * (1.0 + t)).astype(BF)
            slope = 0.5 * (1.0 + t) + 0.5 * v * (1.0 - t * t) * (
                0.7978845608028654 * (1.0 + 3 * 0.044715 * v * v)
            )
            gpre[y, span] = (up * slope).astype(BF)

    def total(src, k):
        def f(chip):
            return sum(nn(src[y, cut(256 * chip, 256)], fw[fslab(y, k)]) for y in range(4))

        return f

    sb = Scatter(h, net, (b0, b1, b2, b3))
    sb.begin(total(gpre, 0))
    for c in ff_y + ff_z:
        c.gone()
    sa = Scatter(h, net, (a0, a1, a2, a3))
    for j in range(4):
        sa.term(j, total(hid, 1))
    one = {}
    for d in (2, 1, 3, 0):
        y = lax.rem(h.y + d, 4)
        fw[fslab(y, 0)] = tn(gpre[y], fs[...]).astype(BF)
        fw[fslab(y, 1)] = tn(hid[y], ga[...]).astype(BF)
        base = (2 * y + 1 - par) * FPAD
        land = yr.at[d - 1] if d else wx
        one[d] = [
            net.send(fw.at[cut(base + off, size)], land.at[pl.ds(off, size)], to)
            for off, size, to in ((0, A_ROWS, zm), (A_ROWS, B_ROWS, zp))
        ]
        if d == 2:
            sb.relayed()

    load = pltpu.make_async_copy(saved, fs, loc.at[1])
    load.start()
    gs = sb.result()
    normed, inv = stats(res[...])
    up = ga[my_rows].astype(F32)
    gres = up + norm_back(gs, vecs[3:4], normed, inv)
    gsave[...] = gres
    low = gres.astype(BF)
    ba[my_rows] = low
    gather = Gather(h, net, ba)
    gather.start()
    v0[2:3, 0:D] = rows_of(gs * normed)
    v0[3:4, 0:D] = rows_of(gs)
    v0[4:5, 0:D] = rows_of(low.astype(F32))
    v0[5:6, 0:D] = rows_of(up)
    for d in ys:
        pl.semaphore_signal(hz, inc=1, device_id=d, device_id_type=MESH)
    gather.ready(0)
    gather.ready(1)
    for y in range(4):
        v0[2 + y : 3 + y, 1664 : 1664 + FPAD] = rows_of(gpre[y].astype(F32))

    for s in range(4):
        if s > 1:
            gather.ready(s)
        span = cut(256 * gather.chip(s), 256)
        gat[span] = nt(ba[span], wt[wspan(3)]).astype(BF)
    sa.first()
    sa.side(1)
    sa.side(2)
    for kind in range(4):
        for c in by_y[kind, 0] + by_y[kind, 1] + by_y[kind, 2] + by_z[kind]:
            c.gone()
    wt[wspan(3)] = tn(att[...], ba[...]).astype(BF)
    for d in (zm, zp):
        pl.semaphore_signal(hb, inc=1, device_id=d, device_id_type=MESH)

    two = {}

    def collect(d):
        for c in one[d]:
            c.got()
        y = lax.rem(h.y + d, 4)
        span = fslab(y, par)
        other = yr[d - 1, 0:FPAD] if d else wx[0:FPAD]
        fw[span] = (fw[span].astype(F32) + other.astype(F32)).astype(BF)
        if d:
            two[d] = net.send(fw.at[span], ga.at[pl.ds(FPAD * (d - 1), FPAD)], ys[d - 1])

    def attend_back(pair):
        lanes = pl.ds(128 * pair, 128)
        dk[...] = jnp.zeros_like(dk)
        dv[...] = jnp.zeros_like(dv)
        for i in range(4):
            n = 256 * (i + 1)
            mask = masks[MASK_AT[i] : MASK_AT[i] + n]
            dqs, dks, dvs = [], [], []
            for q, k, v, g in zip(
                halves(qkv[0, 256 * i : n, lanes]), halves(qkv[1, 0:n, lanes]),
                halves(qkv[2, 0:n, lanes]), halves(gat[256 * i : n, lanes]),
            ):
                q = q * 0.125
                probs = probs_t(k, q, mask)
                dvs.append(nn(probs.astype(BF), g))
                prod = probs * nt(v, g)
                ds = (prod - probs * jnp.sum(prod, axis=0, keepdims=True)).astype(BF)
                dks.append(nn(ds, q))
                dqs.append(tn(ds, k) * 0.125)
            dv[:n] += join(dvs)
            dk[:n] += join(dks)
            qkv[0, 256 * i : n, lanes] = join(dqs).astype(BF)
        qkv[1, :, lanes] = dk[...].astype(BF)
        qkv[2, :, lanes] = dv[...].astype(BF)

    pl.semaphore_wait(hz, 3)
    collect(2)
    collect(1)
    sa.relayed()
    attend_back(0)
    collect(3)
    collect(0)
    pl.semaphore_signal(ho, inc=1, device_id=zo, device_id_type=MESH)
    for d in ys:
        pl.semaphore_signal(hy, inc=1, device_id=d, device_id_type=MESH)

    def turn_back(v, dst):
        t = jnp.transpose(v.astype(BF))
        for g in range(4):
            dst[g] = t[QUARTER * g : QUARTER * (g + 1)]

    turn_back(res[...] + sa.result() + vecs[5:6], rt)
    by_gx(lambda g: rt.at[g], lambda g: layer_out.at[:, lanes_of(g)])
    lo_own = pltpu.make_async_copy(rt.at[h.gx], layer_out.at[:, lanes_of(h.gx)], loc.at[2])
    lo_own.start()

    def dw(kind):
        return wt if kind == 3 else a0

    wone = {}

    def send_one(kind, k):
        start, at, size, cond = chunks(1 - par)[k]
        half = size // 2
        wone[kind, k] = [
            net.send(
                dw(kind).at[wrow(kind, start + half * i, half)],
                ba.at[pl.ds(128 * kind + at + half * i, half)], to, send_if=cond, recv_if=cond,
            )
            for i, to in ((0, zm), (1, zp))
        ]

    pl.semaphore_wait(hb, 2)
    for k in range(3):
        send_one(3, k)
    attend_back(1)
    load.wait()

    @pl.loop(0, 3)
    def _(kind):
        a0[cut(FRAME * kind, FRAME)] = tn(qkv[kind], fs[...]).astype(BF)

    for k in range(3):
        for kind in range(3):
            send_one(kind, k)
    sb = Scatter(h, net, (b0, b1, b2, b3))
    sb.begin(lambda chip: sum(nn(qkv[k, cut(256 * chip, 256)], wt[wspan(k)]) for k in range(3)))

    wtwo = {}

    def send_two(kind, k):
        slot, held = kind // 3, h.holds(kind)
        home = h.block(kind, h.p)[0] // 2
        start, at, size, cond = chunks(par)[k]
        mine = wrow(kind, start, size)
        for c in wone[kind, k]:
            c.got()

        def add():
            ref = dw(kind)
            s = ref[mine].astype(F32) + ba[128 * kind + at : 128 * kind + at + size].astype(F32)
            ref[mine] = s.astype(BF)

        if cond is None:
            add()
        else:
            pl.when(cond)(add)
        for d in (2, 1, 3):
            goes, comes = lax.rem(h.y + d, 4) == home, held
            if cond is not None:
                goes, comes = goes & cond, comes & cond
            wtwo.setdefault(kind, []).append(
                net.send(
                    dw(kind).at[mine], yr.at[d - 1, pl.ds(128 * slot + at, size)], ys[d - 1],
                    send_if=goes, recv_if=comes,
                )
            )

    pl.semaphore_wait(hy, 3)
    for k in range(3):
        send_two(3, k)
    for kind in range(3):
        send_two(kind, 0)
    sb.relayed()
    for k in (1, 2):
        for kind in range(3):
            send_two(kind, k)
    v0[0:1, 1664:VW] = rows_of(qkv[0].astype(F32))
    v0[1:2, 1664:VW] = rows_of(qkv[2].astype(F32))

    s = fw[fslab(h.y, par)].astype(F32)
    for d in (1, 2, 3):
        two[d].got()
        s = s + ga[FPAD * (d - 1) : FPAD * d].astype(F32)
    s2[0:FPAD] = s.astype(BF)
    pl.semaphore_wait(ho, 1)
    three = net.send(s2.at[pl.ds(0, FPAD)], wx.at[pl.ds(0, FPAD)], zo)

    gf = sb.result()
    normed, inv = stats(rows[...].astype(F32))
    low = gsave[...] + norm_back(gf, vecs[0:1], normed, inv)
    v0[0:1, 0:D] = rows_of(gf * normed)
    v0[1:2, 0:D] = rows_of(gf)
    for c in grds:
        c.gone()
    turn_back(low, rg)
    by_gx(lambda g: rg.at[g], lambda g: input_grad.at[:, lanes_of(g)])
    ig_own = pltpu.make_async_copy(rg.at[h.gx], input_grad.at[:, lanes_of(h.gx)], loc.at[0])
    ig_own.start()
    vys = [net.send(v0, vy.at[h.y], d) for d in ys]
    vy[h.y] = v0[...]

    three.got()
    full = (s2[0:FPAD].astype(F32) + wx[0:FPAD].astype(F32)).astype(BF)
    pl.semaphore_signal(ho, inc=1, device_id=zo, device_id_type=MESH)
    for g in range(4):
        rff[g] = full[:, QUARTER * g : QUARTER * (g + 1)]
    four = by_gx(lambda g: rff.at[g], lambda g: ffo.at[par, g])
    ffo_own = pltpu.make_async_copy(rff.at[h.gx], ffo.at[par, h.gx], loc.at[3])
    ffo_own.start()
    three.gone()

    spans = ((HALF * par, half_own, 0, HALF, None), (192 + EXTRA * par, extra_own, HALF, EXTRA, last))
    pl.semaphore_wait(ho, 1)
    wthree = {}
    for kind in range(4):
        slot, held = kind // 3, h.holds(kind)
        for c in wtwo[kind]:
            c.got()
        for start, _, at, size, cond in spans:
            ok = held if cond is None else held & cond
            low_at = 128 * slot + at

            @pl.when(ok)
            def _(kind=kind, start=start, size=size, low_at=low_at):
                s = dw(kind)[wrow(kind, start, size)].astype(F32)
                for d in range(3):
                    s = s + yr[d, low_at : low_at + size].astype(F32)
                s2[low_at : low_at + size] = s.astype(BF)

            wthree.setdefault(kind, []).append(
                net.send(
                    s2.at[pl.ds(low_at, size)], wx.at[pl.ds(low_at, size)], zo, send_if=ok, recv_if=ok
                )
            )

    for c in vys:
        c.got()
    vz[h.z] = (vy[0] + vy[1]) + (vy[2] + vy[3])
    vzs = [net.send(vz.at[h.z], vz.at[h.z], h.rel(dz=d)) for d in (1, 2, 3)]

    ffo_own.wait()
    for c in four:
        c.got()
    five = []
    for at, size, to in ((0, A_ROWS, zm), (A_ROWS, B_ROWS, zp)):
        ref = ffo.at[par, :, pl.ds(at, size)]
        five.append(net.send(ref, ref, to))

    for c in vzs:
        c.got()
    vx[h.p] = (vz[0] + vz[1]) + (vz[2] + vz[3])
    vxs = [net.send(vx.at[h.p], vx.at[h.p], d) for d in h.ring()]

    for kind in range(4):
        slot, held = kind // 3, h.holds(kind)
        gy, place = h.block(kind, h.p)
        gyt, placet = h.block(kind, h.p - 1)
        xh, xht, yt = lax.rem(gy, 2), lax.rem(gyt, 2), gyt // 2
        for c in wthree[kind]:
            c.got()
        for _, mine, at, size, cond in spans:
            ok = held if cond is None else held & cond
            low_at = 128 * slot + at

            @pl.when(ok)
            def _(slot=slot, at=at, size=size, low_at=low_at):
                span = slice(low_at, low_at + size)
                full = (s2[span].astype(F32) + wx[span].astype(F32)).astype(BF)
                for g in range(4):
                    rwa[slot, g, at : at + size] = full[:, QUARTER * g : QUARTER * (g + 1)]

            for g in range(4):
                same = (g == h.gx) & (xh == h.xh)
                net.send(
                    rwa.at[slot, g, pl.ds(at, size)], frames.at[place, mine], (h.z, g, gy),
                    send_if=ok & jnp.logical_not(same), rs=(rsm if cond is None else rsn).at[place],
                )

                @pl.when(ok & same)
                def _(slot=slot, g=g, place=place, mine=mine, at=at, size=size):
                    frames[place, mine] = rwa[slot, g, at : at + size]

        for g in range(4):
            same = (g == h.gx) & (xht == h.xh) & (yt == h.y)
            ok = held & (h.p > 0) & (par == 0)
            net.send(
                rwa.at[slot, g, pl.ds(0, TAIL)], tl.at[placet], (h.z, g, gyt),
                send_if=ok & jnp.logical_not(same), rs=rst.at[placet],
            )

            @pl.when(ok & same)
            def _(slot=slot, g=g, placet=placet):
                tl[placet] = rwa[slot, g, 0:TAIL]

    wfive = {}
    for i in range(4):
        p, kind = h.unit(i)
        four_heads = p == 7
        far = p != h.p

        @pl.when(far)
        def _(i=i):
            push(
                frames.at[0, pl.ds(0, HALF)], frames.at[i, pl.ds(0, HALF)], ss.at[0], rsm.at[i], ys[0]
            ).wait_recv()

        @pl.when(far & four_heads)
        def _(i=i):
            push(
                frames.at[0, pl.ds(0, EXTRA)], frames.at[i, pl.ds(0, EXTRA)], ss.at[0], rsn.at[i], ys[0]
            ).wait_recv()

        follow = (p + 1) // 2 if i == 3 else (kind * 8 + p + 1) // 6
        has_tail = jnp.logical_not(four_heads)

        @pl.when(has_tail & (par == 0) & jnp.logical_not((p + 1 == h.p) & (follow == h.y)))
        def _(i=i):
            push(tl.at[0], tl.at[i], ss.at[0], rst.at[i], ys[0]).wait_recv()

        for base, size, cond in (
            (HALF * par, 48, None), (192 + EXTRA * par, 16, four_heads),
        ):
            for k, to in ((0, zm), (1, zp)):
                ref = frames.at[i, cut(base + size * k, size)]
                wfive.setdefault(i, []).append(net.send(ref, ref, to, send_if=cond, recv_if=cond))
        for k, to in ((0, zm), (1, zp)):
            ref = tl.at[i, pl.ds(32 * k, 32)]
            wfive[i].append(
                net.send(
                    ref, ref, to, send_if=has_tail & (par == 0), recv_if=has_tail & (par == 1)
                )
            )

    for c in four + five:
        c.got()
        c.gone()
    for k, dst in ((0, gfc), (1, got_)):
        fetch = pltpu.make_async_copy(ffo.at[k], rff, loc.at[3])
        fetch.start()
        fetch.wait()
        for g in range(4):
            t32[SUB * g : SUB * (g + 1)] = rff[g].astype(F32)[0:SUB]
        if k:
            out_copy.wait()
        stage[...] = jnp.transpose(t32[...]).astype(BF)
        out_copy = pltpu.make_async_copy(stage, dst, loc.at[1])
        out_copy.start()

    out_copy.wait()
    for c in vxs:
        c.got()
    total_v = vx[0]
    for p in range(1, 8):
        total_v = total_v + vx[p]
    small[0:8, 0:QUARTER] = pick([total_v[:, QUARTER * g : QUARTER * (g + 1)] for g in range(4)], h.gx)
    for k in (0, 1):
        parts = [vx[p, k : k + 1, 1664 : 1664 + (FRAME if p == 7 else 192)] for p in range(8)]
        small[8 + k : 9 + k] = join(parts)
    small[10:11, 0 : 4 * SUB] = join([vx[4 * h.xh + g, pl.ds(2 + h.y, 1), 1664 : 1664 + SUB] for g in range(4)])
    for i in range(4):
        p, _ = h.unit(i)
        for c in wfive[i]:
            c.got()
        scr[0:FRAME, 0:QUARTER] = frames[i].astype(F32)

        @pl.when(p < 7)
        def _(i=i):
            scr[192 : 192 + TAIL, 0:QUARTER] = tl[i].astype(F32)

        t32[SUB * i : SUB * (i + 1)] = scr[pl.ds(pl.multiple_of(8 * p, 8), SUB), 0:QUARTER]
    stage[...] = jnp.transpose(t32[...]).astype(BF)
    out_copy = pltpu.make_async_copy(stage, gwa, loc.at[1])
    out_copy.start()
    out_copy.wait()
    lo_own.wait()
    ig_own.wait()
    net.finish()


def layer(*args):
    any_ = pl.BlockSpec(memory_space=pl.ANY)
    scratch = [
        pltpu.VMEM((SEQ, D), BF),
        pltpu.VMEM((SEQ, D), BF),
        pltpu.VMEM((SEQ, D), BF),
        pltpu.VMEM((SEQ, D), BF),
        pltpu.VMEM((8 * FPAD, D), BF),
        pltpu.VMEM((3, SEQ, FRAME), BF),
        pltpu.VMEM((SEQ, FRAME), BF),
        pltpu.VMEM((SEQ, FRAME), BF),
        pltpu.VMEM((2560, 256), BF),
        pltpu.VMEM((4, SEQ, FPAD), BF),
        pltpu.VMEM((4, SEQ, FPAD), BF),
        pltpu.VMEM((SEQ, 2 * HEAD_DIM), F32),
        pltpu.VMEM((SEQ, 2 * HEAD_DIM), F32),
        *Scatter.scratch(),
        *Scatter.scratch(),
        pltpu.VMEM((4, QUARTER, ROWS), BF),
        pltpu.VMEM((4, QUARTER, ROWS), BF),
        pltpu.VMEM((8, QUARTER), F32),
        pltpu.VMEM((2, 4, HALF + EXTRA, QUARTER), BF),
        pltpu.VMEM((4, FPAD, QUARTER), BF),
        pltpu.VMEM((4, FRAME, QUARTER), BF),
        pltpu.VMEM((2, TAIL, QUARTER), BF),
        pltpu.VMEM((2, TAIL, QUARTER), BF),
        pltpu.VMEM((336, QUARTER), F32),
        pltpu.VMEM((4 * SUB, QUARTER), F32),
        pltpu.VMEM((QUARTER, 4 * SUB), BF),
        pltpu.VMEM((4, FPAD, QUARTER), BF),
        pltpu.VMEM((4, 8, QUARTER), F32),
        pltpu.VMEM((8, D), F32),
        pltpu.VMEM((1, 128), jnp.int32),
        pltpu.VMEM((8, FPAD), F32),
        pltpu.VMEM((4, 8, FPAD), F32),
        pltpu.VMEM((ROWS, D), F32),
        pltpu.VMEM((ROWS, D), F32),
        pltpu.VMEM((ROWS, D), BF),
        pltpu.VMEM((3, FRAME, D), BF),
        pltpu.VMEM((FRAME, D), BF),
        pltpu.VMEM((FRAME, D), BF),
        pltpu.VMEM((4, TAIL, QUARTER), BF),
        pltpu.VMEM((8, VW), F32),
        pltpu.VMEM((4, 8, VW), F32),
        pltpu.VMEM((4, 8, VW), F32),
        pltpu.VMEM((8, 8, VW), F32),
        pltpu.SemaphoreType.DMA((Net.SIZE,)),
        pltpu.SemaphoreType.DMA((Net.SIZE,)),
        pltpu.SemaphoreType.DMA((2, 4)),
        pltpu.SemaphoreType.DMA((2, 4)),
        pltpu.SemaphoreType.DMA((1,)),
        pltpu.SemaphoreType.DMA((4,)),
        pltpu.SemaphoreType.DMA((4,)),
        pltpu.SemaphoreType.DMA((4,)),
        pltpu.SemaphoreType.DMA((4,)),
        pltpu.SemaphoreType.REGULAR,
        pltpu.SemaphoreType.REGULAR,
        pltpu.SemaphoreType.REGULAR,
        pltpu.SemaphoreType.REGULAR,
    ]
    return pl.pallas_call(
        layer_kernel,
        out_shape=[
            jax.ShapeDtypeStruct((QUARTER, 4 * ROWS), BF),
            jax.ShapeDtypeStruct((QUARTER, 4 * ROWS), BF),
            jax.ShapeDtypeStruct((QUARTER, 4 * SUB), BF),
            jax.ShapeDtypeStruct((QUARTER, 4 * SUB), BF),
            jax.ShapeDtypeStruct((QUARTER, 4 * SUB), BF),
            jax.ShapeDtypeStruct((16, D), F32),
            jax.ShapeDtypeStruct((2, 4, FPAD, QUARTER), BF),
            jax.ShapeDtypeStruct((SEQ, D), BF),
        ],
        in_specs=[VMEM, any_, any_, VMEM, VMEM, any_, any_] + [VMEM] * 9,
        out_specs=[any_, any_, any_, any_, any_, VMEM, any_, any_],
        scratch_shapes=scratch,
        compiler_params=pltpu.CompilerParams(
            collective_id=0, has_side_effects=True, vmem_limit_bytes=64 * 2**20 - 2**16
        ),
        name="layer",
    )(*args)


def per_device(
    tokens_in, segments, norm1_gain, norm1_bias, qkv_weight, query_bias, value_bias, proj_weight,
    proj_bias, norm2_gain, norm2_bias, fc_weight, fc_bias, out_weight, out_bias, out_grad,
):
    layer_out, input_grad, gwa, gfc, got, small, _, _ = layer(
        segments, tokens_in.T, out_grad.T, qkv_weight, proj_weight, fc_weight, out_weight,
        norm1_gain, norm1_bias, proj_bias, norm2_gain, norm2_bias, out_bias,
        query_bias, value_bias, fc_bias,
    )
    return (
        layer_out.T,
        input_grad.T.astype(F32),
        small[0, :QUARTER],
        small[1, :QUARTER],
        gwa[:, : 3 * SUB].astype(F32),
        small[8],
        small[9],
        gwa[:, 3 * SUB :].astype(F32),
        small[4, :QUARTER],
        small[2, :QUARTER],
        small[3, :QUARTER],
        gfc.astype(F32),
        small[10, : 4 * SUB],
        got.astype(F32),
        small[5, :QUARTER],
    )


def solution(mesh):
    return jax.shard_map(
        per_device,
        mesh=mesh,
        in_specs=(
            P(("dp", "gy"), "gx"), P(("dp", "gx"), "gy"), P("gx"), P("gx"), P("gx", "gy"), P(), P(),
            P("gx", "gy"), P("gx"), P("gx"), P("gx"), P("gx", "gy"), P("gy"), P("gx", "gy"), P("gx"),
            P(("dp", "gy"), "gx"),
        ),
        out_specs=(
            P(("dp", "gy"), "gx"), P(("dp", "gy"), "gx"), P("gx"), P("gx"), P("gx", "gy"), P(), P(),
            P("gx", "gy"), P("gx"), P("gx"), P("gx"), P("gx", "gy"), P("gy"), P("gx", "gy"), P("gx"),
        ),
        check_vma=False,
    )
```
